32 devices in a mesh: dp: 16 (over z, y, x), tp: 2 (over core).
Axes of the slice: x: 2, y: 2, z: 4, core: 2. Of those that a mesh axis runs over, the one named last changes fastest.
Arguments:
- hidden: bfloat16 [64, 256, 410], P('dp', 'tp'), may hold values from -6 to 6
- memory: bfloat16 [64, 256, 410], P('dp', 'tp'), may hold values from -6 to 6
- segment_length: int32 [64], P('dp'), may hold values from 1 to 256, as said below
- memory_length: int32 [64], P('dp'), may hold values from 0 to 256
- doc_reset: int32 [64, 256], P('dp'), may hold values from 0 to 1
- w_query: bfloat16 [410, 410], replicated, may hold values from -0.3125 to 0.3125
- w_key: bfloat16 [410, 410], replicated, may hold values from -0.3125 to 0.3125
- w_value: bfloat16 [410, 410], replicated, may hold values from -0.3125 to 0.3125
- w_pos: bfloat16 [410, 410], replicated, may hold values from -0.3125 to 0.3125
- bias_u: float32 [410], replicated, may hold values from -3 to 3
- bias_v: float32 [410], replicated, may hold values from -3 to 3
- w_out: bfloat16 [410, 410], replicated, may hold values from -1.25 to 1.25
- first_gain: float32 [410], replicated, may hold values from 0.5 to 1.5
- first_shift: float32 [410], replicated, may hold values from -2 to 2
- ffn_in: bfloat16 [410, 2100], P(None, 'tp'), may hold values from -0.3125 to 0.3125
- ffn_in_bias: bfloat16 [2100], P('tp'), may hold values from -3 to 3
- ffn_out: bfloat16 [2100, 410], P('tp'), may hold values from -0.125 to 0.125
- ffn_out_bias: float32 [410], replicated, may hold values from -2 to 2
- second_gain: float32 [410], replicated, may hold values from 0.5 to 1.5
- second_shift: float32 [410], replicated, may hold values from -2 to 2
- out_grad: bfloat16 [64, 256, 410], P('dp', 'tp'), may hold values from -6 to 6
Outputs:
- new_memory: bfloat16 [64, 256, 410], P('dp', 'tp')
- activations: bfloat16 [64, 256, 410], P('dp', 'tp')
- input_grad: float32 [64, 256, 410], P('dp', 'tp')
- grad_query: float32 [410, 410], replicated
- grad_key: float32 [410, 410], replicated
- grad_value: float32 [410, 410], replicated
- grad_pos: float32 [410, 410], replicated
- grad_bias_u: float32 [410], replicated
- grad_bias_v: float32 [410], replicated
- grad_out: float32 [410, 410], replicated
- grad_first_gain: float32 [410], replicated
- grad_first_shift: float32 [410], replicated
- grad_ffn_in: float32 [410, 2100], P(None, 'tp')
- grad_ffn_in_bias: float32 [2100], P('tp')
- grad_ffn_out: float32 [2100, 410], P('tp')
- grad_ffn_out_bias: float32 [410], replicated
- grad_second_gain: float32 [410], replicated
- grad_second_shift: float32 [410], replicated
The draws below stay inside these ranges and needn't reach their ends.
Inputs may be any that keep to these rules, and one draw needn't show every extreme that they name: In each group of 4 consecutive streams one stream, which one drawn from the seed, has segment_length 256, memory_length 256 and no reset.
All inputs are finite; a program needn't handle non-finite values.
Results may differ from the reference program's by a relative error of at most 0.015.
Values may be sent and summed in bfloat16 or wider, within the bound.
No kernel may reach another device: no remote copies, remote signals or barrier semaphores. Data moves between devices by JAX's collectives and lax.ppermute only.
A program may use at most 192 MiB of HBM per device.

```python
import math
import jax
import jax.numpy as jnp
from jax import lax

D = 410
HEADS = 10
DHEAD = 41
FF = 2100
SEG = 256
MEM = 256
STREAMS_DEV = 4
STREAMS = 64


def chosen_streams(key):
    group_count = STREAMS // STREAMS_DEV
    offsets = jax.random.randint(key, (group_count,), 0, STREAMS_DEV)
    stream_ids = jnp.arange(STREAMS)
    return stream_ids % STREAMS_DEV == jnp.repeat(offsets, STREAMS_DEV)


def draw_segment_length(key, part):
    chosen = chosen_streams(key)
    key = jax.random.fold_in(key, 3)
    drawn = jax.random.randint(key, (STREAMS,), 1, SEG + 1)
    return jnp.where(chosen, SEG, drawn).astype(jnp.int32)


def draw_memory_length(key, part):
    chosen = chosen_streams(key)
    key = jax.random.fold_in(key, 5)
    drawn = jax.random.randint(key, (STREAMS,), 0, MEM + 1)
    return jnp.where(chosen, MEM, drawn).astype(jnp.int32)


def draw_doc_reset(key, part):
    chosen = chosen_streams(key)
    key = jax.random.fold_in(key, 7)
    drawn = jax.random.randint(key, (STREAMS, SEG), 0, max(4, SEG // 4))
    starts = jnp.where(drawn == 0, 1, 0)
    return jnp.where(chosen[:, None], 0, starts).astype(jnp.int32)


def levels(key, dims, shards, smallest, high):
    factor_of, own = 1.0, jax.random.fold_in(key, 6)
    for position, blocks in shards:
        steps = jnp.exp(jax.random.uniform(jax.random.fold_in(own, position), (blocks,), jnp.float32, smallest / len(shards), high / len(shards)))
        factor_of = factor_of * jnp.repeat(steps, dims[position] // blocks).reshape([-1 if axis == position else 1 for axis in range(len(dims))])
    return factor_of


def noise(key, extent, scale, reach, split=(), held_as=jnp.bfloat16):
    level = levels(key, extent, split, -0.22, 0.18) if split else 1.0
    entries = jax.random.normal(key, extent, jnp.float32) * scale * level
    return jnp.minimum(jnp.maximum(entries, -reach), reach).astype(held_as)


def setup_inputs(seed: int = 0) -> dict:
    keys = jax.random.split(jax.random.key(seed), 22)
    return {
        "hidden": noise(keys[0], (STREAMS, SEG, D), 1.0, 6.0, ((0, 16), (1, 2))),
        "memory": noise(keys[1], (STREAMS, MEM, D), 1.0, 6.0, ((0, 16), (1, 2))),
        "segment_length": draw_segment_length(jax.random.fold_in(keys[21], 71), 0),
        "memory_length": draw_memory_length(jax.random.fold_in(keys[21], 71), 0),
        "doc_reset": draw_doc_reset(jax.random.fold_in(keys[21], 71), 0),
        "w_query": noise(keys[5], (D, D), D ** -0.5, 0.3125),
        "w_key": noise(keys[6], (D, D), D ** -0.5, 0.3125),
        "w_value": noise(keys[7], (D, D), D ** -0.5, 0.3125),
        "w_pos": noise(keys[8], (D, D), D ** -0.5, 0.3125),
        "bias_u": noise(keys[9], (D,), 0.5, 3.0, (), jnp.float32),
        "bias_v": noise(keys[10], (D,), 0.5, 3.0, (), jnp.float32),
        "w_out": noise(keys[11], (D, D), (D // 16) ** -0.5, 1.25),
        "first_gain": jnp.clip(1.0 + 0.1 * jax.random.normal(keys[12], (D,), jnp.float32), 0.5, 1.5),
        "first_shift": noise(keys[13], (D,), 0.3, 2.0, (), jnp.float32),
        "ffn_in": noise(keys[14], (D, FF), D ** -0.5, 0.3125, ((1, 2),)),
        "ffn_in_bias": noise(keys[15], (FF,), 0.5, 3.0, ((0, 2),)),
        "ffn_out": noise(keys[16], (FF, D), FF ** -0.5, 0.125, ((0, 2),)),
        "ffn_out_bias": noise(keys[17], (D,), 0.3, 2.0, (), jnp.float32),
        "second_gain": jnp.clip(1.0 + 0.1 * jax.random.normal(keys[18], (D,), jnp.float32), 0.5, 1.5),
        "second_shift": noise(keys[19], (D,), 0.3, 2.0, (), jnp.float32),
        "out_grad": noise(keys[20], (STREAMS, SEG, D), 1.0, 6.0, ((0, 16), (1, 2))),
    }


@jax.custom_vjp
def low(v):
    return lax.optimization_barrier(v.astype(jnp.bfloat16)).astype(jnp.float32)

@jax.custom_vjp
def low_back(v):
    return v

def low_keep(v):
    return (low(v), None)

def low_pass(kept, grad):
    return (grad,)

def back_keep(v):
    return (v, None)

def back_low(kept, grad):
    return (low(grad),)
low.defvjp(low_keep, low_pass)
low_back.defvjp(back_keep, back_low)
EPSILON = 1e-05
NEG_LARGE = -1e+30

def product(left, right):
    return jnp.dot(left, right, precision=lax.Precision.HIGHEST, preferred_element_type=jnp.float32)

def layer_norm(values, norm_gain, norm_shift):
    row_mean = lax.optimization_barrier(jnp.mean(values, axis=-1, keepdims=True))
    centred = values - row_mean
    variance = lax.optimization_barrier(jnp.mean(centred * centred, axis=-1, keepdims=True))
    return centred * lax.rsqrt(variance + EPSILON) * norm_gain + norm_shift

def position_table(feature_count, row_total, farthest):
    distance = farthest - jnp.arange(row_total).astype(jnp.float32)
    inverse = 1.0 / 10000.0 ** (jnp.arange(0, feature_count, 2).astype(jnp.float32) / feature_count)
    angles = distance[:, None] * inverse[None, :]
    return jnp.concatenate([jnp.sin(angles), jnp.cos(angles)], axis=1)

def heads_of(values):
    return values.reshape(values.shape[:-1] + (HEADS, DHEAD))

def allowed_keys(doc_reset, segment_length, memory_length):
    documents = jnp.cumsum(doc_reset, axis=1)
    positions = jnp.arange(SEG)
    slot_ids = jnp.arange(MEM)
    memory_ok = (slot_ids[None, None, :] >= (MEM - memory_length)[:, None, None]) & (documents[:, :, None] == 0)
    earlier = positions[None, :, None] > positions[None, None, :]
    same_doc = documents[:, :, None] == documents[:, None, :]
    is_valid = positions[None, None, :] < segment_length[:, None, None]
    diagonal = positions[None, :, None] == positions[None, None, :]
    segment_ok = earlier & same_doc & is_valid | diagonal
    return jnp.concatenate([memory_ok, segment_ok], axis=2)

def attend_stream(query_u, query_v, key_heads, value_heads, rel_heads, allowed):
    content = jnp.einsum('qhe,khe->hqk', query_u, key_heads, precision=lax.Precision.HIGHEST)
    relative = jnp.einsum('qhe,phe->hqp', query_v, rel_heads, precision=lax.Precision.HIGHEST)
    shift_index = SEG - 1 - jnp.arange(SEG)[:, None] + jnp.arange(MEM + SEG)[None, :]
    shift_index = jnp.broadcast_to(shift_index.astype(jnp.int32)[None], (HEADS, SEG, MEM + SEG))
    shifted = jnp.take_along_axis(relative, shift_index, axis=2)
    scores = low_back((content + shifted) * (1.0 / math.sqrt(DHEAD)))
    scores = jnp.where(allowed[None], scores, NEG_LARGE)
    top_score = lax.optimization_barrier(jnp.max(scores, axis=2, keepdims=True))
    exp_terms = jnp.exp(scores - top_score)
    attn_probs = low(exp_terms / lax.optimization_barrier(jnp.sum(exp_terms, axis=2, keepdims=True)))
    return jnp.einsum('hqk,khe->qhe', attn_probs, value_heads, precision=lax.Precision.HIGHEST)

def forward(weight_set, hidden_in, memory_in, allowed, pos_table):
    w_query, w_key, w_value, w_pos, bias_u, bias_v, w_out, first_gain, first_shift, ffn_in, ffn_in_bias, ffn_out, ffn_out_bias, second_gain, second_shift = weight_set
    joined = jnp.concatenate([memory_in, hidden_in], axis=1)
    queries = low_back(product(hidden_in, w_query))
    key_rows = low(product(joined, w_key))
    value_rows = low(product(joined, w_value))
    rel_heads = heads_of(low(product(pos_table, w_pos)))
    query_u = heads_of(low(queries + bias_u))
    query_v = heads_of(low(queries + bias_v))

    def one_stream(packed):
        return attend_stream(packed[0], packed[1], packed[2], packed[3], rel_heads, packed[4])
    attended = lax.map(jax.checkpoint(one_stream), (query_u, query_v, heads_of(key_rows), heads_of(value_rows), allowed))
    attended = low(low_back(attended.reshape(hidden_in.shape)))
    branch = low_back(product(attended, w_out))
    first_norm = layer_norm(hidden_in + branch, first_gain, first_shift)
    inner_pre = low_back(product(low(first_norm), ffn_in) + ffn_in_bias)
    active = low(jax.nn.gelu(inner_pre, approximate=True))
    ffn_result = low_back(product(active, ffn_out))
    return layer_norm(first_norm + ffn_result + ffn_out_bias, second_gain, second_shift)

def reference(hidden, memory, segment_length, memory_length, doc_reset, w_query, w_key, w_value, w_pos, bias_u, bias_v, w_out, first_gain, first_shift, ffn_in, ffn_in_bias, ffn_out, ffn_out_bias, second_gain, second_shift, out_grad):
    weights = tuple((member.astype(jnp.float32) for member in (w_query, w_key, w_value, w_pos, bias_u, bias_v, w_out, first_gain, first_shift, ffn_in, ffn_in_bias, ffn_out, ffn_out_bias, second_gain, second_shift)))
    pos_table = low(position_table(D, MEM + 2 * SEG, MEM + SEG - 1))
    group_size = math.gcd(STREAMS, max(1, 4096 // SEG))
    group_count = STREAMS // group_size

    def grouped(values):
        return values.reshape((group_count, group_size) + values.shape[1:])
    packs = (grouped(hidden.astype(jnp.float32)), grouped(memory.astype(jnp.float32)), grouped(segment_length), grouped(memory_length), grouped(doc_reset), grouped(out_grad.astype(jnp.float32)))

    def scan_step(totals, packed):
        hidden_part, memory_part, seg_part, mem_part, reset_part, cot_part = packed
        allowed = allowed_keys(reset_part, seg_part, mem_part)

        def run_layer(weight_set, hidden_in):
            return forward(weight_set, hidden_in, memory_part, allowed, pos_table)
        result, pullback = jax.vjp(run_layer, weights, hidden_part)
        grad_weights, grad_hidden = pullback(cot_part)
        return (jax.tree.map(jnp.add, totals, grad_weights), (result, grad_hidden))
    totals, (results, grad_hidden) = lax.scan(scan_step, jax.tree.map(jnp.zeros_like, weights), packs)
    grad_query, grad_key, grad_value, grad_pos, grad_bias_u, grad_bias_v, grad_out, grad_first_gain, grad_first_shift, grad_ffn_in, grad_ffn_in_bias, grad_ffn_out, grad_ffn_out_bias, grad_second_gain, grad_second_shift = totals
    documents = jnp.cumsum(doc_reset, axis=1)
    keep_rows = (documents == documents[:, -1:]) & (jnp.arange(SEG)[None, :] < segment_length[:, None])
    new_memory = jnp.where(keep_rows[:, :, None], hidden, jnp.zeros_like(hidden))
    activations = results.reshape(STREAMS, SEG, D).astype(jnp.bfloat16)
    input_grad = grad_hidden.reshape(STREAMS, SEG, D)
    return (new_memory, activations, input_grad, grad_query, grad_key, grad_value, grad_pos, grad_bias_u, grad_bias_v, grad_out, grad_first_gain, grad_first_shift, grad_ffn_in, grad_ffn_in_bias, grad_ffn_out, grad_ffn_out_bias, grad_second_gain, grad_second_shift)
```

```python
import math

import jax
import jax.numpy as jnp
import ml_dtypes
import numpy as np
from jax import lax
from jax.experimental import pallas as pl
from jax.experimental.pallas import tpu as pltpu
from jax.sharding import PartitionSpec as P

D = 410
HEADS = 10
DHEAD = 41
SEG = 256
MEM = 256
KEYS = MEM + SEG
HALF = 128
PAIRS = HEADS // 2
WIDE = PAIRS * 128
ROWS = 416
SPAN = 768
EPSILON = 1e-05
NEG_LARGE = -1e30
FACTOR = 1.0 / math.sqrt(DHEAD)
LOW = jnp.bfloat16
F32 = jnp.float32
VMEM_BYTES = 56 * 1024 * 1024


def position_table():
    distance = (KEYS - 1 - np.arange(SPAN)).astype(np.float32)
    inverse = np.float32(1.0) / np.float32(10000.0) ** (
        np.arange(0, D, 2).astype(np.float32) / np.float32(D)
    )
    angles = distance[:, None] * inverse[None, :].astype(np.float32)
    table = np.concatenate([np.sin(angles), np.cos(angles)], axis=1)
    return table.astype(ml_dtypes.bfloat16)


def mm(left, right):
    return lax.dot_general(left, right, (((1,), (0,)), ((), ())), preferred_element_type=F32)


def mm_nt(left, right):
    return lax.dot_general(left, right, (((1,), (1,)), ((), ())), preferred_element_type=F32)


def expander(rows):
    row = lax.broadcasted_iota(jnp.int32, (rows, WIDE), 0)
    lane = lax.broadcasted_iota(jnp.int32, (rows, WIDE), 1)
    inside = lane & 63
    hit = (inside < DHEAD) & (row == (lane >> 6) * DHEAD + inside)
    return jnp.where(hit, 1.0, 0.0).astype(LOW)


def compressor():
    row = lax.broadcasted_iota(jnp.int32, (WIDE, D), 0)
    lane = lax.broadcasted_iota(jnp.int32, (WIDE, D), 1)
    inside = row & 63
    hit = (inside < DHEAD) & (lane == (row >> 6) * DHEAD + inside)
    return jnp.where(hit, 1.0, 0.0).astype(LOW)


def identity(size):
    row = lax.broadcasted_iota(jnp.int32, (size, size), 0)
    lane = lax.broadcasted_iota(jnp.int32, (size, size), 1)
    return jnp.where(row == lane, 1.0, 0.0).astype(LOW)


def reversal(size):
    row = lax.broadcasted_iota(jnp.int32, (size, size), 0)
    lane = lax.broadcasted_iota(jnp.int32, (size, size), 1)
    return jnp.where(row + lane == size - 1, 1.0, 0.0).astype(LOW)


def prep_kernel(wq, wk, wv, wp, wo, bias_u, bias_v, pos, o_q, o_kv, o_rel, o_wo, o_bias):
    expand = expander(D)
    q_wide = mm(wq[...], expand).astype(LOW)
    k_wide = mm(wk[...], expand).astype(LOW)
    v_wide = mm(wv[...], expand).astype(LOW)
    rel = mm(pos[...], wp[...]).astype(LOW)
    rel = mm(rel, expand).astype(LOW)
    for bias_index, bias in enumerate((bias_u, bias_v)):
        value = jnp.broadcast_to(bias[...], (8, D))
        high = value.astype(LOW)
        rest = value - high.astype(F32)
        middle = rest.astype(LOW)
        last = (rest - middle.astype(F32)).astype(LOW)
        wide = mm(high, expand) + mm(middle, expand) + mm(last, expand)
        for p in range(PAIRS):
            o_bias[p, bias_index] = wide[:, 128 * p : 128 * p + 128]
    for p in range(PAIRS):
        part = slice(128 * p, 128 * p + 128)
        o_q[p] = q_wide[:, part]
        o_kv[p, :, :128] = k_wide[:, part]
        o_kv[p, :, 128:] = v_wide[:, part]
        o_rel[p] = rel[:, part]
    o_wo[...] = mm(compressor(), wo[...]).astype(LOW)


def attend_kernel(
    place, seg_len, mem_len, hidden, memory, received, reset, wq, wkv, rel, bias,
    o_probs, o_kv, o_uv, o_att, o_joined, mask
):
    core = place[0]
    stream = pl.program_id(0)
    own = 2 * core + stream
    mine = pl.multiple_of(HALF * core, HALF)
    other = pl.multiple_of(HALF * (1 - core), HALF)

    @pl.when(pl.program_id(1) == 0)
    def start():
        o_joined[0, pl.ds(mine, HALF)] = memory[own]
        o_joined[0, pl.ds(other, HALF)] = received[2 + stream]
        o_joined[0, pl.ds(MEM + mine, HALF)] = hidden[own]
        o_joined[0, pl.ds(MEM + other, HALF)] = received[stream]
        starts = jnp.broadcast_to(reset[pl.ds(own, 1), :].astype(F32), (8, SEG)).astype(LOW)
        row = lax.broadcasted_iota(jnp.int32, (SEG, SEG), 0)
        lane = lax.broadcasted_iota(jnp.int32, (SEG, SEG), 1)
        lower = jnp.where(row >= lane, 1.0, 0.0).astype(LOW)
        doc_column = mm_nt(lower, starts)[:, :1]
        doc_row = mm_nt(starts, lower)[:1, :]
        memory_ok = (lane >= MEM - mem_len[own]) & (doc_column == 0.0)
        segment_ok = ((row > lane) & (doc_row == doc_column) & (lane < seg_len[own])) | (row == lane)
        mask[:, :MEM] = jnp.where(memory_ok, 0.0, NEG_LARGE)
        mask[:, MEM:] = jnp.where(segment_ok, 0.0, NEG_LARGE)

    pair_rows = mm(o_joined[0], wkv[0]).astype(LOW)
    o_kv[0, 0] = pair_rows
    queries = mm(o_joined[0, MEM:], wq[0])
    query_u = (queries + bias[0, 0, :1]).astype(LOW)
    query_v = (queries + bias[0, 1, :1]).astype(LOW)
    o_uv[0, 0, :, :128] = query_u
    o_uv[0, 0, :, 128:] = query_v
    first_head = lax.broadcasted_iota(jnp.int32, (HALF, 128), 1) < 64
    zero = jnp.zeros((HALF, 128), LOW)
    for b in range(2):
        count = KEYS if b else KEYS - HALF
        width = count + HALF
        rows = slice(HALF * b, HALF * b + HALF)
        start_row = HALF - HALF * b
        outs = []
        for h in range(2):
            if h == 0:
                u_h = jnp.where(first_head, query_u[rows], zero)
                v_h = jnp.where(first_head, query_v[rows], zero)
            else:
                u_h = jnp.where(first_head, zero, query_u[rows])
                v_h = jnp.where(first_head, zero, query_v[rows])
            content = mm_nt(u_h, pair_rows[:count, :128])
            relative = mm_nt(v_h, rel[0, start_row : start_row + width])
            relative = pltpu.roll(relative, count + 1, 1, stride=1, stride_axis=0)[:, :count]
            scores = (content + relative) * FACTOR + mask[rows, :count]
            exp_terms = jnp.exp(scores - jnp.max(scores, axis=1, keepdims=True))
            total = jnp.sum(exp_terms, axis=1, keepdims=True)
            probs = (exp_terms * (1.0 / total)).astype(LOW)
            o_probs[0, 0, h, rows, :count] = probs
            if b == 0:
                o_probs[0, 0, h, rows, count:] = jnp.zeros((HALF, HALF), LOW)
            outs.append(mm(probs, pair_rows[:count, 128:]))
        o_att[0, rows] = jnp.where(first_head, outs[0], outs[1]).astype(LOW)


def norm_forward(values):
    centred = values - jnp.mean(values, axis=1, keepdims=True)
    scale = lax.rsqrt(jnp.mean(centred * centred, axis=1, keepdims=True) + EPSILON)
    return centred * scale, scale


def norm_backward(grad, x_hat, scale):
    return scale * (
        grad
        - jnp.mean(grad, axis=1, keepdims=True)
        - x_hat * jnp.mean(grad * x_hat, axis=1, keepdims=True)
    )


GELU_A = math.sqrt(2.0 / math.pi)
GELU_B = 0.044715


def gelu_both(x):
    square = x * x
    bent = jnp.tanh(x * (GELU_A + (GELU_A * GELU_B) * square))
    half_up = 0.5 + 0.5 * bent
    slope = half_up + (0.5 * x) * (1.0 - bent * bent) * (GELU_A + (3.0 * GELU_A * GELU_B) * square)
    return x * half_up, slope


def total_rows(values):
    return jnp.sum(values, axis=0, keepdims=True)


def ffn_kernel(
    place, att, joined, out_grad, received, wo, win_a, win_b, bin_a, bin_b, wout_a, wout_b,
    gain_1, shift_1, bias_out, gain_2, shift_2,
    o_act, o_first, o_ga, o_own, o_other, o_out,
    og, low_in, gb_all, gs_all, active, inner, vecs
):
    core = place[0]
    mine = pl.multiple_of(HALF * core, HALF)
    other = pl.multiple_of(HALF * (1 - core), HALF)
    hidden_units = win_a.shape[1]
    chunks = [(a, min(a + 256, hidden_units)) for a in range(0, hidden_units, 256)]
    halves = ((win_a, bin_a, wout_a), (win_b, bin_b, wout_b))
    low_in[:, 384:] = jnp.where(
        lax.broadcasted_iota(jnp.int32, (2 * SEG, 128), 1) == D - 384, 1.0, 0.0
    ).astype(LOW)
    gs_all[:, 384:] = jnp.zeros((2 * SEG, 128), LOW)
    vecs[...] = jnp.zeros_like(vecs)
    for s in range(2):
        og[s, pl.ds(mine, HALF)] = out_grad[2 * core + s]
        og[s, pl.ds(other, HALF)] = received[4 + s]
        rows = slice(SEG * s, SEG * s + SEG)
        hid = joined[s, MEM:].astype(F32)
        hat_1, scale_1 = norm_forward(hid + mm(att[s], wo[...]))
        first = hat_1 * gain_1[...] + shift_1[...]
        first_low = first.astype(LOW)
        low_in[rows, :D] = first_low
        ffn_sum = None
        slopes = []
        for which, (win, b_in, wout) in enumerate(halves):
            for a, z in chunks:
                pre = mm(first_low, win[:, a:z]) + b_in[:, a:z].astype(F32)
                act, slope = gelu_both(pre)
                act = act.astype(LOW)
                slopes.append(slope)
                active[which, rows, a:z] = act
                part = mm(act, wout[a:z])
                ffn_sum = part if ffn_sum is None else ffn_sum + part
        hat_2, scale_2 = norm_forward(first + ffn_sum + bias_out[...])
        o_act[s] = (hat_2 * gain_2[...] + shift_2[...]).astype(LOW)
        cot = og[s].astype(F32)
        vecs[2:3] += total_rows(cot * hat_2)
        vecs[3:4] += total_rows(cot)
        grad_second = norm_backward(cot * gain_2[...], hat_2, scale_2)
        vecs[4:5] += total_rows(grad_second)
        gs_low = grad_second.astype(LOW)
        gs_all[rows, :D] = gs_low
        grad_first = grad_second
        index = 0
        for which, (win, b_in, wout) in enumerate(halves):
            for a, z in chunks:
                grad_inner = (mm_nt(gs_low, wout[a:z]) * slopes[index]).astype(LOW)
                index += 1
                inner[which, rows, a:z] = grad_inner
                grad_first = grad_first + mm_nt(grad_inner, win[:, a:z])
        vecs[0:1] += total_rows(grad_first * hat_1)
        vecs[1:2] += total_rows(grad_first)
        grad_pre = norm_backward(grad_first * gain_1[...], hat_1, scale_1)
        o_first[s] = grad_pre
        grad_branch = grad_pre.astype(LOW)
        gb_all[rows] = grad_branch
        o_ga[s] = mm_nt(grad_branch, wo[...]).astype(LOW)
    in_t = low_in[...].T[:ROWS]
    gs_t = gs_all[...].T[:ROWS]
    for which, pack in ((1, o_other), (0, o_own)):
        for block in range(-(-hidden_units // 128)):
            a, z = 128 * block, min(128 * block + 128, hidden_units)
            pack[0, ROWS * block : ROWS * block + ROWS, : z - a] = mm(
                in_t, inner[which, :, a:z]
            ).astype(LOW)
            pack[1, ROWS * block : ROWS * block + ROWS, : z - a] = mm(
                gs_t, active[which, :, a:z]
            ).astype(LOW)
    grad_out = None
    for s in range(2):
        part = mm(att[s].T, gb_all[SEG * s : SEG * s + SEG])
        grad_out = part if grad_out is None else grad_out + part
    grad_out = mm(expander(ROWS), grad_out.astype(LOW))
    grad_out = grad_out + mm(pick_rows(8), vecs[...].astype(LOW))
    store_blocks(o_out, 0, grad_out)


def pick_rows(count):
    row = lax.broadcasted_iota(jnp.int32, (ROWS, count), 0)
    lane = lax.broadcasted_iota(jnp.int32, (ROWS, count), 1)
    return jnp.where((row == D + lane), 1.0, 0.0).astype(LOW)


def store_blocks(ref, base, values):
    low = values.astype(LOW)
    for block in range(4):
        a, z = 128 * block, min(128 * block + 128, D)
        ref[base + ROWS * block : base + ROWS * block + ROWS, : z - a] = low[:, a:z]


def back_kernel(
    probs, kv, uv, rel, ga, joined, wq, wkv, pos, first_grad, o_input, o_pack,
    scores, grel, dkv, wide, bias_sums
):
    pair = pl.program_id(0)
    stream = pl.program_id(1)
    flip = reversal(HALF)
    first_head = lax.broadcasted_iota(jnp.int32, (HALF, 128), 1) < 64
    zero = jnp.zeros((HALF, 128), LOW)
    key_rows = kv[0, 0, :, :128]
    value_rows = kv[0, 0, :, 128:]
    grad_att = ga[0]
    u_t = uv[0, 0, :, :128].T
    ga_t = grad_att.T

    @pl.when((pair == 0) & (stream == 0))
    def first_step():
        o_input[...] = first_grad[...]

    @pl.when(stream == 0)
    def clear():
        grel[...] = jnp.zeros_like(grel)
        bias_sums[pair] = jnp.zeros((8, 128), F32)

    grad_q = [None, None]
    sum_u = jnp.zeros((1, 128), F32)
    sum_v = jnp.zeros((1, 128), F32)
    for b in range(2):
        count = KEYS if b else KEYS - HALF
        width = count + HALF
        rows = slice(HALF * b, HALF * b + HALF)
        start_row = HALF - HALF * b
        v_t = mm(flip, uv[0, 0, rows, 128:]).astype(LOW).T
        parts = []
        for h in range(2):
            ga_h = jnp.where(first_head, grad_att[rows], zero) if h == 0 else jnp.where(
                first_head, zero, grad_att[rows]
            )
            grad_probs = mm_nt(ga_h, value_rows[:count])
            attn = probs[0, 0, h, rows, :count].astype(F32)
            inner = jnp.sum(grad_probs * attn, axis=1, keepdims=True)
            grad_scores = (attn * (grad_probs - inner)).astype(LOW)
            scores[h, rows, :count] = grad_scores
            if b == 0:
                scores[h, rows, count:] = jnp.zeros((HALF, HALF), LOW)
            turned = mm(flip, grad_scores)
            spread = jnp.concatenate([turned, jnp.zeros((HALF, HALF), F32)], axis=1)
            spread = pltpu.roll(spread, 0, 1, stride=1, stride_axis=0).astype(LOW)
            grad_u = mm(turned.astype(LOW), key_rows[:count])
            grad_v = mm(spread, rel[0, start_row : start_row + width])
            grel[64 * h : 64 * h + 64, start_row : start_row + width] += mm(
                v_t[64 * h : 64 * h + 64], spread
            )
            parts.append((grad_u, grad_v))
        grad_u = jnp.where(first_head, parts[0][0], parts[1][0]) * FACTOR
        grad_v = jnp.where(first_head, parts[0][1], parts[1][1]) * FACTOR
        sum_u = sum_u + total_rows(grad_u)
        sum_v = sum_v + total_rows(grad_v)
        grad_q[b] = mm(flip, (grad_u + grad_v).astype(LOW)).astype(LOW)
    bias_sums[pair, 0:1] += sum_u
    bias_sums[pair, 1:2] += sum_v
    for h in range(2):
        part = slice(64 * h, 64 * h + 64)
        dkv[part] = (mm(u_t[part], scores[h]) * FACTOR).astype(LOW)
        dkv[128 + 64 * h : 192 + 64 * h] = mm(ga_t[part], probs[0, 0, h]).astype(LOW)
    grad_queries = jnp.concatenate(grad_q, axis=0)
    token_grads = jnp.concatenate([grad_queries, dkv[:, MEM:].T], axis=1)
    token_weights = jnp.concatenate([wq[0], wkv[0]], axis=1)
    o_input[stream] += mm_nt(token_grads, token_weights)
    weight_kv = mm(dkv[...], joined[0])
    weight_q = mm(grad_queries.T, joined[0, MEM:])

    @pl.when(stream == 0)
    def store_first():
        wide[pair, :256] = weight_kv
        wide[pair, 256:384] = weight_q

    @pl.when(stream == 1)
    def store_second():
        wide[pair, :256] += weight_kv
        wide[pair, 256:384] += weight_q
        wide[pair, 384:512] = mm((grel[...] * FACTOR).astype(LOW), pos[...])

    @pl.when((pair == PAIRS - 1) & (stream == 1))
    def last_step():
        pick = expander(ROWS)
        back = compressor()
        for m in range(4):
            total = None
            for p in range(PAIRS):
                part = mm(
                    pick[:, 128 * p : 128 * p + 128], wide[p, 128 * m : 128 * m + 128].astype(LOW)
                )
                total = part if total is None else total + part
            if m == 2:
                vectors = None
                for p in range(PAIRS):
                    part = mm(bias_sums[p].astype(LOW), back[128 * p : 128 * p + 128])
                    vectors = part if vectors is None else vectors + part
                total = total + mm(pick_rows(8), vectors.astype(LOW))
            store_blocks(o_pack, 4 * ROWS * m, total)


def unpack_attention_kernel(pack_out, pack, o_out, o_key, o_value, o_query, o_pos, o_vec_a, o_vec_b):
    unit = identity(128)
    for block in range(4):
        a, z = 128 * block, min(128 * block + 128, D)
        part = pack_out[ROWS * block : ROWS * block + ROWS, : z - a].astype(F32)
        o_out[:, a:z] = part[:D]
        o_vec_a[:, a:z] = part[408:416]
        for m, ref in enumerate((o_key, o_value, o_query, o_pos)):
            base = 4 * ROWS * m + ROWS * block
            ref[a:z, :] = mm_nt(unit, pack[base : base + ROWS, :])[: z - a, :D]
            if m == 2:
                o_vec_b[:, a:z] = pack[base + 400 : base + ROWS, : z - a].astype(F32)[8:]


def unpack_ffn_kernel(pack, o_in, o_bias, o_out):
    unit = identity(128)
    units = o_in.shape[1]
    for block in range(-(-units // 128)):
        a, z = 128 * block, min(128 * block + 128, units)
        part = pack[0, ROWS * block : ROWS * block + ROWS, : z - a].astype(F32)
        o_in[:, a:z] = part[:D]
        o_bias[:, a:z] = part[408:416]
        o_out[a:z, :] = mm_nt(unit, pack[1, ROWS * block : ROWS * block + ROWS, :])[: z - a, :D]


def whole_spec():
    return pl.BlockSpec(memory_space=pltpu.VMEM)


def scalar_spec():
    return pl.BlockSpec(memory_space=pltpu.SMEM)


def params(**more):
    return pltpu.CompilerParams(vmem_limit_bytes=VMEM_BYTES, **more)


def cost(flops, moved):
    return pl.CostEstimate(flops=int(flops), bytes_accessed=int(moved), transcendentals=0)


def shape(dims, dtype=LOW):
    return jax.ShapeDtypeStruct(dims, dtype)


def prepare(w_query, w_key, w_value, w_pos, w_out, bias_u, bias_v, pos_table):
    return pl.pallas_call(
        prep_kernel,
        out_shape=(
            shape((PAIRS, D, 128)),
            shape((PAIRS, D, 256)),
            shape((PAIRS, SPAN, 128)),
            shape((WIDE, D)),
            shape((PAIRS, 2, 8, 128), F32),
        ),
        in_specs=[whole_spec()] * 8,
        out_specs=(whole_spec(),) * 5,
        compiler_params=params(),
        cost_estimate=cost(3e9, 5e6),
        name="prepare_weights",
    )(w_query, w_key, w_value, w_pos, w_out, bias_u[None], bias_v[None], pos_table)


def attend(place, seg_len, mem_len, hidden, memory, received, reset, wq, wkv, rel, bias):
    def fixed(dims):
        return pl.BlockSpec(dims, lambda s, p, *_: (0,) * len(dims))

    def paired(dims):
        return pl.BlockSpec((1,) + dims, lambda s, p, *_: (p,) + (0,) * len(dims))

    def both(dims):
        return pl.BlockSpec((1, 1) + dims, lambda s, p, *_: (s, p) + (0,) * len(dims))

    return pl.pallas_call(
        attend_kernel,
        grid_spec=pltpu.PrefetchScalarGridSpec(
            num_scalar_prefetch=3,
            grid=(2, PAIRS),
            in_specs=[
                fixed(hidden.shape),
                fixed(memory.shape),
                fixed(received.shape),
                fixed(reset.shape),
                paired((D, 128)),
                paired((D, 256)),
                paired((SPAN, 128)),
                paired((2, 8, 128)),
            ],
            out_specs=[
                both((2, SEG, KEYS)),
                both((KEYS, 256)),
                both((SEG, 256)),
                pl.BlockSpec((1, SEG, 128), lambda s, p, *_: (s, 0, p)),
                pl.BlockSpec((1, KEYS, D), lambda s, p, *_: (s, 0, 0)),
            ],
            scratch_shapes=[pltpu.VMEM((SEG, KEYS), F32)],
        ),
        out_shape=(
            shape((2, PAIRS, 2, SEG, KEYS)),
            shape((2, PAIRS, KEYS, 256)),
            shape((2, PAIRS, SEG, 256)),
            shape((2, SEG, WIDE)),
            shape((2, KEYS, D)),
        ),
        compiler_params=params(),
        cost_estimate=cost(8e9, 12e6),
        name="attend",
    )(place, seg_len, mem_len, hidden, memory, received, reset, wq, wkv, rel, bias)


def feed_forward(place, att, joined, out_grad, received, wo, own, other, vectors):
    units = own[0].shape[1]
    blocks = -(-units // 128)
    weights = (own[0], other[0], own[1], other[1], own[2], other[2])
    return pl.pallas_call(
        ffn_kernel,
        out_shape=(
            shape((2, SEG, D)),
            shape((2, SEG, D), F32),
            shape((2, SEG, WIDE)),
            shape((2, ROWS * blocks, 128)),
            shape((2, ROWS * blocks, 128)),
            shape((4 * ROWS, 128)),
        ),
        in_specs=[scalar_spec()] + [whole_spec()] * 16,
        out_specs=(whole_spec(),) * 6,
        scratch_shapes=[
            pltpu.VMEM((2, SEG, D), LOW),
            pltpu.VMEM((2 * SEG, 512), LOW),
            pltpu.VMEM((2 * SEG, D), LOW),
            pltpu.VMEM((2 * SEG, 512), LOW),
            pltpu.VMEM((2, 2 * SEG, units), LOW),
            pltpu.VMEM((2, 2 * SEG, units), LOW),
            pltpu.VMEM((8, D), F32),
        ],
        compiler_params=params(),
        cost_estimate=cost(1e10, 15e6),
        name="feed_forward",
    )(place, att, joined, out_grad, received, wo, *weights, *vectors)


def attend_back(probs, kv, uv, rel, ga, joined, wq, wkv, pos_table, first_grad):
    def fixed(dims):
        return pl.BlockSpec(dims, lambda p, s: (0,) * len(dims))

    def paired(dims):
        return pl.BlockSpec((1,) + dims, lambda p, s: (p,) + (0,) * len(dims))

    def both(dims):
        return pl.BlockSpec((1, 1) + dims, lambda p, s: (s, p) + (0,) * len(dims))

    return pl.pallas_call(
        back_kernel,
        grid=(PAIRS, 2),
        in_specs=[
            both((2, SEG, KEYS)),
            both((KEYS, 256)),
            both((SEG, 256)),
            paired((SPAN, 128)),
            pl.BlockSpec((1, SEG, 128), lambda p, s: (s, 0, p)),
            pl.BlockSpec((1, KEYS, D), lambda p, s: (s, 0, 0)),
            paired((D, 128)),
            paired((D, 256)),
            fixed((SPAN, D)),
            fixed((2, SEG, D)),
        ],
        out_specs=[fixed((2, SEG, D)), fixed((16 * ROWS, 128))],
        out_shape=(shape((2, SEG, D), F32), shape((16 * ROWS, 128))),
        scratch_shapes=[
            pltpu.VMEM((2, SEG, KEYS), LOW),
            pltpu.VMEM((128, SPAN), F32),
            pltpu.VMEM((256, KEYS), LOW),
            pltpu.VMEM((PAIRS, 512, D), F32),
            pltpu.VMEM((PAIRS, 8, 128), F32),
        ],
        compiler_params=params(),
        cost_estimate=cost(1.5e10, 15e6),
        name="attend_back",
    )(probs, kv, uv, rel, ga, joined, wq, wkv, pos_table, first_grad)


def unpack_attention(pack_out, pack):
    return pl.pallas_call(
        unpack_attention_kernel,
        out_shape=(shape((D, D), F32),) * 5 + (shape((8, D), F32),) * 2,
        in_specs=[whole_spec()] * 2,
        out_specs=(whole_spec(),) * 7,
        compiler_params=params(),
        name="unpack_attention",
    )(pack_out, pack)


def unpack_ffn(pack, units):
    return pl.pallas_call(
        unpack_ffn_kernel,
        out_shape=(shape((D, units), F32), shape((8, units), F32), shape((units, D), F32)),
        in_specs=[whole_spec()],
        out_specs=(whole_spec(),) * 3,
        compiler_params=params(),
        name="unpack_ffn",
    )(pack)


def swap(values):
    return lax.ppermute(values, "tp", [(0, 1), (1, 0)])


def bits_of(count):
    return [k for k in range(count.bit_length() - 1)]


def reduce_halves(values, bits, axis_size, index):
    for k in bits:
        rows = values.shape[0] // 2
        bit = (index >> k) & 1
        sent = lax.dynamic_slice_in_dim(values, (1 - bit) * rows, rows, 0)
        kept = lax.dynamic_slice_in_dim(values, bit * rows, rows, 0)
        values = kept + lax.ppermute(
            sent, "dp", [(i, i ^ (1 << k)) for i in range(axis_size)]
        )
    return values


def gather_halves(values, bits, axis_size, index):
    for k in reversed(bits):
        came = lax.ppermute(values, "dp", [(i, i ^ (1 << k)) for i in range(axis_size)])
        bit = (index >> k) & 1
        values = jnp.where(
            bit == 0,
            jnp.concatenate([values, came], axis=0),
            jnp.concatenate([came, values], axis=0),
        )
    return values


def padded_rows(values, multiple):
    extra = -values.shape[0] % multiple
    return jnp.pad(values, ((0, extra), (0, 0))) if extra else values


def make_shards(dp_size):
    table = position_table()

    def shards(
        hidden, memory, segment_length, memory_length, doc_reset, w_query, w_key, w_value, w_pos,
        bias_u, bias_v, w_out, first_gain, first_shift, ffn_in, ffn_in_bias, ffn_out, ffn_out_bias,
        second_gain, second_shift, out_grad,
    ):
        core = lax.axis_index("tp")
        index = lax.axis_index("dp")
        place = core[None].astype(jnp.int32)
        units = ffn_in.shape[1]
        pos_table = jnp.asarray(table)

        def halves(values, which):
            return lax.dynamic_slice_in_dim(values, 2 * which, 2, 0)

        sent = jnp.concatenate([halves(a, 1 - core) for a in (hidden, memory, out_grad)], axis=0)
        received = swap(sent)
        other_ffn = (swap(ffn_in), swap(ffn_in_bias[None]), swap(ffn_out))
        own_ffn = (ffn_in, ffn_in_bias[None], ffn_out)

        wq, wkv, rel, wo, bias = prepare(
            w_query, w_key, w_value, w_pos, w_out, bias_u, bias_v, pos_table
        )
        probs, kv, uv, att, joined = attend(
            place, segment_length, memory_length, hidden, memory, received, doc_reset,
            wq, wkv, rel, bias,
        )
        act, first_grad, ga, ffn_own, ffn_other, pack_out = feed_forward(
            place, att, joined, out_grad, received, wo, own_ffn, other_ffn,
            tuple(v[None] for v in (first_gain, first_shift, ffn_out_bias, second_gain, second_shift)),
        )
        bits = bits_of(dp_size)
        ffn_total = (ffn_own + swap(ffn_other)).reshape(-1, 128)
        ffn_rows = ffn_total.shape[0]
        ffn_total = padded_rows(ffn_total, 16 * dp_size)
        ffn_total = gather_halves(
            reduce_halves(ffn_total, bits, dp_size, index), bits, dp_size, index
        )[:ffn_rows]
        grad_in, grad_in_bias, grad_ffn_out = unpack_ffn(ffn_total.reshape(2, -1, 128), units)

        input_own, pack = attend_back(
            probs, kv, uv, rel, ga, joined, wq, wkv, pos_table, first_grad
        )
        total = jnp.concatenate([pack_out, pack], axis=0)
        total_count = total.shape[0]
        total = padded_rows(total, 32 * dp_size)
        half = total.shape[0] // 2
        kept = lax.dynamic_slice_in_dim(total, core * half, half, 0)
        total = kept + swap(lax.dynamic_slice_in_dim(total, (1 - core) * half, half, 0))
        total = gather_halves(
            reduce_halves(total, bits, dp_size, index), bits, dp_size, index
        )
        came = swap(total)
        total = jnp.where(
            core == 0,
            jnp.concatenate([total, came], axis=0),
            jnp.concatenate([came, total], axis=0),
        )[:total_count]
        g_out, g_key, g_value, g_query, g_pos, vec_a, vec_b = unpack_attention(
            total[: 4 * ROWS], total[4 * ROWS :]
        )

        def give_back(values, dtype):
            rows = values.shape[1] // 2
            mine = lax.dynamic_slice_in_dim(values, core * rows, rows, 1)
            theirs = lax.dynamic_slice_in_dim(values, (1 - core) * rows, rows, 1)
            came = swap(theirs.astype(LOW)).astype(dtype)
            mine = mine.astype(dtype)
            return jnp.where(
                core == 0,
                jnp.concatenate([mine, came], axis=0),
                jnp.concatenate([came, mine], axis=0),
            )

        activations = give_back(act, LOW)
        input_grad = give_back(input_own, F32)

        rows = hidden.shape[1]
        positions = core * rows + jnp.arange(rows)
        later = (jnp.arange(SEG)[:, None] > positions[None, :]).astype(LOW)
        resets = jnp.dot(doc_reset.astype(LOW), later, preferred_element_type=F32)
        keep = (resets == 0.0) & (positions[None, :] < segment_length[:, None])
        new_memory = jnp.where(keep[:, :, None], hidden, jnp.zeros_like(hidden))
        return (
            new_memory, activations, input_grad, g_query, g_key, g_value, g_pos,
            vec_b[2], vec_b[3], g_out, vec_a[2], vec_a[3],
            grad_in, grad_in_bias[2], grad_ffn_out, vec_a[6], vec_a[4], vec_a[5],
        )

    return shards


def solution(mesh):
    rows, copied = P("dp", "tp", None), P()
    shards = make_shards(mesh.shape["dp"])
    return jax.shard_map(
        shards,
        mesh=mesh,
        in_specs=(
            rows, rows, P("dp"), P("dp"), P("dp", None),
            copied, copied, copied, copied, copied, copied, copied, copied, copied,
            P(None, "tp"), P("tp"), P("tp", None),
            copied, copied, copied, rows,
        ),
        out_specs=(
            rows, rows, rows, copied, copied, copied, copied, copied, copied, copied, copied, copied,
            P(None, "tp"), P("tp"), P("tp", None), copied, copied, copied,
        ),
        check_vma=False,
    )
```

```python
import functools
import math

import jax
import jax.numpy as jnp
import ml_dtypes
import numpy as np
from jax import lax
from jax.experimental import pallas as pl
from jax.experimental.pallas import tpu as pltpu
from jax.sharding import PartitionSpec as P

D = 410
HEADS = 10
DHEAD = 41
SEG = 256
MEM = 256
KEYS = MEM + SEG
HALF = 128
PAIRS = HEADS // 2
WIDE = PAIRS * 128
ROWS = 416
SPAN = 768
REST = 26
HALF_BLOCKS = 8
EPSILON = 1e-05
NEG_LARGE = -1e30
FACTOR = 1.0 / math.sqrt(DHEAD)
LOG2E = 1.0 / math.log(2.0)
LOW = jnp.bfloat16
VMEM_BYTES = 60 * 1024 * 1024
F32 = jnp.float32


def position_table():
    distance = (KEYS - 1 - np.arange(SPAN)).astype(np.float32)
    inverse = np.float32(1.0) / np.float32(10000.0) ** (
        np.arange(0, D, 2).astype(np.float32) / np.float32(D)
    )
    angles = distance[:, None] * inverse[None, :].astype(np.float32)
    table = np.concatenate([np.sin(angles), np.cos(angles)], axis=1)
    return table.astype(ml_dtypes.bfloat16)


def mm(left, right):
    return lax.dot_general(left, right, (((1,), (0,)), ((), ())), preferred_element_type=F32)


def mm_nt(left, right):
    return lax.dot_general(left, right, (((1,), (1,)), ((), ())), preferred_element_type=F32)


def expander(rows):
    row = lax.broadcasted_iota(jnp.int32, (rows, WIDE), 0)
    lane = lax.broadcasted_iota(jnp.int32, (rows, WIDE), 1)
    inside = lane & 63
    hit = (inside < DHEAD) & (row == (lane >> 6) * DHEAD + inside)
    return jnp.where(hit, 1.0, 0.0).astype(LOW)


def compressor():
    row = lax.broadcasted_iota(jnp.int32, (WIDE, D), 0)
    lane = lax.broadcasted_iota(jnp.int32, (WIDE, D), 1)
    inside = row & 63
    hit = (inside < DHEAD) & (lane == (row >> 6) * DHEAD + inside)
    return jnp.where(hit, 1.0, 0.0).astype(LOW)


def identity(size):
    row = lax.broadcasted_iota(jnp.int32, (size, size), 0)
    lane = lax.broadcasted_iota(jnp.int32, (size, size), 1)
    return jnp.where(row == lane, 1.0, 0.0).astype(LOW)


def reversal(size):
    row = lax.broadcasted_iota(jnp.int32, (size, size), 0)
    lane = lax.broadcasted_iota(jnp.int32, (size, size), 1)
    return jnp.where(row + lane == size - 1, 1.0, 0.0).astype(LOW)


class Mover:
    def __init__(self, sems):
        self.sems, self.used, self.open = sems, 0, []

    def start(self, source, target):
        copy = pltpu.make_async_copy(source, target, self.sems.at[self.used])
        self.used += 1
        copy.start()
        self.open.append(copy)
        return copy

    def finish(self):
        for copy in self.open:
            copy.wait()
        self.open = []

    def wait(self, *copies):
        for copy in copies:
            copy.wait()
        self.open = [c for c in self.open if all(c is not d for d in copies)]


def prep_kernel(
    wq_in, wk_in, wv_in, wp_in, wo_in, bias_u_in, bias_v_in, pos_in, q_out, kv_out, rel_out, wo_out,
    bias_out, wq, wk, wv, wp, wo, bias_u, bias_v, pos, o_q, o_kv, o_rel, o_wo, o_bias, sems
):
    mover = Mover(sems)
    loads = [
        mover.start(a, b)
        for a, b in zip(
            (wp_in, pos_in, wk_in, wv_in, wq_in, wo_in, bias_u_in, bias_v_in),
            (wp, pos, wk, wv, wq, wo, bias_u, bias_v),
        )
    ]
    expand = expander(D)
    mover.wait(*loads[:2])
    rel = mm(pos[...], wp[...]).astype(LOW)
    rel = mm(rel, expand).astype(LOW)
    for p in range(PAIRS):
        o_rel[p] = rel[:, 128 * p : 128 * p + 128]
    mover.start(o_rel, rel_out)
    mover.wait(*loads[2:4])
    k_wide = mm(wk[...], expand).astype(LOW)
    v_wide = mm(wv[...], expand).astype(LOW)
    for p in range(PAIRS):
        o_kv[p, :, :128] = k_wide[:, 128 * p : 128 * p + 128]
        o_kv[p, :, 128:] = v_wide[:, 128 * p : 128 * p + 128]
    mover.start(o_kv, kv_out)
    mover.wait(*loads[4:])
    q_wide = mm(wq[...], expand).astype(LOW)
    for p in range(PAIRS):
        o_q[p] = q_wide[:, 128 * p : 128 * p + 128]
    mover.start(o_q, q_out)
    o_wo[...] = mm(compressor(), wo[...]).astype(LOW)
    mover.start(o_wo, wo_out)
    for bias_index, bias in enumerate((bias_u, bias_v)):
        value = jnp.broadcast_to(bias[...], (8, D))
        high = value.astype(LOW)
        rest = value - high.astype(F32)
        middle = rest.astype(LOW)
        last = (rest - middle.astype(F32)).astype(LOW)
        wide = mm(high, expand) + mm(middle, expand) + mm(last, expand)
        for p in range(PAIRS):
            o_bias[p, bias_index] = wide[:, 128 * p : 128 * p + 128]
    mover.start(o_bias, bias_out)
    mover.finish()


def spread_streams(source, raw, core, unit, store):
    raw[...] = source[...].astype(F32)
    for s in range(2):
        columns = raw[pl.ds(2 * core + s, D, stride=4), :].astype(LOW)
        store(s, mm_nt(unit, columns).astype(LOW))


def layer_kernel(
    place, seg_len, mem_len, hidden_hbm, memory_hbm, hidden_in_hbm, memory_in_hbm, reset_hbm,
    wq_hbm, wkv_hbm, rel_hbm, bias_hbm, wo_hbm, out_grad_hbm, out_grad_in_hbm,
    win_a_hbm, win_b_hbm, bin_a_hbm, bin_b_hbm, wout_a_hbm, wout_b_hbm,
    gain_1_hbm, shift_1_hbm, bias_out_hbm, gain_2_hbm, shift_2_hbm,
    probs_out, kv_out, uv_out, att_out, inv_out, joined_out,
    act_out, first_out, ga_out, own_out, other_out, blocks_out,
    hidden, memory, hidden_in, memory_in, reset, wq, wkv, rel, bias, wo, out_grad, out_grad_in,
    win_a, win_b, bin_a, bin_b, wout_a, wout_b, gain_1, shift_1, bias_out, gain_2, shift_2,
    o_probs, o_kv, o_uv, o_att, o_inv, o_joined, o_act, o_first, o_ga, o_own, o_other, o_out,
    raw, mask, og, low_in, gb_all, gs_all, active, inner, vecs, att, sems, step_sems
):
    mover = Mover(sems)
    loads = [
        mover.start(a, b)
        for a, b in zip(
            (
                memory_hbm, memory_in_hbm, hidden_hbm, hidden_in_hbm, reset_hbm,
                wkv_hbm, wq_hbm, bias_hbm, rel_hbm,
                gain_1_hbm, shift_1_hbm, bias_out_hbm, gain_2_hbm, shift_2_hbm, bin_a_hbm,
                bin_b_hbm, wo_hbm, out_grad_hbm, out_grad_in_hbm,
                win_a_hbm, wout_a_hbm, win_b_hbm, wout_b_hbm,
            ),
            (
                memory, memory_in, hidden, hidden_in, reset, wkv, wq, bias, rel,
                gain_1, shift_1, bias_out, gain_2, shift_2, bin_a,
                bin_b, wo, out_grad, out_grad_in, win_a, wout_a, win_b, wout_b,
            ),
        )
    ]
    core = place[0]
    mine = pl.multiple_of(HALF * core, HALF)
    other = pl.multiple_of(HALF * (1 - core), HALF)
    unit = identity(HALF)
    row = lax.broadcasted_iota(jnp.int32, (SEG, SEG), 0)
    lane = lax.broadcasted_iota(jnp.int32, (SEG, SEG), 1)
    lower = jnp.where(row >= lane, 1.0, 0.0).astype(LOW)
    for index, (source, base) in enumerate(
        ((memory, mine), (memory_in, other), (hidden, MEM + mine), (hidden_in, MEM + other))
    ):

        def store(s, values, base=base):
            o_joined[s, pl.ds(pl.multiple_of(base, HALF), HALF)] = values

        mover.wait(loads[index])
        spread_streams(source, raw.at[index], core, unit, store)
    mover.wait(*loads[4:9])
    mover.start(o_joined, joined_out)
    for s in range(2):
        own = 2 * core + s
        starts = jnp.broadcast_to(reset[pl.ds(own, 1), :].astype(F32), (8, SEG)).astype(LOW)
        doc_column = mm_nt(lower, starts)[:, :1]
        doc_row = mm_nt(starts, lower)[:1, :]
        memory_ok = (lane >= MEM - mem_len[own]) & (doc_column == 0.0)
        segment_ok = ((row > lane) & (doc_row == doc_column) & (lane < seg_len[own])) | (row == lane)
        mask[s, :, :MEM] = jnp.where(memory_ok, 0.0, NEG_LARGE)
        mask[s, :, MEM:] = jnp.where(segment_ok, 0.0, NEG_LARGE)
    first_head = lax.broadcasted_iota(jnp.int32, (HALF, 128), 1) < 64
    zero = jnp.zeros((HALF, 128), LOW)
    ones_lane = (lax.broadcasted_iota(jnp.int32, (KEYS, 256), 1) & 190) == 190

    def step(i, carry):
        p, s = i // 2, lax.rem(i, 2)
        pair_rows = jnp.where(ones_lane, 1.0, mm(o_joined[s], wkv[p])).astype(LOW)
        o_kv[p, s] = pair_rows
        queries = mm(o_joined[s, MEM:], wq[p])
        query_u = (queries + bias[p, 0, :1]).astype(LOW)
        query_v = (queries + bias[p, 1, :1]).astype(LOW)
        o_uv[p, s, :, :128] = query_u
        o_uv[p, s, :, 128:] = query_v
        lanes = pl.ds(pl.multiple_of(128 * p, 128), 128)
        for b in range(2):
            count = KEYS if b else KEYS - HALF
            width = count + HALF
            rows = slice(HALF * b, HALF * b + HALF)
            start_row = HALF - HALF * b

            def stacked(values):
                part = values[rows]
                return jnp.concatenate(
                    [jnp.where(first_head, part, zero), jnp.where(first_head, zero, part)], axis=0
                )

            content = mm_nt(stacked(query_u), pair_rows[:count, :128])
            relative = mm_nt(stacked(query_v), rel[p, start_row : start_row + width])
            spots = mask[s, rows, :count]
            exp_terms = []
            for h in range(2):
                part = slice(HALF * h, HALF * h + HALF)
                turned = pltpu.roll(relative[part], count + 1, 1, stride=1, stride_axis=0)
                scores = (content[part] + turned[:, :count]) * (FACTOR * LOG2E) + spots
                top = jnp.max(scores, axis=1, keepdims=True)
                exp_terms.append(jnp.exp2(scores - top).astype(LOW))
                o_probs[p, s, h, rows, :count] = exp_terms[h]
                if b == 0:
                    o_probs[p, s, h, rows, count:] = jnp.zeros((HALF, HALF), LOW)
            mixed = mm(jnp.concatenate(exp_terms, axis=0), pair_rows[:count, 128:])
            inverse = jnp.where(first_head, 1.0 / mixed[:HALF, 63:64], 1.0 / mixed[HALF:, 127:])
            o_inv[s, rows, lanes] = inverse
            o_att[s, rows, lanes] = jnp.where(first_head, mixed[:HALF], mixed[HALF:]) * inverse
        for copy in step_copies(p, s):
            copy.start()
        return carry

    def step_copies(p, s):
        return [
            pltpu.make_async_copy(a.at[p, s], b.at[p, s], step_sems.at[k, p, s])
            for k, (a, b) in enumerate(((o_probs, probs_out), (o_kv, kv_out), (o_uv, uv_out)))
        ]

    lax.fori_loop(0, 2 * PAIRS, step, 0)
    mover.start(o_att, att_out)
    mover.start(o_inv, inv_out)
    hidden_units = win_a.shape[1]
    chunks = [(a, min(a + 256, hidden_units)) for a in range(0, hidden_units, 256)]
    halves = ((win_a, bin_a, wout_a), (win_b, bin_b, wout_b))
    low_in[:, 384:] = jnp.where(
        lax.broadcasted_iota(jnp.int32, (2 * SEG, 128), 1) == D - 384, 1.0, 0.0
    ).astype(LOW)
    gs_all[:, 384:] = jnp.zeros((2 * SEG, 128), LOW)
    vecs[...] = jnp.zeros_like(vecs)
    att[...] = o_att[...].astype(LOW)
    mover.wait(*loads[9:])
    for index, (source, base) in enumerate(((out_grad, mine), (out_grad_in, other))):

        def store_grad(s, values, base=base):
            og[s, pl.ds(base, HALF)] = values

        spread_streams(source, raw.at[index], core, unit, store_grad)
    for s in range(2):
        rows = slice(SEG * s, SEG * s + SEG)
        hid = o_joined[s, MEM:].astype(F32)
        hat_1, scale_1 = norm_forward(hid + mm(att[s], wo[...]))
        first = hat_1 * gain_1[...] + shift_1[...]
        first_low = first.astype(LOW)
        low_in[rows, :D] = first_low
        ffn_sum = None
        slopes = []
        for which, (win, b_in, wout) in enumerate(halves):
            for a, z in chunks:
                pre = mm(first_low, win[:, a:z]) + b_in[:, a:z].astype(F32)
                act, slope = gelu_both(pre)
                act = act.astype(LOW)
                slopes.append(slope)
                active[which, rows, a:z] = act
                part = mm_nt(act, wout[:, a:z])
                ffn_sum = part if ffn_sum is None else ffn_sum + part
        hat_2, scale_2 = norm_forward(first + ffn_sum + bias_out[...])
        o_act[s] = (hat_2 * gain_2[...] + shift_2[...]).astype(LOW)
        cot = og[s].astype(F32)
        vecs[2:3] += total_rows(cot * hat_2)
        vecs[3:4] += total_rows(cot)
        grad_second = norm_backward(cot * gain_2[...], hat_2, scale_2)
        vecs[4:5] += total_rows(grad_second)
        gs_low = grad_second.astype(LOW)
        gs_all[rows, :D] = gs_low
        grad_first = grad_second
        index = 0
        for which, (win, b_in, wout) in enumerate(halves):
            for a, z in chunks:
                grad_inner = (mm(gs_low, wout[:, a:z]) * slopes[index]).astype(LOW)
                index += 1
                inner[which, rows, a:z] = grad_inner
                grad_first = grad_first + mm_nt(grad_inner, win[:, a:z])
        vecs[0:1] += total_rows(grad_first * hat_1)
        vecs[1:2] += total_rows(grad_first)
        grad_pre = norm_backward(grad_first * gain_1[...], hat_1, scale_1)
        o_first[s] = grad_pre
        grad_branch = grad_pre.astype(LOW)
        gb_all[rows] = grad_branch
        o_ga[s] = mm_nt(grad_branch, wo[...])
    mover.start(o_act, act_out)
    mover.start(o_first, first_out)
    mover.start(o_ga, ga_out)
    grad_out = None
    for s in range(2):
        part = mm(att[s].T, gb_all[SEG * s : SEG * s + SEG])
        grad_out = part if grad_out is None else grad_out + part
    grad_out = mm(expander(ROWS), grad_out.astype(LOW))
    grad_out = (grad_out + mm(pick_rows(8), vecs[...].astype(LOW))).astype(LOW)
    for block in range(3):
        o_out[block] = grad_out[:, 128 * block : 128 * block + 128]
    mover.start(o_out, blocks_out)
    out_rest = mm(grad_out[:, 384:], placer(REST, 2 * REST))
    in_t = low_in[...].T[:ROWS]
    gs_t = gs_all[...].T[:ROWS]
    full = hidden_units // 128
    for which, pack, target in ((1, o_other, other_out), (0, o_own, own_out)):
        rest = out_rest
        for m, (left, right) in enumerate(((in_t, inner), (gs_t, active))):
            for a, z in chunks:
                grads = mm(left, right[which, :, a:z]).astype(LOW)
                for block in range(a // 128, min(-(-z // 128), full)):
                    part = grads[:, 128 * block - a : 128 * block - a + 128]
                    put(pack, ROWS * (full * m + block), part)
                if z > 128 * full:
                    rest = rest + mm(grads[:, 128 * full - a :], placer(REST, m * REST))
        put(pack, ROWS * 2 * full, rest.astype(LOW))
        mover.start(pack, target)
    for p in range(PAIRS):
        for s in range(2):
            for copy in step_copies(p, s):
                copy.wait()
    mover.finish()


def norm_forward(values):
    centred = values - jnp.mean(values, axis=1, keepdims=True)
    scale = lax.rsqrt(jnp.mean(centred * centred, axis=1, keepdims=True) + EPSILON)
    return centred * scale, scale


def norm_backward(grad, x_hat, scale):
    return scale * (
        grad
        - jnp.mean(grad, axis=1, keepdims=True)
        - x_hat * jnp.mean(grad * x_hat, axis=1, keepdims=True)
    )


GELU_A = math.sqrt(2.0 / math.pi)
GELU_B = 0.044715


def gelu_both(x):
    square = x * x
    bent = jnp.tanh(x * (GELU_A + (GELU_A * GELU_B) * square))
    half_up = 0.5 + 0.5 * bent
    slope = half_up + (0.5 * x) * (1.0 - bent * bent) * (GELU_A + (3.0 * GELU_A * GELU_B) * square)
    return x * half_up, slope


def total_rows(values):
    return jnp.sum(values, axis=0, keepdims=True)


def placer(count, offset):
    row = lax.broadcasted_iota(jnp.int32, (count, 128), 0)
    lane = lax.broadcasted_iota(jnp.int32, (count, 128), 1)
    return jnp.where(lane == row + offset, 1.0, 0.0).astype(LOW)


def put(ref, start, values):
    ref[start : start + values.shape[0]] = values


def pick_rows(count):
    row = lax.broadcasted_iota(jnp.int32, (ROWS, count), 0)
    lane = lax.broadcasted_iota(jnp.int32, (ROWS, count), 1)
    return jnp.where(row == D + lane, 1.0, 0.0).astype(LOW)


def back_kernel(*refs, pairs, size):
    refs = list(refs)

    def take(count):
        part = refs[:count]
        del refs[:count]
        return part

    probs_hbm, kv_hbm, uv_hbm, rel_hbm, ga_hbm, att_hbm, inv_hbm, joined_hbm, pos_hbm = take(9)
    earlier = take(8) if size else []
    outs = take(3)
    o_token = outs[0]
    probs, kv, uv, rel, ga, att, inv, joined, pos, scores, grel, dkv, wide, sums = take(14)
    if size:
        blocks, whole = take(2)
    mover = Mover(refs[0])
    loads = [([], []) for _ in pairs]
    for n, pair in enumerate(pairs):
        lanes = slice(128 * pair, 128 * pair + 128)
        loads[n][0].append(mover.start(rel_hbm.at[pair], rel.at[n]))
        for s in range(2):
            for source, target in ((ga_hbm, ga), (att_hbm, att), (inv_hbm, inv)):
                loads[n][s].append(mover.start(source.at[s, :, lanes], target.at[n, s]))
            for source, target in ((uv_hbm, uv), (kv_hbm, kv), (probs_hbm, probs)):
                loads[n][s].append(mover.start(source.at[pair, s], target.at[n, s]))
            if n == 0:
                loads[n][s].append(mover.start(joined_hbm.at[s], joined.at[s]))
    loads[0][1].append(mover.start(pos_hbm, pos))
    rest = []
    if size:
        rest.append(mover.start(earlier[1], blocks))
        base = 0
        for source, tops in zip(earlier[2:5], earlier[5:8]):
            count = source.shape[0]
            rest.append(mover.start(source, wide.at[pl.ds(base, count)]))
            rest.append(mover.start(tops, sums.at[pl.ds(base, count)]))
            base += count
    else:
        base = 0
    flip = reversal(HALF)
    first_head = lax.broadcasted_iota(jnp.int32, (HALF, 128), 1) < 64
    zero = jnp.zeros((HALF, 128), LOW)
    lane = lax.broadcasted_iota(jnp.int32, (SEG, 128), 1)
    into = lax.broadcasted_iota(jnp.int32, (128, 128), 0)
    out = lax.broadcasted_iota(jnp.int32, (128, 128), 1)
    head_sum = jnp.where(((out & 62) == 62) & ((into >> 6) == (out >> 6)), 1.0, 0.0).astype(LOW)
    for n in range(len(pairs)):
        grel[...] = jnp.zeros_like(grel)
        weight_kv, weight_q = None, None
        sum_u = jnp.zeros((1, 128), F32)
        sum_v = jnp.zeros((1, 128), F32)
        for s in range(2):
            mover.wait(*loads[n][s])
            key_rows = kv[n, s, :, :128]
            value_rows = kv[n, s, :, 128:]
            wide_grad = ga[n, s]
            inverse = inv[n, s]
            inner = wide_grad * att[n, s]
            inner_high = inner.astype(LOW)
            inner_low = (inner - inner_high.astype(F32)).astype(LOW)
            row_sums = (mm(inner_high, head_sum) + mm(inner_low, head_sum)) * inverse
            sums_high = row_sums.astype(LOW).astype(F32)
            grad_att = jnp.where(
                (lane & 63) == 62,
                -sums_high,
                jnp.where((lane & 63) == 63, sums_high - row_sums, wide_grad * inverse),
            ).astype(LOW)
            u_t = uv[n, s, :, :128].T
            ga_t = grad_att.T
            grad_q = []
            for b in range(2):
                count = KEYS if b else KEYS - HALF
                width = count + HALF
                rows = slice(HALF * b, HALF * b + HALF)
                start_row = HALF - HALF * b
                v_t = mm(flip, uv[n, s, rows, 128:]).astype(LOW).T
                part = grad_att[rows]
                both = jnp.concatenate(
                    [jnp.where(first_head, part, zero), jnp.where(first_head, zero, part)], axis=0
                )
                grad_probs = mm_nt(both, value_rows[:count])
                turned, spread = [], []
                for h in range(2):
                    attn = probs[n, s, h, rows, :count].astype(F32)
                    grad_scores = (attn * grad_probs[HALF * h : HALF * h + HALF]).astype(LOW)
                    scores[s, h, rows, :count] = grad_scores
                    if b == 0:
                        scores[s, h, rows, count:] = jnp.zeros((HALF, HALF), LOW)
                    back = mm(flip, grad_scores)
                    turned.append(back.astype(LOW))
                    back = jnp.concatenate([back, jnp.zeros((HALF, HALF), F32)], axis=1)
                    spread.append(pltpu.roll(back, 0, 1, stride=1, stride_axis=0).astype(LOW))
                    grel[64 * h : 64 * h + 64, start_row : start_row + width] += mm(
                        v_t[64 * h : 64 * h + 64], spread[h]
                    )
                grad_u = mm(jnp.concatenate(turned, axis=0), key_rows[:count])
                grad_v = mm(jnp.concatenate(spread, axis=0), rel[n, start_row : start_row + width])
                grad_u = jnp.where(first_head, grad_u[:HALF], grad_u[HALF:]) * FACTOR
                grad_v = jnp.where(first_head, grad_v[:HALF], grad_v[HALF:]) * FACTOR
                sum_u = sum_u + total_rows(grad_u)
                sum_v = sum_v + total_rows(grad_v)
                grad_q.append(mm(flip, (grad_u + grad_v).astype(LOW)).astype(LOW))
            for h in range(2):
                part = slice(64 * h, 64 * h + 64)
                dkv[s, part] = (mm(u_t[part], scores[s, h]) * FACTOR).astype(LOW)
                dkv[s, 128 + 64 * h : 192 + 64 * h] = mm(ga_t[part], probs[n, s, h]).astype(LOW)
            grad_queries = jnp.concatenate(grad_q, axis=0)
            o_token[n, s, :, :128] = grad_queries
            o_token[n, s, :, 128:] = dkv[s, :, MEM:].T
            part_kv = mm(dkv[s], joined[s])
            part_q = mm(grad_queries.T, joined[s, MEM:])
            weight_kv = part_kv if weight_kv is None else weight_kv + part_kv
            weight_q = part_q if weight_q is None else weight_q + part_q
        spot = base + n
        wide[spot, :128] = weight_q.astype(LOW)
        wide[spot, 128:384] = weight_kv.astype(LOW)
        wide[spot, 384:] = mm((grel[...] * FACTOR).astype(LOW), pos[...]).astype(LOW)
        sums[spot] = jnp.concatenate([sum_u, sum_v, jnp.zeros((6, 128), F32)], axis=0)
    if size:
        mover.wait(*rest)
        pack_attention(earlier[0], blocks, wide, sums, outs[1], outs[2], whole)
    else:
        outs[1][...] = wide[...]
        outs[2][...] = sums[...]


def pack_attention(place, out_blocks, wides, sums, keep, send, whole):
    core = place[0]
    pick = expander(ROWS)
    back = compressor()
    rest = jnp.zeros((ROWS, 128), F32)
    for m in range(4):
        total = None
        for p in range(PAIRS):
            part = mm(pick[:, 128 * p : 128 * p + 128], wides[p, 128 * m : 128 * m + 128])
            total = part if total is None else total + part
        if m == 0:
            vectors = None
            for p in range(PAIRS):
                part = mm(sums[p].astype(LOW), back[128 * p : 128 * p + 128])
                vectors = part if vectors is None else vectors + part
            total = total + mm(pick_rows(8), vectors.astype(LOW))
        total = total.astype(LOW)
        for block in range(3):
            whole[3 * m + block] = total[:, 128 * block : 128 * block + 128]
        rest = rest + mm(total[:, 384:], placer(REST, m * REST))
    whole[12] = rest.astype(LOW)
    for block in range(3):
        whole[13 + block] = out_blocks[block]
    half = whole.shape[0] // 2
    for block in range(half):
        keep[ROWS * block : ROWS * block + ROWS] = whole[core * half + block]
        send[ROWS * block : ROWS * block + ROWS] = whole[(1 - core) * half + block]
    if keep.shape[0] > half * ROWS:
        extra = keep.shape[0] - half * ROWS
        keep[half * ROWS :] = jnp.zeros((extra, 128), LOW)
        send[half * ROWS :] = jnp.zeros((extra, 128), LOW)


def input_kernel(first_grad, t0, t1, t2, t3, wq, wkv, o_input):
    for s in range(2):
        total = first_grad[s]
        p = 0
        for tokens in (t0, t1, t2, t3):
            for n in range(tokens.shape[0]):
                total = total + mm_nt(tokens[n, s, :, :128], wq[p])
                total = total + mm_nt(tokens[n, s, :, 128:], wkv[p])
                p += 1
        o_input[s] = total


def gathered(where, target, base, pieces, per_side):
    size = pieces[0].shape[0] // per_side
    for side, ref in enumerate(pieces):

        def body(r, carry, side=side, ref=ref):
            spot = jnp.bitwise_xor(r + side * per_side, where)
            row = pl.multiple_of(base + spot * size, 16)
            target[pl.ds(row, size)] = ref[pl.ds(pl.multiple_of(r * size, 16), size)]
            return carry

        lax.fori_loop(0, per_side, body, 0)


def unpack_attention_kernel(
    places, a0, a1, b0, b1, o_rest, o_query, o_key, o_value, o_pos, o_out,
    o_vec_a, o_vec_b, whole, *, per_side
):
    core = places[2]
    total = 2 * a0.shape[0]
    gathered(places[0], whole, core * total, (a0, a1), per_side)
    gathered(places[1], whole, (1 - core) * total, (b0, b1), per_side)
    half = HALF_BLOCKS

    def fetch(block):
        start = (block // half) * total + ROWS * (block % half)
        return whole[start : start + ROWS]

    unit = identity(128)
    rest = fetch(12)
    for m, ref in enumerate((o_query, o_key, o_value, o_pos)):
        for block in range(3):
            part = fetch(3 * m + block)
            ref[128 * block : 128 * block + 128, :] = mm_nt(unit, part)[:, :D]
            if m == 0:
                o_vec_b[:, 128 * block : 128 * block + 128] = part[400:].astype(F32)[8:]
        tail = mm_nt(placer(REST, m * REST), rest)
        ref[384:, :] = tail[:, :D]
        if m == 0:
            o_vec_b[:, 384:] = rest[400:, :REST].astype(F32)[8:]
    for block in range(3):
        part = fetch(13 + block).astype(F32)
        o_out[:, 128 * block : 128 * block + 128] = part[:D]
        o_vec_a[:, 128 * block : 128 * block + 128] = part[408:]
    tail = mm_nt(o_rest[...], placer(REST, 2 * REST))
    o_out[:, 384:] = tail[:D]
    o_vec_a[:, 384:] = tail[408:]


def unpack_ffn_kernel(places, a0, a1, o_in, o_bias, o_out_t, o_rest, whole, *, per_side):
    gathered(places[0], whole, 0, (a0, a1), per_side)
    units = o_in.shape[1]
    full = units // 128
    for block in range(full):
        lanes = slice(128 * block, 128 * block + 128)
        part = whole[ROWS * block : ROWS * block + ROWS].astype(F32)
        o_in[:, lanes] = part[:D]
        o_bias[:, lanes] = part[D : D + 1]
        start = ROWS * (full + block)
        o_out_t[:, lanes] = whole[start : start + ROWS].astype(F32)[:D]
    rest = whole[ROWS * 2 * full : ROWS * 2 * full + ROWS]
    o_rest[...] = rest
    left = units - 128 * full
    part = mm_nt(rest, placer(left, 0))
    o_in[:, 128 * full :] = part[:D]
    o_bias[:, 128 * full :] = part[D : D + 1]
    o_out_t[:, 128 * full :] = mm_nt(rest, placer(left, left))[:D]


def whole_spec():
    return pl.BlockSpec(memory_space=pltpu.VMEM)


def far_spec():
    return pl.BlockSpec(memory_space=pltpu.HBM)


def scalar_spec():
    return pl.BlockSpec(memory_space=pltpu.SMEM)


def params():
    return pltpu.CompilerParams(vmem_limit_bytes=VMEM_BYTES)


def cost(flops, moved):
    return pl.CostEstimate(flops=int(flops), bytes_accessed=int(moved), transcendentals=0)


def shape(dims, dtype=LOW):
    return jax.ShapeDtypeStruct(dims, dtype)


def prepare(w_query, w_key, w_value, w_pos, w_out, bias_u, bias_v, pos_table):
    operands = (w_query, w_key, w_value, w_pos, w_out, bias_u[None], bias_v[None], pos_table)
    results = (
        ((PAIRS, D, 128), LOW),
        ((PAIRS, D, 256), LOW),
        ((PAIRS, SPAN, 128), LOW),
        ((WIDE, D), LOW),
        ((PAIRS, 2, 8, 128), F32),
    )
    return pl.pallas_call(
        prep_kernel,
        out_shape=tuple(shape(*r) for r in results),
        in_specs=[far_spec()] * len(operands),
        out_specs=(far_spec(),) * len(results),
        scratch_shapes=[pltpu.VMEM(a.shape, a.dtype) for a in operands]
        + [pltpu.VMEM(*r) for r in results]
        + [pltpu.SemaphoreType.DMA((16,))],
        compiler_params=params(),
        cost_estimate=cost(3e9, 5e6),
        name="prepare_weights",
    )(*operands)


def layer(place, seg_len, mem_len, rows, reset, wq, wkv, rel, bias, wo, out_grads, own, other, vectors, size):
    units = own[0].shape[1]
    weights = (own[0], other[0], own[1], other[1], own[2], other[2])
    operands = (*rows, reset, wq, wkv, rel, bias, wo, *out_grads, *weights, *vectors)
    results = (
        ((PAIRS, 2, 2, SEG, KEYS), LOW),
        ((PAIRS, 2, KEYS, 256), LOW),
        ((PAIRS, 2, SEG, 256), LOW),
        ((2, SEG, WIDE), F32),
        ((2, SEG, WIDE), F32),
        ((2, KEYS, D), LOW),
        ((2, SEG, D), LOW),
        ((2, SEG, D), F32),
        ((2, SEG, WIDE), F32),
        ((size, 128), LOW),
        ((size, 128), LOW),
        ((3, ROWS, 128), LOW),
    )
    return pl.pallas_call(
        layer_kernel,
        out_shape=tuple(shape(*r) for r in results),
        in_specs=[scalar_spec()] * 3 + [far_spec()] * len(operands),
        out_specs=(far_spec(),) * len(results),
        scratch_shapes=[pltpu.VMEM(a.shape, a.dtype) for a in operands]
        + [pltpu.VMEM(*r) for r in results]
        + [
            pltpu.VMEM((4, 4 * D, 128), F32),
            pltpu.VMEM((2, SEG, KEYS), F32),
            pltpu.VMEM((2, SEG, D), LOW),
            pltpu.VMEM((2 * SEG, 512), LOW),
            pltpu.VMEM((2 * SEG, D), LOW),
            pltpu.VMEM((2 * SEG, 512), LOW),
            pltpu.VMEM((2, 2 * SEG, units), LOW),
            pltpu.VMEM((2, 2 * SEG, units), LOW),
            pltpu.VMEM((8, D), F32),
            pltpu.VMEM((2, SEG, WIDE), LOW),
            pltpu.SemaphoreType.DMA((32,)),
            pltpu.SemaphoreType.DMA((3, PAIRS, 2)),
        ],
        compiler_params=params(),
        cost_estimate=cost(2e10, 3e7),
        name="layer",
    )(place, seg_len, mem_len, *operands)


def attend_back(pairs, operands, extra=(), size=0):
    count = len(pairs)
    total = PAIRS if size else count
    results = [shape((count, 2, SEG, 384))]
    if size:
        results += [shape((size, 128)), shape((size, 128))]
    else:
        results += [shape((count, 512, D)), shape((count, 8, 128), F32)]
    scratch = [
        pltpu.VMEM((count, 2, 2, SEG, KEYS), LOW),
        pltpu.VMEM((count, 2, KEYS, 256), LOW),
        pltpu.VMEM((count, 2, SEG, 256), LOW),
        pltpu.VMEM((count, SPAN, 128), LOW),
        pltpu.VMEM((count, 2, SEG, 128), F32),
        pltpu.VMEM((count, 2, SEG, 128), F32),
        pltpu.VMEM((count, 2, SEG, 128), F32),
        pltpu.VMEM((2, KEYS, D), LOW),
        pltpu.VMEM((SPAN, D), LOW),
        pltpu.VMEM((2, 2, SEG, KEYS), LOW),
        pltpu.VMEM((128, SPAN), F32),
        pltpu.VMEM((2, 256, KEYS), LOW),
        pltpu.VMEM((total, 512, D), LOW),
        pltpu.VMEM((total, 8, 128), F32),
    ]
    if size:
        scratch += [pltpu.VMEM(extra[1].shape, LOW), pltpu.VMEM((2 * HALF_BLOCKS, ROWS, 128), LOW)]
    return pl.pallas_call(
        functools.partial(back_kernel, pairs=pairs, size=size),
        out_shape=tuple(results),
        in_specs=[far_spec()] * 9 + ([scalar_spec()] + [far_spec()] * 7 if size else []),
        out_specs=(whole_spec(),) * 3,
        scratch_shapes=scratch + [pltpu.SemaphoreType.DMA((40,))],
        compiler_params=params(),
        cost_estimate=cost(1.5e10 * count, 8e6),
        name=f"attend_back_{pairs[0]}",
    )(*operands, *extra)


def input_gradient(first_grad, tokens, wq, wkv):
    return pl.pallas_call(
        input_kernel,
        out_shape=shape((2, SEG, D), F32),
        in_specs=[whole_spec()] * (3 + len(tokens)),
        out_specs=whole_spec(),
        compiler_params=params(),
        cost_estimate=cost(1.6e9, 6e6),
        name="input_gradient",
    )(first_grad, *tokens, wq, wkv)


def unpack_attention(places, pieces, rest, dp_size):
    total = sum(p.shape[0] for p in pieces)
    return pl.pallas_call(
        functools.partial(unpack_attention_kernel, per_side=dp_size // 2),
        out_shape=(shape((D, D), F32),) * 5 + (shape((8, D), F32),) * 2,
        in_specs=[scalar_spec()] + [whole_spec()] * 5,
        out_specs=(whole_spec(),) * 7,
        scratch_shapes=[pltpu.VMEM((total, 128), LOW)],
        compiler_params=params(),
        cost_estimate=cost(5e8, 6e6),
        name="unpack_attention",
    )(places, *pieces, rest)


def unpack_ffn(places, pieces, units, dp_size):
    total = sum(p.shape[0] for p in pieces)
    return pl.pallas_call(
        functools.partial(unpack_ffn_kernel, per_side=dp_size // 2),
        out_shape=(
            shape((D, units), F32), shape((1, units), F32), shape((D, units), F32),
            shape((ROWS, 128)),
        ),
        in_specs=[scalar_spec()] + [whole_spec()] * 2,
        out_specs=(whole_spec(),) * 4,
        scratch_shapes=[pltpu.VMEM((total, 128), LOW)],
        compiler_params=params(),
        cost_estimate=cost(5e8, 6e6),
        name="unpack_ffn",
    )(places, *pieces)


def swap(values):
    return lax.ppermute(values, "tp", [(0, 1), (1, 0)])


def orders_of(dp_size):
    bits = list(range(dp_size.bit_length() - 1))
    turned = list(bits)
    for k in range(0, len(bits) - 1, 2):
        turned[k], turned[k + 1] = bits[k + 1], bits[k]
    return bits, turned


class Ring:
    def __init__(self, dp_size, index, core):
        self.size, self.orders = dp_size, orders_of(dp_size)
        self.steps = len(self.orders[0])
        self.bits = [
            jnp.where(core == 0, (index >> a) & 1, (index >> b) & 1)
            for a, b in zip(*self.orders)
        ]

    def place(self, index, order):
        spot = 0
        for k in self.orders[order]:
            spot = 2 * spot + ((index >> k) & 1)
        return spot

    def send(self, values, step):
        pairs = []
        for i in range(self.size):
            for c in range(2):
                pairs.append((2 * i + c, 2 * (i ^ (1 << self.orders[c][step])) + c))
        return lax.ppermute(values, ("dp", "tp"), pairs)

    def sides(self, keep, came, step):
        rows = keep.shape[0] // 2
        bit = self.bits[step]

        def side(which):
            start = which * rows
            return lax.dynamic_slice_in_dim(keep, start, rows, 0) + lax.dynamic_slice_in_dim(
                came, start, rows, 0
            )

        return side(1 - bit), side(bit)


def after(value, *others):
    return lax.optimization_barrier((value,) + others)


def rounded_rows(rows, unit):
    return -(-rows // unit) * unit


def make_shards(dp_size):
    table = position_table()

    def shards(
        hidden, memory, segment_length, memory_length, doc_reset, w_query, w_key, w_value, w_pos,
        bias_u, bias_v, w_out, first_gain, first_shift, ffn_in, ffn_in_bias, ffn_out, ffn_out_bias,
        second_gain, second_shift, out_grad,
    ):
        core = lax.axis_index("tp")
        index = lax.axis_index("dp")
        place = core[None].astype(jnp.int32)
        units = ffn_in.shape[1]
        pos_table = jnp.asarray(table)

        def by_feature(values):
            return values.transpose(2, 0, 1).reshape(-1, values.shape[1])

        hidden_t, memory_t, out_grad_t = (by_feature(a) for a in (hidden, memory, out_grad))
        hidden_in, memory_in, out_grad_in = swap(hidden_t), swap(memory_t), swap(out_grad_t)
        own_ffn = (ffn_in, ffn_in_bias[None], ffn_out.T)
        other_ffn = tuple(swap(a) for a in own_ffn)

        wq, wkv, rel, wo, bias = prepare(
            w_query, w_key, w_value, w_pos, w_out, bias_u, bias_v, pos_table
        )
        full = units // 128
        unit = 16 * dp_size
        (
            probs, kv, uv, att, inv, joined, act, first_grad, ga, ffn_own, ffn_other, out_blocks
        ) = layer(
            place, segment_length, memory_length, (hidden_t, memory_t, hidden_in, memory_in),
            doc_reset, wq, wkv, rel, bias, wo, (out_grad_t, out_grad_in), own_ffn, other_ffn,
            tuple(v[None] for v in (first_gain, first_shift, ffn_out_bias, second_gain, second_shift)),
            rounded_rows(ROWS * (2 * full + 1), unit),
        )
        ring = Ring(dp_size, index, core)
        straight, turned = ring.place(index, 0), ring.place(index, 1)
        places = jnp.stack(
            [
                jnp.where(core == 0, straight, turned),
                jnp.where(core == 0, turned, straight),
                core,
            ]
        ).astype(jnp.int32)

        def give_back(values, dtype):
            rows = values.shape[1] // 2
            mine = lax.dynamic_slice_in_dim(values, core * rows, rows, 1)
            theirs = lax.dynamic_slice_in_dim(values, (1 - core) * rows, rows, 1)
            came = swap(theirs.astype(LOW)).astype(dtype)
            mine = mine.astype(dtype)
            return jnp.where(
                core == 0,
                jnp.concatenate([mine, came], axis=0),
                jnp.concatenate([came, mine], axis=0),
            )

        groups = ((0, 1), (2,), (3,), (4,))
        tokens, wides, biases = [], [], []
        steps = ring.steps
        keep, came = ffn_own, swap(ffn_other)
        slots = max(steps, len(groups))
        for slot in range(slots):
            if slot < steps:
                sent, kept = ring.sides(keep, came, slot)
                sent, kept, ga = after(sent, kept, ga)
                keep, came = kept, ring.send(sent, slot)
            if slot < len(groups):
                last = slot == len(groups) - 1
                result = attend_back(
                    groups[slot],
                    (probs, kv, uv, rel, ga, att, inv, joined, pos_table),
                    (place, out_blocks, *wides, *biases) if last else (),
                    rounded_rows(ROWS * HALF_BLOCKS, unit) if last else 0,
                )
                came, *result = after(came, *result)
                tokens.append(result[0])
                if last:
                    att_keep, att_send = result[1:]
                else:
                    wides.append(result[1])
                    biases.append(result[2])
        values = keep + came
        spread = ring.send(values, steps - 1)
        att_came = swap(att_send)
        gathers = list(range(steps - 2, -1, -1))
        for step in range(steps):
            sent, kept = ring.sides(att_keep, att_came, step)
            att_keep, att_came = kept, ring.send(sent, step)
            if gathers:
                if len(gathers) > 0 and step < steps - 1:
                    values = jnp.concatenate([values, spread], axis=0)
                    spread = ring.send(values, gathers.pop(0))
            if step == 0:
                input_own = input_gradient(first_grad, tokens, wq, wkv)
                att_came, input_own = after(att_came, input_own)
            elif step == 1:
                activations, input_grad = give_back(act, LOW), give_back(input_own, F32)
                att_came, activations, input_grad = after(att_came, activations, input_grad)
        ffn_pieces = (values, spread)
        values = att_keep + att_came
        for step in range(steps - 1, 0, -1):
            came = ring.send(values, step)
            if step == 1:
                filled = unpack_ffn(places, ffn_pieces, units, dp_size)
                came, *filled = after(came, *filled)
            values = jnp.concatenate([values, came], axis=0)
        grad_in, grad_in_bias, grad_ffn_out_t, rest = filled
        came = ring.send(values, 0)
        near = swap(values)
        came, near = after(came, near)
        g_query, g_key, g_value, g_pos, g_out, vec_a, vec_b = unpack_attention(
            places, (values, came, near, swap(came)), rest, dp_size
        )

        rows = hidden.shape[1]
        positions = core * rows + jnp.arange(rows)
        later = (jnp.arange(SEG)[:, None] > positions[None, :]).astype(LOW)
        resets = jnp.dot(doc_reset.astype(LOW), later, preferred_element_type=F32)
        keep = (resets == 0.0) & (positions[None, :] < segment_length[:, None])
        new_memory = jnp.where(keep[:, :, None], hidden, jnp.zeros_like(hidden))
        return (
            new_memory, activations, input_grad, g_query, g_key, g_value, g_pos,
            vec_b[2], vec_b[3], g_out, vec_a[2], vec_a[3],
            grad_in, grad_in_bias[0], grad_ffn_out_t.T, vec_a[6], vec_a[4], vec_a[5],
        )

    return shards


def solution(mesh):
    rows, copied = P("dp", "tp", None), P()
    shards = make_shards(mesh.shape["dp"])
    return jax.shard_map(
        shards,
        mesh=mesh,
        in_specs=(
            rows, rows, P("dp"), P("dp"), P("dp", None),
            copied, copied, copied, copied, copied, copied, copied, copied, copied,
            P(None, "tp"), P("tp"), P("tp", None),
            copied, copied, copied, rows,
        ),
        out_specs=(
            rows, rows, rows, copied, copied, copied, copied, copied, copied, copied, copied, copied,
            P(None, "tp"), P("tp"), P("tp", None), copied, copied, copied,
        ),
        check_vma=False,
    )
```

```python
import functools
import math

import jax
import jax.numpy as jnp
import ml_dtypes
import numpy as np
from jax import lax
from jax.experimental import pallas as pl
from jax.experimental.layout import Layout, with_layout_constraint
from jax.experimental.pallas import tpu as pltpu
from jax.sharding import PartitionSpec as P

D = 410
HEADS = 10
DHEAD = 41
SEG = 256
MEM = 256
KEYS = MEM + SEG
HALF = 128
PAIRS = HEADS // 2
WIDE = PAIRS * 128
ROWS = 416
SPAN = 768
REST = 26
HALF_BLOCKS = 8
EPSILON = 1e-05
NEG_LARGE = -1e30
FACTOR = 1.0 / math.sqrt(DHEAD)
LOG2E = 1.0 / math.log(2.0)
LOW = jnp.bfloat16
VMEM_BYTES = 60 * 1024 * 1024
LESS_BYTES = 24 * 1024 * 1024
F32 = jnp.float32


def position_table():
    distance = (KEYS - 1 - np.arange(SPAN)).astype(np.float32)
    inverse = np.float32(1.0) / np.float32(10000.0) ** (
        np.arange(0, D, 2).astype(np.float32) / np.float32(D)
    )
    angles = distance[:, None] * inverse[None, :].astype(np.float32)
    table = np.concatenate([np.sin(angles), np.cos(angles)], axis=1)
    return table.astype(ml_dtypes.bfloat16)


def mm(left, right):
    return lax.dot_general(left, right, (((1,), (0,)), ((), ())), preferred_element_type=F32)


def mm_nt(left, right):
    return lax.dot_general(left, right, (((1,), (1,)), ((), ())), preferred_element_type=F32)


def expander(rows):
    row = lax.broadcasted_iota(jnp.int32, (rows, WIDE), 0)
    lane = lax.broadcasted_iota(jnp.int32, (rows, WIDE), 1)
    inside = lane & 63
    hit = (inside < DHEAD) & (row == (lane >> 6) * DHEAD + inside)
    return jnp.where(hit, 1.0, 0.0).astype(LOW)


def compressor():
    row = lax.broadcasted_iota(jnp.int32, (WIDE, D), 0)
    lane = lax.broadcasted_iota(jnp.int32, (WIDE, D), 1)
    inside = row & 63
    hit = (inside < DHEAD) & (lane == (row >> 6) * DHEAD + inside)
    return jnp.where(hit, 1.0, 0.0).astype(LOW)


def identity(size):
    row = lax.broadcasted_iota(jnp.int32, (size, size), 0)
    lane = lax.broadcasted_iota(jnp.int32, (size, size), 1)
    return jnp.where(row == lane, 1.0, 0.0).astype(LOW)


def reversal(size):
    row = lax.broadcasted_iota(jnp.int32, (size, size), 0)
    lane = lax.broadcasted_iota(jnp.int32, (size, size), 1)
    return jnp.where(row + lane == size - 1, 1.0, 0.0).astype(LOW)


class Mover:
    def __init__(self, sems):
        self.sems, self.used, self.open = sems, 0, []

    def start(self, source, target):
        copy = pltpu.make_async_copy(source, target, self.sems.at[self.used])
        self.used += 1
        copy.start()
        self.open.append(copy)
        return copy

    def finish(self):
        for copy in self.open:
            copy.wait()
        self.open = []

    def wait(self, *copies):
        for copy in copies:
            copy.wait()
        self.open = [c for c in self.open if all(c is not d for d in copies)]


def prep_kernel(
    wq_in, wk_in, wv_in, wp_in, wo_in, bias_u_in, bias_v_in, pos_in, q_out, kv_out, rel_out, wo_out,
    bias_out, wq, wk, wv, wp, wo, bias_u, bias_v, pos, o_q, o_kv, o_rel, o_wo, o_bias, sems
):
    mover = Mover(sems)
    loads = [
        mover.start(a, b)
        for a, b in zip(
            (wp_in, pos_in, wk_in, wv_in, wq_in, wo_in, bias_u_in, bias_v_in),
            (wp, pos, wk, wv, wq, wo, bias_u, bias_v),
        )
    ]
    expand = expander(D)
    mover.wait(*loads[:2])
    rel = mm(pos[...], wp[...]).astype(LOW)
    rel = mm(rel, expand).astype(LOW)
    for p in range(PAIRS):
        o_rel[p] = rel[:, 128 * p : 128 * p + 128]
    mover.start(o_rel, rel_out)
    mover.wait(*loads[2:4])
    k_wide = mm(wk[...], expand).astype(LOW)
    v_wide = mm(wv[...], expand).astype(LOW)
    for p in range(PAIRS):
        o_kv[p, :, :128] = k_wide[:, 128 * p : 128 * p + 128]
        o_kv[p, :, 128:] = v_wide[:, 128 * p : 128 * p + 128]
    mover.start(o_kv, kv_out)
    mover.wait(*loads[4:])
    q_wide = mm(wq[...], expand).astype(LOW)
    for p in range(PAIRS):
        o_q[p] = q_wide[:, 128 * p : 128 * p + 128]
    mover.start(o_q, q_out)
    o_wo[...] = mm(compressor(), wo[...]).astype(LOW)
    mover.start(o_wo, wo_out)
    for bias_index, bias in enumerate((bias_u, bias_v)):
        value = jnp.broadcast_to(bias[...], (8, D))
        high = value.astype(LOW)
        rest = value - high.astype(F32)
        middle = rest.astype(LOW)
        last = (rest - middle.astype(F32)).astype(LOW)
        wide = mm(high, expand) + mm(middle, expand) + mm(last, expand)
        for p in range(PAIRS):
            o_bias[p, bias_index] = wide[:, 128 * p : 128 * p + 128]
    mover.start(o_bias, bias_out)
    mover.finish()


def spread_streams(source, raw, core, unit, store):
    raw[...] = source[...].astype(F32)
    for s in range(2):
        columns = raw[pl.ds(2 * core + s, D, stride=4), :].astype(LOW)
        store(s, mm_nt(unit, columns).astype(LOW))


def layer_kernel(
    place, seg_len, mem_len, hidden_hbm, memory_hbm, hidden_in_hbm, memory_in_hbm, reset_hbm,
    wq_hbm, wkv_hbm, rel_hbm, bias_hbm, wo_hbm, out_grad_hbm, out_grad_in_hbm,
    win_a_hbm, win_b_hbm, bin_a_hbm, bin_b_hbm, wout_a_hbm, wout_b_hbm,
    gain_1_hbm, shift_1_hbm, bias_out_hbm, gain_2_hbm, shift_2_hbm,
    probs_out, kv_out, uv_out, att_out, inv_out, joined_out,
    act_out, first_out, ga_out, own_out, other_out, blocks_out,
    hidden, memory, hidden_in, memory_in, reset, wq, wkv, rel, bias, wo, out_grad, out_grad_in,
    win_a, win_b, bin_a, bin_b, wout_a, wout_b, gain_1, shift_1, bias_out, gain_2, shift_2,
    o_probs, o_kv, o_uv, o_att, o_inv, o_joined, o_act, o_first, o_ga, o_own, o_other, o_out,
    raw, mask, og, low_in, gb_all, gs_all, active, inner, vecs, att, slopes, sems, step_sems
):
    mover = Mover(sems)
    loads = [
        mover.start(a, b)
        for a, b in zip(
            (
                memory_hbm, memory_in_hbm, hidden_hbm, hidden_in_hbm, reset_hbm,
                wkv_hbm, wq_hbm, bias_hbm, rel_hbm,
                gain_1_hbm, shift_1_hbm, bias_out_hbm, gain_2_hbm, shift_2_hbm, bin_a_hbm,
                bin_b_hbm, wo_hbm, out_grad_hbm, out_grad_in_hbm,
                win_a_hbm, wout_a_hbm, win_b_hbm, wout_b_hbm,
            ),
            (
                memory, memory_in, hidden, hidden_in, reset, wkv, wq, bias, rel,
                gain_1, shift_1, bias_out, gain_2, shift_2, bin_a,
                bin_b, wo, out_grad, out_grad_in, win_a, wout_a, win_b, wout_b,
            ),
        )
    ]
    core = place[0]
    mine = pl.multiple_of(HALF * core, HALF)
    other = pl.multiple_of(HALF * (1 - core), HALF)
    unit = identity(HALF)
    row = lax.broadcasted_iota(jnp.int32, (SEG, SEG), 0)
    lane = lax.broadcasted_iota(jnp.int32, (SEG, SEG), 1)
    lower = jnp.where(row >= lane, 1.0, 0.0).astype(LOW)
    for index, (source, base) in enumerate(
        ((memory, mine), (memory_in, other), (hidden, MEM + mine), (hidden_in, MEM + other))
    ):

        def store(s, values, base=base):
            o_joined[s, pl.ds(pl.multiple_of(base, HALF), HALF)] = values

        mover.wait(loads[index])
        spread_streams(source, raw.at[index], core, unit, store)
    mover.wait(*loads[4:9])
    mover.start(o_joined, joined_out)
    for s in range(2):
        own = 2 * core + s
        starts = jnp.broadcast_to(reset[pl.ds(own, 1), :].astype(F32), (8, SEG)).astype(LOW)
        doc_column = mm_nt(lower, starts)[:, :1]
        doc_row = mm_nt(starts, lower)[:1, :]
        memory_ok = (lane >= MEM - mem_len[own]) & (doc_column == 0.0)
        segment_ok = ((row > lane) & (doc_row == doc_column) & (lane < seg_len[own])) | (row == lane)
        mask[s, :, :MEM] = jnp.where(memory_ok, 0.0, NEG_LARGE)
        mask[s, :, MEM:] = jnp.where(segment_ok, 0.0, NEG_LARGE)
    first_head = lax.broadcasted_iota(jnp.int32, (HALF, 128), 1) < 64
    zero = jnp.zeros((HALF, 128), LOW)
    ones_lane = (lax.broadcasted_iota(jnp.int32, (KEYS, 256), 1) & 190) == 190

    for p in range(PAIRS):
        for s in range(2):
            pair_rows = jnp.where(ones_lane, 1.0, mm(o_joined[s], wkv[p])).astype(LOW)
            o_kv[p, s] = pair_rows
            queries = mm(o_joined[s, MEM:], wq[p])
            o_uv[p, s, :, :128] = (queries + bias[p, 0, :1]).astype(LOW)
            o_uv[p, s, :, 128:] = (queries + bias[p, 1, :1]).astype(LOW)

    def stacked(values):
        return jnp.concatenate(
            [jnp.where(first_head, values, zero), jnp.where(first_head, zero, values)], axis=0
        )

    def score(p, s, b):
        count = KEYS if b else KEYS - HALF
        rows = slice(HALF * b, HALF * b + HALF)
        start_row = HALF - HALF * b
        content = mm_nt(stacked(o_uv[p, s, rows, :128]), o_kv[p, s, :count, :128])
        relative = mm_nt(stacked(o_uv[p, s, rows, 128:]), rel[p, start_row : start_row + count])
        spots = mask[s, rows, :count]
        scores = []
        for h in range(2):
            part = slice(HALF * h, HALF * h + HALF)
            turned = pltpu.roll(relative[part], count - HALF + 1, 1, stride=1, stride_axis=0)
            scores.append((content[part] + turned) * (FACTOR * LOG2E) + spots)
        return scores

    def soften(p, s, b, scores):
        count = KEYS if b else KEYS - HALF
        rows = slice(HALF * b, HALF * b + HALF)
        exp_terms = []
        for h in range(2):
            top = jnp.max(scores[h], axis=1, keepdims=True)
            exp_terms.append(jnp.exp2(scores[h] - top).astype(LOW))
            o_probs[p, s, h, rows, :count] = exp_terms[h]
            if b == 0:
                o_probs[p, s, h, rows, count:] = jnp.zeros((HALF, HALF), LOW)
        return jnp.concatenate(exp_terms, axis=0)

    def mix(p, s, b, exp_terms):
        lanes = pl.ds(pl.multiple_of(128 * p, 128), 128)
        count = KEYS if b else KEYS - HALF
        rows = slice(HALF * b, HALF * b + HALF)
        mixed = mm(exp_terms, o_kv[p, s, :count, 128:])
        inverse = jnp.where(first_head, 1.0 / mixed[:HALF, 63:64], 1.0 / mixed[HALF:, 127:])
        o_inv[s, rows, lanes] = inverse
        o_att[s, rows, lanes] = jnp.where(first_head, mixed[:HALF], mixed[HALF:]) * inverse

    def step(p, carry):
        blocks = [(s, b) for s in range(2) for b in range(2)]
        scores, mixing = score(p, *blocks[0]), None
        for k, block in enumerate(blocks):
            following = score(p, *blocks[k + 1]) if k + 1 < len(blocks) else None
            exp_terms = soften(p, *block, scores)
            if mixing is not None:
                mix(p, *mixing)
            mixing, scores = (*block, exp_terms), following
        mix(p, *mixing)
        for s in range(2):
            for copy in step_copies(p, s):
                copy.start()
        return carry

    def step_copies(p, s):
        return [
            pltpu.make_async_copy(a.at[p, s], b.at[p, s], step_sems.at[k, p, s])
            for k, (a, b) in enumerate(((o_probs, probs_out), (o_kv, kv_out), (o_uv, uv_out)))
        ]

    lax.fori_loop(0, PAIRS, step, 0)
    mover.start(o_att, att_out)
    mover.start(o_inv, inv_out)
    hidden_units = win_a.shape[1]
    chunks = [(a, min(a + 256, hidden_units)) for a in range(0, hidden_units, 256)]
    halves = ((win_a, bin_a, wout_a), (win_b, bin_b, wout_b))
    low_in[:, 384:] = jnp.where(
        lax.broadcasted_iota(jnp.int32, (2 * SEG, 128), 1) == D - 384, 1.0, 0.0
    ).astype(LOW)
    gs_all[:, 384:] = jnp.zeros((2 * SEG, 128), LOW)
    vecs[...] = jnp.zeros_like(vecs)
    att[...] = o_att[...].astype(LOW)
    mover.wait(*loads[9:])
    for index, (source, base) in enumerate(((out_grad, mine), (out_grad_in, other))):

        def store_grad(s, values, base=base):
            og[s, pl.ds(base, HALF)] = values

        spread_streams(source, raw.at[index], core, unit, store_grad)
    tokens = 2 * SEG
    hid = o_joined[:, MEM:].reshape(tokens, D).astype(F32)
    hat_1, scale_1 = norm_forward(hid + mm(att[...].reshape(tokens, WIDE), wo[...]))
    first = hat_1 * gain_1[...] + shift_1[...]
    first_low = first.astype(LOW)
    low_in[:, :D] = first_low
    ffn_sum = first + bias_out[...]
    for which, (win, b_in, wout) in enumerate(halves):
        for a, z in chunks:
            pre = mm(first_low, win[:, a:z]) + b_in[:, a:z].astype(F32)
            act, slope = gelu_both(pre)
            act = act.astype(LOW)
            slopes[which, :, a:z] = slope
            active[which, :, a:z] = act
            ffn_sum = ffn_sum + mm_nt(act, wout[:, a:z])
    hat_2, scale_2 = norm_forward(ffn_sum)
    o_act[...] = (hat_2 * gain_2[...] + shift_2[...]).astype(LOW).reshape(2, SEG, D)
    cot = og[...].reshape(tokens, D).astype(F32)
    vecs[2:3] = total_rows(cot * hat_2)
    vecs[3:4] = total_rows(cot)
    grad_second = norm_backward(cot * gain_2[...], hat_2, scale_2)
    vecs[4:5] = total_rows(grad_second)
    gs_low = grad_second.astype(LOW)
    gs_all[:, :D] = gs_low
    grad_first = grad_second
    for which, (win, b_in, wout) in enumerate(halves):
        for a, z in chunks:
            grad_inner = (mm(gs_low, wout[:, a:z]) * slopes[which, :, a:z]).astype(LOW)
            inner[which, :, a:z] = grad_inner
            grad_first = grad_first + mm_nt(grad_inner, win[:, a:z])
    vecs[0:1] = total_rows(grad_first * hat_1)
    vecs[1:2] = total_rows(grad_first)
    grad_pre = norm_backward(grad_first * gain_1[...], hat_1, scale_1)
    o_first[...] = grad_pre.reshape(2, SEG, D)
    grad_branch = grad_pre.astype(LOW)
    gb_all[...] = grad_branch
    o_ga[...] = mm_nt(grad_branch, wo[...]).reshape(2, SEG, WIDE)
    mover.start(o_act, act_out)
    mover.start(o_first, first_out)
    mover.start(o_ga, ga_out)
    grad_out = None
    for s in range(2):
        part = mm(att[s].T, gb_all[SEG * s : SEG * s + SEG])
        grad_out = part if grad_out is None else grad_out + part
    grad_out = mm(expander(ROWS), grad_out.astype(LOW))
    grad_out = (grad_out + mm(pick_rows(8), vecs[...].astype(LOW))).astype(LOW)
    for block in range(3):
        o_out[block] = grad_out[:, 128 * block : 128 * block + 128]
    mover.start(o_out, blocks_out)
    out_rest = mm(grad_out[:, 384:], placer(REST, 2 * REST))
    in_t = low_in[...].T[:ROWS]
    gs_t = gs_all[...].T[:ROWS]
    full = hidden_units // 128
    for which, pack, target in ((1, o_other, other_out), (0, o_own, own_out)):
        rest = out_rest
        for m, (left, right) in enumerate(((in_t, inner), (gs_t, active))):
            for a, z in chunks:
                grads = mm(left, right[which, :, a:z]).astype(LOW)
                for block in range(a // 128, min(-(-z // 128), full)):
                    part = grads[:, 128 * block - a : 128 * block - a + 128]
                    put(pack, ROWS * (full * m + block), part)
                if z > 128 * full:
                    rest = rest + mm(grads[:, 128 * full - a :], placer(REST, m * REST))
        put(pack, ROWS * 2 * full, rest.astype(LOW))
        mover.start(pack, target)
    for p in range(PAIRS):
        for s in range(2):
            for copy in step_copies(p, s):
                copy.wait()
    mover.finish()


def norm_forward(values):
    centred = values - jnp.mean(values, axis=1, keepdims=True)
    scale = lax.rsqrt(jnp.mean(centred * centred, axis=1, keepdims=True) + EPSILON)
    return centred * scale, scale


def norm_backward(grad, x_hat, scale):
    return scale * (
        grad
        - jnp.mean(grad, axis=1, keepdims=True)
        - x_hat * jnp.mean(grad * x_hat, axis=1, keepdims=True)
    )


GELU_A = math.sqrt(2.0 / math.pi)
GELU_B = 0.044715


def gelu_both(x):
    square = x * x
    bent = jnp.tanh(x * (GELU_A + (GELU_A * GELU_B) * square))
    half_up = 0.5 + 0.5 * bent
    slope = half_up + (0.5 * x) * (1.0 - bent * bent) * (GELU_A + (3.0 * GELU_A * GELU_B) * square)
    return x * half_up, slope


def total_rows(values):
    return jnp.sum(values, axis=0, keepdims=True)


def placer(count, offset):
    row = lax.broadcasted_iota(jnp.int32, (count, 128), 0)
    lane = lax.broadcasted_iota(jnp.int32, (count, 128), 1)
    return jnp.where(lane == row + offset, 1.0, 0.0).astype(LOW)


def put(ref, start, values):
    ref[start : start + values.shape[0]] = values


def pick_rows(count):
    row = lax.broadcasted_iota(jnp.int32, (ROWS, count), 0)
    lane = lax.broadcasted_iota(jnp.int32, (ROWS, count), 1)
    return jnp.where(row == D + lane, 1.0, 0.0).astype(LOW)


def back_kernel(*refs, pairs, size):
    refs = list(refs)

    def take(count):
        part = refs[:count]
        del refs[:count]
        return part

    probs_hbm, kv_hbm, uv_hbm, rel_hbm, ga_hbm, att_hbm, inv_hbm, joined_hbm, pos_hbm = take(9)
    earlier = take(8) if size else []
    outs = take(3)
    o_token = outs[0]
    probs, kv, uv, rel, ga, att, inv, joined, pos, scores, spread, grel, dkv, wide, sums = take(15)
    if size:
        blocks, whole = take(2)
    mover = Mover(refs[0])
    loads = [([], []) for _ in pairs]
    for n, pair in enumerate(pairs):
        lanes = slice(128 * pair, 128 * pair + 128)
        for s in range(2):
            for source, target in ((ga_hbm, ga), (att_hbm, att), (inv_hbm, inv)):
                loads[n][s].append(mover.start(source.at[s, :, lanes], target.at[n, s]))
            for source, target in ((uv_hbm, uv), (kv_hbm, kv), (probs_hbm, probs)):
                loads[n][s].append(mover.start(source.at[pair, s], target.at[n, s]))
            if s == 0:
                loads[n][s].append(mover.start(rel_hbm.at[pair], rel.at[n]))
            if n == 0:
                loads[n][s].append(mover.start(joined_hbm.at[s], joined.at[s]))
    loads[0][1].append(mover.start(pos_hbm.at[pl.ds(0, KEYS)], pos))
    rest = []
    if size:
        rest.append(mover.start(earlier[1], blocks))
        base = 0
        for source, tops in zip(earlier[2:5], earlier[5:8]):
            count = source.shape[0]
            rest.append(mover.start(source, wide.at[pl.ds(base, count)]))
            rest.append(mover.start(tops, sums.at[pl.ds(base, count)]))
            base += count
    else:
        base = 0
    flip = reversal(HALF)
    first_head = lax.broadcasted_iota(jnp.int32, (HALF, 128), 1) < 64
    zero = jnp.zeros((HALF, 128), LOW)
    lane = lax.broadcasted_iota(jnp.int32, (SEG, 128), 1)
    into = lax.broadcasted_iota(jnp.int32, (128, 128), 0)
    out = lax.broadcasted_iota(jnp.int32, (128, 128), 1)
    head_sum = jnp.where(((out & 62) == 62) & ((into >> 6) == (out >> 6)), 1.0, 0.0).astype(LOW)
    for n in range(len(pairs)):
        grad_atts, u_ts, ga_ts = [], [], []
        for s in range(2):
            mover.wait(*loads[n][s])
            wide_grad = ga[n, s]
            inverse = inv[n, s]
            inner = wide_grad * att[n, s]
            inner_high = inner.astype(LOW)
            inner_low = (inner - inner_high.astype(F32)).astype(LOW)
            row_sums = (mm(inner_high, head_sum) + mm(inner_low, head_sum)) * inverse
            sums_high = row_sums.astype(LOW).astype(F32)
            grad_atts.append(
                jnp.where(
                    (lane & 63) == 62,
                    -sums_high,
                    jnp.where((lane & 63) == 63, sums_high - row_sums, wide_grad * inverse),
                ).astype(LOW)
            )
            u_ts.append(uv[n, s, :, :128].T)
            ga_ts.append(grad_atts[s].T)
        v_ts = [
            jnp.concatenate(
                [
                    mm(flip, uv[n, s, HALF * b : HALF * b + HALF, 128:]).astype(LOW).T
                    for s in range(2)
                ],
                axis=1,
            )
            for b in range(2)
        ]

        def differentiate(s, b):
            count = KEYS if b else KEYS - HALF
            part = grad_atts[s][HALF * b : HALF * b + HALF]
            both = jnp.concatenate(
                [jnp.where(first_head, part, zero), jnp.where(first_head, zero, part)], axis=0
            )
            return mm_nt(both, kv[n, s, :count, 128:])

        def spread_out(s, b, grad_probs):
            count = KEYS if b else KEYS - HALF
            rows = slice(HALF * b, HALF * b + HALF)
            for h in range(2):
                attn = probs[n, s, h, rows, :count].astype(F32)
                grad_scores = (attn * grad_probs[HALF * h : HALF * h + HALF]).astype(LOW)
                scores[s, h, rows, :count] = grad_scores
                if b == 0:
                    scores[s, h, rows, count:] = jnp.zeros((HALF, HALF), LOW)
                turned = pltpu.roll(mm(flip, grad_scores), 0, 1, stride=1, stride_axis=0)
                spread[b, h, HALF * s : HALF * s + HALF, :count] = turned.astype(LOW)

        def collect(s, b):
            count = KEYS if b else KEYS - HALF
            rows = slice(HALF * b, HALF * b + HALF)
            start_row = HALF - HALF * b

            def both(values):
                product = jnp.where(first_head, values[:HALF], values[HALF:])
                return product * FACTOR

            grad_u = both(
                mm(
                    jnp.concatenate([scores[s, h, rows, :count] for h in range(2)], axis=0),
                    kv[n, s, :count, :128],
                )
            )
            part = slice(HALF * s, HALF * s + HALF)
            grad_v = both(
                mm(
                    jnp.concatenate([spread[b, h, part, :count] for h in range(2)], axis=0),
                    rel[n, start_row : start_row + count],
                )
            )
            high = grad_v.astype(LOW)
            low = (grad_v - high.astype(F32)).astype(LOW)
            grad_q = (grad_u + (mm(flip, high) + mm(flip, low))).astype(LOW)
            o_token[n, s, rows, :128] = grad_q
            return total_rows(grad_u), total_rows(grad_v)

        parts = [(s, b) for s in range(2) for b in range(2)]
        grad_probs = differentiate(*parts[0])
        tops = []
        for k, part in enumerate(parts):
            following = differentiate(*parts[k + 1]) if k + 1 < len(parts) else None
            spread_out(*part, grad_probs)
            if k:
                tops.append(collect(*parts[k - 1]))
            grad_probs = following
        tops.append(collect(*parts[-1]))
        sum_u, sum_v = (sum(t[1:], t[0]) for t in zip(*tops))
        weight_kv, weight_q = None, None
        for s in range(2):
            for h in range(2):
                part = slice(64 * h, 64 * h + 64)
                dkv[s, part] = (mm(u_ts[s][part], scores[s, h]) * FACTOR).astype(LOW)
                dkv[s, 128 + 64 * h : 192 + 64 * h] = mm(ga_ts[s][part], probs[n, s, h]).astype(LOW)
            o_token[n, s, :, 128:] = dkv[s, :, MEM:].T
            part_kv = mm(dkv[s], joined[s])
            part_q = mm(o_token[n, s, :, :128].T, joined[s, MEM:])
            weight_kv = part_kv if weight_kv is None else weight_kv + part_kv
            weight_q = part_q if weight_q is None else weight_q + part_q
        for h in range(2):
            part = slice(64 * h, 64 * h + 64)
            first = mm(v_ts[0][part], spread[0, h, :, : KEYS - HALF])
            second = mm(v_ts[1][part], spread[1, h])
            grel[part, :HALF] = second[:, :HALF]
            grel[part, HALF:KEYS] = second[:, HALF:] + first
        spot = base + n
        wide[spot, :128] = weight_q.astype(LOW)
        wide[spot, 128:384] = weight_kv.astype(LOW)
        wide[spot, 384:] = mm((grel[...] * FACTOR).astype(LOW), pos[...]).astype(LOW)
        sums[spot] = jnp.concatenate([sum_u, sum_v, jnp.zeros((6, 128), F32)], axis=0)
    if size:
        mover.wait(*rest)
        pack_attention(earlier[0], blocks, wide, sums, outs[1], outs[2], whole)
    else:
        outs[1][...] = wide[...]
        outs[2][...] = sums[...]


def pack_attention(place, out_blocks, wides, sums, keep, send, whole):
    core = place[0]
    pick = expander(ROWS)
    back = compressor()
    rest = jnp.zeros((ROWS, 128), F32)
    for m in range(4):
        total = None
        for p in range(PAIRS):
            part = mm(pick[:, 128 * p : 128 * p + 128], wides[p, 128 * m : 128 * m + 128])
            total = part if total is None else total + part
        if m == 0:
            vectors = None
            for p in range(PAIRS):
                part = mm(sums[p].astype(LOW), back[128 * p : 128 * p + 128])
                vectors = part if vectors is None else vectors + part
            total = total + mm(pick_rows(8), vectors.astype(LOW))
        total = total.astype(LOW)
        for block in range(3):
            whole[3 * m + block] = total[:, 128 * block : 128 * block + 128]
        rest = rest + mm(total[:, 384:], placer(REST, m * REST))
    whole[12] = rest.astype(LOW)
    for block in range(3):
        whole[13 + block] = out_blocks[block]
    half = whole.shape[0] // 2
    for block in range(half):
        keep[ROWS * block : ROWS * block + ROWS] = whole[core * half + block]
        send[ROWS * block : ROWS * block + ROWS] = whole[(1 - core) * half + block]
    if keep.shape[0] > half * ROWS:
        extra = keep.shape[0] - half * ROWS
        keep[half * ROWS :] = jnp.zeros((extra, 128), LOW)
        send[half * ROWS :] = jnp.zeros((extra, 128), LOW)


def input_kernel(*refs, count):
    sources, (result_hbm, *targets), (o_input, sems) = (
        refs[:count], refs[count : 2 * count + 1], refs[2 * count + 1 :]
    )
    mover = Mover(sems)
    loads = [mover.start(a, b) for a, b in zip(sources, targets)]
    first_grad, wq, wkv, *tokens = targets
    mover.wait(*loads[:3])
    total = [first_grad[s] for s in range(2)]
    p = 0
    for token, load in zip(tokens, loads[3:]):
        mover.wait(load)
        for n in range(token.shape[0]):
            weights = jnp.concatenate([wq[p], wkv[p]], axis=1)
            for s in range(2):
                total[s] = total[s] + mm_nt(token[n, s], weights)
            p += 1
    for s in range(2):
        o_input[s] = total[s]
        mover.start(o_input.at[s], result_hbm.at[s])
    mover.finish()


def gathered(where, target, base, pieces, per_side):
    size = pieces[0].shape[0] // per_side
    for side, ref in enumerate(pieces):

        def body(r, carry, side=side, ref=ref):
            spot = jnp.bitwise_xor(r + side * per_side, where)
            row = pl.multiple_of(base + spot * size, 16)
            target[pl.ds(row, size)] = ref[pl.ds(pl.multiple_of(r * size, 16), size)]
            return carry

        lax.fori_loop(0, per_side, body, 0)


def unpack_attention_kernel(
    places, a0, a1, b0, b1, o_rest, o_query, o_key, o_value, o_pos, o_out,
    o_bias_u, o_bias_v, o_gain_1, o_shift_1, o_gain_2, o_shift_2, o_ffn_bias, whole, *, per_side
):
    core = places[2]
    total = 2 * a0.shape[0]
    gathered(places[0], whole, core * total, (a0, a1), per_side)
    gathered(places[1], whole, (1 - core) * total, (b0, b1), per_side)
    half = HALF_BLOCKS

    def fetch(block):
        start = (block // half) * total + ROWS * (block % half)
        return whole[start : start + ROWS]

    def vectors(targets, rows, start):
        for k, ref in enumerate(targets):
            ref[:, start : start + rows.shape[1]] = rows[k : k + 1]

    norms = (o_gain_1, o_shift_1, o_gain_2, o_shift_2, o_ffn_bias)
    unit = identity(128)
    rest = fetch(12)
    for m, ref in enumerate((o_query, o_key, o_value, o_pos)):
        for block in range(3):
            part = fetch(3 * m + block)
            ref[128 * block : 128 * block + 128, :] = mm_nt(unit, part)[:, :D]
            if m == 0:
                vectors((o_bias_u, o_bias_v), part[400:].astype(F32)[10:], 128 * block)
        tail = mm_nt(placer(REST, m * REST), rest)
        ref[384:, :] = tail[:, :D]
        if m == 0:
            vectors((o_bias_u, o_bias_v), rest[400:, :REST].astype(F32)[10:], 384)
    for block in range(3):
        part = fetch(13 + block).astype(F32)
        o_out[:, 128 * block : 128 * block + 128] = part[:D]
        vectors(norms, part[D:], 128 * block)
    tail = mm_nt(o_rest[...], placer(REST, 2 * REST))
    o_out[:, 384:] = tail[:D]
    vectors(norms, tail[D:], 384)


def unpack_ffn_kernel(places, a0, a1, o_in, o_bias, o_out_t, o_rest, whole, *, per_side):
    gathered(places[0], whole, 0, (a0, a1), per_side)
    units = o_in.shape[1]
    full = units // 128
    for block in range(full):
        lanes = slice(128 * block, 128 * block + 128)
        part = whole[ROWS * block : ROWS * block + ROWS].astype(F32)
        o_in[:, lanes] = part[:D]
        o_bias[:, lanes] = part[D : D + 1]
        start = ROWS * (full + block)
        o_out_t[:, lanes] = whole[start : start + ROWS].astype(F32)[:D]
    rest = whole[ROWS * 2 * full : ROWS * 2 * full + ROWS]
    o_rest[...] = rest
    left = units - 128 * full
    part = mm_nt(rest, placer(left, 0))
    o_in[:, 128 * full :] = part[:D]
    o_bias[:, 128 * full :] = part[D : D + 1]
    o_out_t[:, 128 * full :] = mm_nt(rest, placer(left, left))[:D]


def whole_spec():
    return pl.BlockSpec(memory_space=pltpu.VMEM)


def any_spec():
    return pl.BlockSpec(memory_space=pl.ANY)


def far_spec():
    return pl.BlockSpec(memory_space=pltpu.HBM)


def scalar_spec():
    return pl.BlockSpec(memory_space=pltpu.SMEM)


def params(limit=VMEM_BYTES):
    return pltpu.CompilerParams(vmem_limit_bytes=limit)


def cost(flops, moved):
    return pl.CostEstimate(flops=int(flops), bytes_accessed=int(moved), transcendentals=0)


def shape(dims, dtype=LOW):
    return jax.ShapeDtypeStruct(dims, dtype)


def prepare(w_query, w_key, w_value, w_pos, w_out, bias_u, bias_v, pos_table):
    operands = (w_query, w_key, w_value, w_pos, w_out, bias_u[None], bias_v[None], pos_table)
    results = (
        ((PAIRS, D, 128), LOW),
        ((PAIRS, D, 256), LOW),
        ((PAIRS, SPAN, 128), LOW),
        ((WIDE, D), LOW),
        ((PAIRS, 2, 8, 128), F32),
    )
    return pl.pallas_call(
        prep_kernel,
        out_shape=tuple(shape(*r) for r in results),
        in_specs=[far_spec()] * len(operands),
        out_specs=(far_spec(),) * len(results),
        scratch_shapes=[pltpu.VMEM(a.shape, a.dtype) for a in operands]
        + [pltpu.VMEM(*r) for r in results]
        + [pltpu.SemaphoreType.DMA((16,))],
        compiler_params=params(),
        cost_estimate=cost(3e9, 5e6),
        name="prepare_weights",
    )(*operands)


def layer(place, seg_len, mem_len, rows, reset, wq, wkv, rel, bias, wo, out_grads, own, other, vectors, size):
    units = own[0].shape[1]
    weights = (own[0], other[0], own[1], other[1], own[2], other[2])
    operands = (*rows, reset, wq, wkv, rel, bias, wo, *out_grads, *weights, *vectors)
    results = (
        ((PAIRS, 2, 2, SEG, KEYS), LOW),
        ((PAIRS, 2, KEYS, 256), LOW),
        ((PAIRS, 2, SEG, 256), LOW),
        ((2, SEG, WIDE), F32),
        ((2, SEG, WIDE), F32),
        ((2, KEYS, D), LOW),
        ((2, SEG, D), LOW),
        ((2, SEG, D), F32),
        ((2, SEG, WIDE), F32),
        ((size, 128), LOW),
        ((size, 128), LOW),
        ((3, ROWS, 128), LOW),
    )
    return pl.pallas_call(
        layer_kernel,
        out_shape=tuple(shape(*r) for r in results),
        in_specs=[scalar_spec()] * 3
        + [any_spec() if k in (2, 3, 11, 13, 15, 17) else far_spec() for k in range(len(operands))],
        out_specs=(far_spec(),) * len(results),
        scratch_shapes=[pltpu.VMEM(a.shape, a.dtype) for a in operands]
        + [pltpu.VMEM(*r) for r in results]
        + [
            pltpu.VMEM((4, 4 * D, 128), F32),
            pltpu.VMEM((2, SEG, KEYS), F32),
            pltpu.VMEM((2, SEG, D), LOW),
            pltpu.VMEM((2 * SEG, 512), LOW),
            pltpu.VMEM((2 * SEG, D), LOW),
            pltpu.VMEM((2 * SEG, 512), LOW),
            pltpu.VMEM((2, 2 * SEG, units), LOW),
            pltpu.VMEM((2, 2 * SEG, units), LOW),
            pltpu.VMEM((8, D), F32),
            pltpu.VMEM((2, SEG, WIDE), LOW),
            pltpu.VMEM((2, 2 * SEG, units), F32),
            pltpu.SemaphoreType.DMA((48,)),
            pltpu.SemaphoreType.DMA((3, PAIRS, 2)),
        ],
        compiler_params=params(),
        cost_estimate=cost(2e10, 3e7),
        name="layer",
    )(place, seg_len, mem_len, *operands)


def attend_back(pairs, operands, extra=(), size=0):
    count = len(pairs)
    total = PAIRS if size else count
    if not pairs[0]:
        operands = [pltpu.with_memory_space_constraint(a, pltpu.HBM) for a in operands]
    results = [shape((count, 2, SEG, 384))]
    if size:
        results += [shape((size, 128)), shape((size, 128))]
    else:
        results += [shape((count, 512, D)), shape((count, 8, 128), F32)]
    scratch = [
        pltpu.VMEM((count, 2, 2, SEG, KEYS), LOW),
        pltpu.VMEM((count, 2, KEYS, 256), LOW),
        pltpu.VMEM((count, 2, SEG, 256), LOW),
        pltpu.VMEM((count, SPAN, 128), LOW),
        pltpu.VMEM((count, 2, SEG, 128), F32),
        pltpu.VMEM((count, 2, SEG, 128), F32),
        pltpu.VMEM((count, 2, SEG, 128), F32),
        pltpu.VMEM((2, KEYS, D), LOW),
        pltpu.VMEM((KEYS, D), LOW),
        pltpu.VMEM((2, 2, SEG, KEYS), LOW),
        pltpu.VMEM((2, 2, SEG, KEYS), LOW),
        pltpu.VMEM((128, KEYS), F32),
        pltpu.VMEM((2, 256, KEYS), LOW),
        pltpu.VMEM((total, 512, D), LOW),
        pltpu.VMEM((total, 8, 128), F32),
    ]
    if size:
        scratch += [pltpu.VMEM(extra[1].shape, LOW), pltpu.VMEM((2 * HALF_BLOCKS, ROWS, 128), LOW)]
    return pl.pallas_call(
        functools.partial(back_kernel, pairs=pairs, size=size),
        out_shape=tuple(results),
        in_specs=[any_spec() if pairs[0] else far_spec()] * 9 + ([scalar_spec()] + [far_spec()] * 7 if size else []),
        out_specs=(whole_spec(),) * 3,
        scratch_shapes=scratch + [pltpu.SemaphoreType.DMA((40,))],
        compiler_params=params(LESS_BYTES),
        cost_estimate=cost(1.5e10 * count, 8e6),
        name=f"attend_back_{pairs[0]}",
    )(*operands, *extra)


def input_gradient(first_grad, tokens, wq, wkv):
    operands = [
        pltpu.with_memory_space_constraint(a, pltpu.HBM) for a in (first_grad, wq, wkv, *tokens)
    ]
    return pl.pallas_call(
        functools.partial(input_kernel, count=len(operands)),
        out_shape=shape((2, SEG, D), F32),
        in_specs=[far_spec()] * len(operands),
        out_specs=far_spec(),
        scratch_shapes=[pltpu.VMEM(a.shape, a.dtype) for a in operands]
        + [pltpu.VMEM((2, SEG, D), F32), pltpu.SemaphoreType.DMA((len(operands) + 2,))],
        compiler_params=params(LESS_BYTES),
        cost_estimate=cost(1.6e9, 6e6),
        name="input_gradient",
    )(*operands)


def unpack_attention(places, pieces, rest, dp_size):
    total = sum(p.shape[0] for p in pieces)
    return pl.pallas_call(
        functools.partial(unpack_attention_kernel, per_side=dp_size // 2),
        out_shape=(shape((D, D), F32),) * 5 + (shape((1, D), F32),) * 7,
        in_specs=[scalar_spec()] + [whole_spec()] * 5,
        out_specs=(whole_spec(),) * 12,
        scratch_shapes=[pltpu.VMEM((total, 128), LOW)],
        compiler_params=params(LESS_BYTES),
        cost_estimate=cost(5e8, 6e6),
        name="unpack_attention",
    )(places, *pieces, rest)


def unpack_ffn(places, pieces, units, dp_size):
    total = sum(p.shape[0] for p in pieces)
    return pl.pallas_call(
        functools.partial(unpack_ffn_kernel, per_side=dp_size // 2),
        out_shape=(
            shape((D, units), F32), shape((1, units), F32), shape((D, units), F32),
            shape((ROWS, 128)),
        ),
        in_specs=[scalar_spec()] + [whole_spec()] * 2,
        out_specs=(whole_spec(),) * 4,
        scratch_shapes=[pltpu.VMEM((total, 128), LOW)],
        compiler_params=params(LESS_BYTES),
        cost_estimate=cost(5e8, 6e6),
        name="unpack_ffn",
    )(places, *pieces)


def swap(values):
    return lax.ppermute(values, "tp", [(0, 1), (1, 0)])


def orders_of(dp_size):
    bits = list(range(dp_size.bit_length() - 1))
    turned = list(bits)
    for k in range(0, len(bits) - 1, 2):
        turned[k], turned[k + 1] = bits[k + 1], bits[k]
    return bits, turned


class Ring:
    def __init__(self, dp_size, index, core):
        self.size, self.orders = dp_size, orders_of(dp_size)
        self.steps = len(self.orders[0])
        self.bits = [
            jnp.where(core == 0, (index >> a) & 1, (index >> b) & 1)
            for a, b in zip(*self.orders)
        ]

    def place(self, index, order):
        spot = 0
        for k in self.orders[order]:
            spot = 2 * spot + ((index >> k) & 1)
        return spot

    def send(self, values, step):
        pairs = []
        for i in range(self.size):
            for c in range(2):
                pairs.append((2 * i + c, 2 * (i ^ (1 << self.orders[c][step])) + c))
        return lax.ppermute(values, ("dp", "tp"), pairs)

    def sides(self, keep, came, step):
        rows = keep.shape[0] // 2
        bit = self.bits[step]

        def side(which):
            start = which * rows
            return lax.dynamic_slice_in_dim(keep, start, rows, 0) + lax.dynamic_slice_in_dim(
                came, start, rows, 0
            )

        return side(1 - bit), side(bit)


def after(value, *others):
    return lax.optimization_barrier((value,) + others)


def rounded_rows(rows, unit):
    return -(-rows // unit) * unit


def make_shards(dp_size):
    table = position_table()

    def shards(
        hidden, memory, segment_length, memory_length, doc_reset, w_query, w_key, w_value, w_pos,
        bias_u, bias_v, w_out, first_gain, first_shift, ffn_in, ffn_in_bias, ffn_out, ffn_out_bias,
        second_gain, second_shift, out_grad,
    ):
        core = lax.axis_index("tp")
        index = lax.axis_index("dp")
        place = core[None].astype(jnp.int32)
        units = ffn_in.shape[1]
        pos_table = jnp.asarray(table)

        def by_feature(values):
            return values.transpose(2, 0, 1).reshape(-1, values.shape[1])

        hidden_t, memory_t, out_grad_t = (by_feature(a) for a in (hidden, memory, out_grad))
        hidden_in, memory_in, out_grad_in = swap(hidden_t), swap(memory_t), swap(out_grad_t)
        own_ffn = (ffn_in, ffn_in_bias[None], ffn_out.T)
        other_ffn = tuple(swap(a) for a in own_ffn)

        wq, wkv, rel, wo, bias = prepare(
            w_query, w_key, w_value, w_pos, w_out, bias_u, bias_v, pos_table
        )
        full = units // 128
        unit = 16 * dp_size
        (
            probs, kv, uv, att, inv, joined, act, first_grad, ga, ffn_own, ffn_other, out_blocks
        ) = layer(
            place, segment_length, memory_length, (hidden_t, memory_t, hidden_in, memory_in),
            doc_reset, wq, wkv, rel, bias, wo, (out_grad_t, out_grad_in), own_ffn, other_ffn,
            tuple(v[None] for v in (first_gain, first_shift, ffn_out_bias, second_gain, second_shift)),
            rounded_rows(ROWS * (2 * full + 1), unit),
        )
        ring = Ring(dp_size, index, core)
        straight, turned = ring.place(index, 0), ring.place(index, 1)
        places = jnp.stack(
            [
                jnp.where(core == 0, straight, turned),
                jnp.where(core == 0, turned, straight),
                core,
            ]
        ).astype(jnp.int32)

        def give_back(values, dtype):
            rows = values.shape[1] // 2
            mine = lax.dynamic_slice_in_dim(values, core * rows, rows, 1)
            theirs = lax.dynamic_slice_in_dim(values, (1 - core) * rows, rows, 1)
            came = swap(theirs.astype(LOW)).astype(dtype)
            mine = mine.astype(dtype)
            whole = jnp.where(
                core == 0,
                jnp.concatenate([mine, came], axis=0),
                jnp.concatenate([came, mine], axis=0),
            )
            return with_layout_constraint(whole, Layout(major_to_minor=(2, 0, 1)))

        def kept_memory(hidden):
            rows = hidden.shape[1]
            positions = core * rows + jnp.arange(rows)
            later = (jnp.arange(SEG)[:, None] > positions[None, :]).astype(LOW)
            resets = jnp.dot(doc_reset.astype(LOW), later, preferred_element_type=F32)
            keep = (resets == 0.0) & (positions[None, :] < segment_length[:, None])
            by_feature = hidden.transpose(2, 0, 1)
            return jnp.where(keep[None], by_feature, jnp.zeros_like(by_feature))

        steps = ring.steps
        backs = [(0,), (1, 2), (3,), (4,)]
        operands = [probs, kv, uv, rel, ga, att, inv, joined, pos_table]
        tokens, wides, biases = [], [], []

        def back_slot(waited):
            pairs = backs.pop(0)
            last = not backs
            result = attend_back(
                pairs,
                operands,
                (place, out_blocks, *wides, *biases) if last else (),
                rounded_rows(ROWS * HALF_BLOCKS, unit) if last else 0,
            )
            waited, *result = after(waited, *result)
            tokens.append(result[0])
            if last:
                return waited, result[1:]
            wides.append(result[1])
            biases.append(result[2])
            return waited, None

        keep, came = ffn_own, swap(ffn_other)
        came, _ = back_slot(came)
        packed = None
        for step in range(steps):
            sent, kept = ring.sides(keep, came, step)
            if backs:
                sent, kept, operands[4] = after(sent, kept, operands[4])
            elif packed:
                sent, kept, packed[0] = after(sent, kept, packed[0])
            keep, came = kept, ring.send(sent, step)
            if backs:
                came, packed = back_slot(came)
        att_keep, att_send = packed
        att_came = swap(att_send)
        places, att_came = after(places, att_came)
        gathers = list(range(steps - 1, -1, -1))
        values = spread = None
        for step in range(steps):
            sent, kept = ring.sides(att_keep, att_came, step)
            att_keep, att_came = kept, ring.send(sent, step)
            if step == 0:
                keep, _ = after(keep, sent)
                values = keep + came
                spread = ring.send(values, gathers.pop(0))
            elif step > 1 and len(gathers) > 1:
                values, spread, _ = after(values, spread, sent)
                values = jnp.concatenate([values, spread], axis=0)
                spread = ring.send(values, gathers.pop(0))
            if step == 0:
                first_grad, att_keep = after(first_grad, att_keep)
                input_own = input_gradient(first_grad, tokens, wq, wkv)
                att_came, input_own = after(att_came, input_own)
            elif step == 3:
                act, late_hidden, att_keep = after(act, hidden, att_keep)
                activations, new_memory = give_back(act, LOW), kept_memory(late_hidden)
                att_came, activations, new_memory = after(att_came, activations, new_memory)
        summed = att_keep + att_came
        for k in gathers:
            values, spread, _ = after(values, spread, summed)
            values = jnp.concatenate([values, spread], axis=0)
            spread = ring.send(values, k)
        ffn_pieces = (values, spread)
        values = summed
        for step in range(steps - 1, 0, -1):
            came = ring.send(values, step)
            if step == steps - 1:
                input_own, values = after(input_own, values)
                input_grad = give_back(input_own, F32)
                came, input_grad = after(came, input_grad)
            values = jnp.concatenate([values, came], axis=0)
        came = ring.send(values, 0)
        near = swap(values)
        filled = list(unpack_ffn(places, ffn_pieces, units, dp_size))
        filled[1] = filled[1].reshape(-1)
        came, near, *filled = after(came, near, *filled)
        grad_in, grad_in_bias, grad_ffn_out_t, rest = filled
        g_query, g_key, g_value, g_pos, g_out, *vectors = unpack_attention(
            places, (values, came, near, swap(came)), rest, dp_size
        )
        g_bias_u, g_bias_v, g_gain_1, g_shift_1, g_gain_2, g_shift_2, g_ffn_bias = (
            v[0] for v in vectors
        )

        def by_token(values):
            return values.transpose(1, 2, 0)

        return (
            by_token(new_memory), activations, input_grad,
            g_query, g_key, g_value, g_pos, g_bias_u, g_bias_v, g_out, g_gain_1, g_shift_1,
            grad_in, grad_in_bias, grad_ffn_out_t.T, g_ffn_bias, g_gain_2, g_shift_2,
        )

    return shards


def solution(mesh):
    rows, copied = P("dp", "tp", None), P()
    shards = make_shards(mesh.shape["dp"])
    return jax.shard_map(
        shards,
        mesh=mesh,
        in_specs=(
            rows, rows, P("dp"), P("dp"), P("dp", None),
            copied, copied, copied, copied, copied, copied, copied, copied, copied,
            P(None, "tp"), P("tp"), P("tp", None),
            copied, copied, copied, rows,
        ),
        out_specs=(
            rows, rows, rows, copied, copied, copied, copied, copied, copied, copied, copied, copied,
            P(None, "tp"), P("tp"), P("tp", None), copied, copied, copied,
        ),
        check_vma=False,
    )
```

```python
import functools
import math

import jax
import jax.numpy as jnp
import ml_dtypes
import numpy as np
from jax import lax
from jax.experimental import pallas as pl
from jax.experimental.layout import Layout, with_layout_constraint
from jax.experimental.pallas import tpu as pltpu
from jax.sharding import PartitionSpec as P

D = 410
HEADS = 10
DHEAD = 41
SEG = 256
MEM = 256
KEYS = MEM + SEG
HALF = 128
PAIRS = HEADS // 2
WIDE = PAIRS * 128
ROWS = 416
SPAN = 768
REST = 26
HALF_BLOCKS = 8
RECEIVED = (2, 3, 11, 13, 17)
EPSILON = 1e-05
NEG_LARGE = -1e30
FACTOR = 1.0 / math.sqrt(DHEAD)
LOG2E = 1.0 / math.log(2.0)
LOW = jnp.bfloat16
VMEM_BYTES = 60 * 1024 * 1024
LAYER_BYTES = 54 * 1024 * 1024
LESS_BYTES = 20 * 1024 * 1024
F32 = jnp.float32


def position_table():
    distance = (KEYS - 1 - np.arange(SPAN)).astype(np.float32)
    inverse = np.float32(1.0) / np.float32(10000.0) ** (
        np.arange(0, D, 2).astype(np.float32) / np.float32(D)
    )
    angles = distance[:, None] * inverse[None, :].astype(np.float32)
    table = np.concatenate([np.sin(angles), np.cos(angles)], axis=1)
    return table.astype(ml_dtypes.bfloat16)


def mm(left, right):
    return lax.dot_general(left, right, (((1,), (0,)), ((), ())), preferred_element_type=F32)


def mm_nt(left, right):
    return lax.dot_general(left, right, (((1,), (1,)), ((), ())), preferred_element_type=F32)


def expander(rows):
    row = lax.broadcasted_iota(jnp.int32, (rows, WIDE), 0)
    lane = lax.broadcasted_iota(jnp.int32, (rows, WIDE), 1)
    inside = lane & 63
    hit = (inside < DHEAD) & (row == (lane >> 6) * DHEAD + inside)
    return jnp.where(hit, 1.0, 0.0).astype(LOW)


def compressor():
    row = lax.broadcasted_iota(jnp.int32, (WIDE, D), 0)
    lane = lax.broadcasted_iota(jnp.int32, (WIDE, D), 1)
    inside = row & 63
    hit = (inside < DHEAD) & (lane == (row >> 6) * DHEAD + inside)
    return jnp.where(hit, 1.0, 0.0).astype(LOW)


def identity(size):
    row = lax.broadcasted_iota(jnp.int32, (size, size), 0)
    lane = lax.broadcasted_iota(jnp.int32, (size, size), 1)
    return jnp.where(row == lane, 1.0, 0.0).astype(LOW)


def reversal(size):
    row = lax.broadcasted_iota(jnp.int32, (size, size), 0)
    lane = lax.broadcasted_iota(jnp.int32, (size, size), 1)
    return jnp.where(row + lane == size - 1, 1.0, 0.0).astype(LOW)


class Mover:
    def __init__(self, sems):
        self.sems, self.used, self.open = sems, 0, []

    def start(self, source, target):
        copy = pltpu.make_async_copy(source, target, self.sems.at[self.used])
        self.used += 1
        copy.start()
        self.open.append(copy)
        return copy

    def finish(self):
        for copy in self.open:
            copy.wait()
        self.open = []

    def wait(self, *copies):
        for copy in copies:
            copy.wait()
        self.open = [c for c in self.open if all(c is not d for d in copies)]


def prep_kernel(
    wq_in, wk_in, wv_in, wp_in, wo_in, bias_u_in, bias_v_in, pos_in, q_out, kv_out, rel_out, wo_out,
    bias_out, wq, wk, wv, wp, wo, bias_u, bias_v, pos, o_q, o_kv, o_rel, o_wo, o_bias, sems
):
    mover = Mover(sems)
    loads = [
        mover.start(a, b)
        for a, b in zip(
            (wp_in, pos_in, wk_in, wv_in, wq_in, wo_in, bias_u_in, bias_v_in),
            (wp, pos, wk, wv, wq, wo, bias_u, bias_v),
        )
    ]
    expand = expander(D)
    mover.wait(*loads[:2])
    rel = mm(pos[...], wp[...]).astype(LOW)
    rel = mm(rel, expand).astype(LOW)
    for p in range(PAIRS):
        o_rel[p] = rel[:, 128 * p : 128 * p + 128]
    mover.start(o_rel, rel_out)
    mover.wait(*loads[2:4])
    k_wide = mm(wk[...], expand).astype(LOW)
    v_wide = mm(wv[...], expand).astype(LOW)
    for p in range(PAIRS):
        o_kv[p, :, :128] = k_wide[:, 128 * p : 128 * p + 128]
        o_kv[p, :, 128:] = v_wide[:, 128 * p : 128 * p + 128]
    mover.start(o_kv, kv_out)
    mover.wait(*loads[4:])
    q_wide = mm(wq[...], expand).astype(LOW)
    for p in range(PAIRS):
        o_q[p] = q_wide[:, 128 * p : 128 * p + 128]
    mover.start(o_q, q_out)
    o_wo[...] = mm(compressor(), wo[...]).astype(LOW)
    mover.start(o_wo, wo_out)
    for bias_index, bias in enumerate((bias_u, bias_v)):
        value = jnp.broadcast_to(bias[...], (8, D))
        high = value.astype(LOW)
        rest = value - high.astype(F32)
        middle = rest.astype(LOW)
        last = (rest - middle.astype(F32)).astype(LOW)
        wide = mm(high, expand) + mm(middle, expand) + mm(last, expand)
        for p in range(PAIRS):
            o_bias[p, bias_index] = wide[:, 128 * p : 128 * p + 128]
    mover.start(o_bias, bias_out)
    mover.finish()


def spread_streams(source, raw, core, unit, store):
    raw[...] = source[...].astype(F32)
    for s in range(2):
        columns = raw[pl.ds(2 * core + s, D, stride=4), :].astype(LOW)
        store(s, mm_nt(unit, columns).astype(LOW))


def layer_kernel(
    place, seg_len, mem_len, hidden_hbm, memory_hbm, hidden_in_hbm, memory_in_hbm, reset_hbm,
    wq_hbm, wkv_hbm, rel_hbm, bias_hbm, wo_hbm, out_grad_hbm, out_grad_in_hbm,
    win_a_hbm, win_b_hbm, bin_a_hbm, bin_b_hbm, wout_a_hbm, wout_b_hbm,
    gain_1_hbm, shift_1_hbm, bias_out_hbm, gain_2_hbm, shift_2_hbm,
    probs_out, kv_out, uv_out, att_out, inv_out, joined_out,
    act_out, first_out, ga_out, own_out, other_out, blocks_out,
    hidden, memory, hidden_in, memory_in, reset, wq, wkv, rel, bias, wo, out_grad, out_grad_in,
    win_a, win_b, bin_a, bin_b, wout_a, wout_b, gain_1, shift_1, bias_out, gain_2, shift_2,
    o_probs, o_kv, o_uv, o_att, o_inv, o_joined, o_act, o_first, o_ga, o_own, o_other, o_out,
    raw, mask, og, low_in, gb_all, gs_all, active, inner, vecs, att, slopes, sems, step_sems
):
    mover = Mover(sems)
    loads = [
        mover.start(a, b)
        for a, b in zip(
            (
                memory_hbm, memory_in_hbm, hidden_hbm, hidden_in_hbm, reset_hbm,
                wkv_hbm, wq_hbm, bias_hbm, rel_hbm,
                gain_1_hbm, shift_1_hbm, bias_out_hbm, gain_2_hbm, shift_2_hbm, bin_a_hbm,
                bin_b_hbm, wo_hbm, out_grad_hbm, out_grad_in_hbm,
                win_a_hbm, wout_a_hbm, win_b_hbm, wout_b_hbm,
            ),
            (
                memory, memory_in, hidden, hidden_in, reset, wkv, wq, bias, rel,
                gain_1, shift_1, bias_out, gain_2, shift_2, bin_a,
                bin_b, wo, out_grad, out_grad_in, win_a, wout_a, win_b, wout_b,
            ),
        )
    ]
    core = place[0]
    mine = pl.multiple_of(HALF * core, HALF)
    other = pl.multiple_of(HALF * (1 - core), HALF)
    unit = identity(HALF)
    row = lax.broadcasted_iota(jnp.int32, (SEG, SEG), 0)
    lane = lax.broadcasted_iota(jnp.int32, (SEG, SEG), 1)
    lower = jnp.where(row >= lane, 1.0, 0.0).astype(LOW)
    for index, (source, base) in enumerate(
        ((memory, mine), (memory_in, other), (hidden, MEM + mine), (hidden_in, MEM + other))
    ):

        def store(s, values, base=base):
            o_joined[s, pl.ds(pl.multiple_of(base, HALF), HALF)] = values

        mover.wait(loads[index])
        spread_streams(source, raw.at[index], core, unit, store)
    mover.wait(*loads[4:9])
    mover.start(o_joined, joined_out)
    for s in range(2):
        own = 2 * core + s
        starts = jnp.broadcast_to(reset[pl.ds(own, 1), :].astype(F32), (8, SEG)).astype(LOW)
        doc_column = mm_nt(lower, starts)[:, :1]
        doc_row = mm_nt(starts, lower)[:1, :]
        memory_ok = (lane >= MEM - mem_len[own]) & (doc_column == 0.0)
        segment_ok = ((row > lane) & (doc_row == doc_column) & (lane < seg_len[own])) | (row == lane)
        mask[s, :, :MEM] = jnp.where(memory_ok, 0.0, NEG_LARGE)
        mask[s, :, MEM:] = jnp.where(segment_ok, 0.0, NEG_LARGE)
    first_head = lax.broadcasted_iota(jnp.int32, (HALF, 128), 1) < 64
    zero = jnp.zeros((HALF, 128), LOW)
    ones_lane = (lax.broadcasted_iota(jnp.int32, (KEYS, 256), 1) & 190) == 190

    for p in range(PAIRS):
        for s in range(2):
            pair_rows = jnp.where(ones_lane, 1.0, mm(o_joined[s], wkv[p])).astype(LOW)
            o_kv[p, s] = pair_rows
            queries = mm(o_joined[s, MEM:], wq[p])
            o_uv[p, s, :, :128] = (queries + bias[p, 0, :1]).astype(LOW)
            o_uv[p, s, :, 128:] = (queries + bias[p, 1, :1]).astype(LOW)

    def stacked(values):
        return jnp.concatenate(
            [jnp.where(first_head, values, zero), jnp.where(first_head, zero, values)], axis=0
        )

    def score(p, s, b):
        count = KEYS if b else KEYS - HALF
        rows = slice(HALF * b, HALF * b + HALF)
        start_row = HALF - HALF * b
        content = mm_nt(stacked(o_uv[p, s, rows, :128]), o_kv[p, s, :count, :128])
        relative = mm_nt(stacked(o_uv[p, s, rows, 128:]), rel[p, start_row : start_row + count])
        spots = mask[s, rows, :count]
        scores = []
        for h in range(2):
            part = slice(HALF * h, HALF * h + HALF)
            turned = pltpu.roll(relative[part], count - HALF + 1, 1, stride=1, stride_axis=0)
            scores.append((content[part] + turned) * (FACTOR * LOG2E) + spots)
        return scores

    def soften(p, s, b, scores):
        count = KEYS if b else KEYS - HALF
        rows = slice(HALF * b, HALF * b + HALF)
        exp_terms = []
        for h in range(2):
            top = jnp.max(scores[h], axis=1, keepdims=True)
            exp_terms.append(jnp.exp2(scores[h] - top).astype(LOW))
            o_probs[p, s, h, rows, :count] = exp_terms[h]
            if b == 0:
                o_probs[p, s, h, rows, count:] = jnp.zeros((HALF, HALF), LOW)
        return jnp.concatenate(exp_terms, axis=0)

    def mix(p, s, b, exp_terms):
        lanes = pl.ds(pl.multiple_of(128 * p, 128), 128)
        count = KEYS if b else KEYS - HALF
        rows = slice(HALF * b, HALF * b + HALF)
        mixed = mm(exp_terms, o_kv[p, s, :count, 128:])
        inverse = jnp.where(first_head, 1.0 / mixed[:HALF, 63:64], 1.0 / mixed[HALF:, 127:])
        o_inv[s, rows, lanes] = inverse
        o_att[s, rows, lanes] = jnp.where(first_head, mixed[:HALF], mixed[HALF:]) * inverse

    def step(p, carry):
        blocks = [(s, b) for s in range(2) for b in range(2)]
        scores, mixing = score(p, *blocks[0]), None
        for k, block in enumerate(blocks):
            following = score(p, *blocks[k + 1]) if k + 1 < len(blocks) else None
            exp_terms = soften(p, *block, scores)
            if mixing is not None:
                mix(p, *mixing)
            mixing, scores = (*block, exp_terms), following
        mix(p, *mixing)
        for s in range(2):
            for copy in step_copies(p, s):
                copy.start()
        return carry

    def step_copies(p, s):
        return [
            pltpu.make_async_copy(a.at[p, s], b.at[p, s], step_sems.at[k, p, s])
            for k, (a, b) in enumerate(((o_probs, probs_out), (o_kv, kv_out), (o_uv, uv_out)))
        ]

    lax.fori_loop(0, PAIRS, step, 0)
    mover.start(o_att, att_out)
    mover.start(o_inv, inv_out)
    hidden_units = win_a.shape[1]
    chunks = [(a, min(a + 256, hidden_units)) for a in range(0, hidden_units, 256)]
    halves = ((win_a, bin_a, wout_a), (win_b, bin_b, wout_b))
    low_in[:, 384:] = jnp.where(
        lax.broadcasted_iota(jnp.int32, (2 * SEG, 128), 1) == D - 384, 1.0, 0.0
    ).astype(LOW)
    gs_all[:, 384:] = jnp.zeros((2 * SEG, 128), LOW)
    vecs[...] = jnp.zeros_like(vecs)
    att[...] = o_att[...].astype(LOW)
    mover.wait(*loads[9:])
    for index, (source, base) in enumerate(((out_grad, mine), (out_grad_in, other))):

        def store_grad(s, values, base=base):
            og[s, pl.ds(base, HALF)] = values

        spread_streams(source, raw.at[index], core, unit, store_grad)
    tokens = 2 * SEG
    hid = o_joined[:, MEM:].reshape(tokens, D).astype(F32)
    hat_1, scale_1 = norm_forward(hid + mm(att[...].reshape(tokens, WIDE), wo[...]))
    first = hat_1 * gain_1[...] + shift_1[...]
    first_low = first.astype(LOW)
    low_in[:, :D] = first_low
    ffn_sum = first + bias_out[...]
    for which, (win, b_in, wout) in enumerate(halves):
        for a, z in chunks:
            pre = mm(first_low, win[:, a:z]) + b_in[:, a:z].astype(F32)
            act, slope = gelu_both(pre)
            act = act.astype(LOW)
            slopes[which, :, a:z] = slope
            active[which, :, a:z] = act
            ffn_sum = ffn_sum + mm_nt(act, wout[:, a:z])
    hat_2, scale_2 = norm_forward(ffn_sum)
    o_act[...] = (hat_2 * gain_2[...] + shift_2[...]).astype(LOW).reshape(2, SEG, D)
    cot = og[...].reshape(tokens, D).astype(F32)
    vecs[2:3] = total_rows(cot * hat_2)
    vecs[3:4] = total_rows(cot)
    grad_second = norm_backward(cot * gain_2[...], hat_2, scale_2)
    vecs[4:5] = total_rows(grad_second)
    gs_low = grad_second.astype(LOW)
    gs_all[:, :D] = gs_low
    grad_first = grad_second
    for which, (win, b_in, wout) in enumerate(halves):
        for a, z in chunks:
            grad_inner = (mm(gs_low, wout[:, a:z]) * slopes[which, :, a:z]).astype(LOW)
            inner[which, :, a:z] = grad_inner
            grad_first = grad_first + mm_nt(grad_inner, win[:, a:z])
    vecs[0:1] = total_rows(grad_first * hat_1)
    vecs[1:2] = total_rows(grad_first)
    grad_pre = norm_backward(grad_first * gain_1[...], hat_1, scale_1)
    o_first[...] = grad_pre.reshape(2, SEG, D)
    grad_branch = grad_pre.astype(LOW)
    gb_all[...] = grad_branch
    o_ga[...] = mm_nt(grad_branch, wo[...]).reshape(2, SEG, WIDE)
    mover.start(o_act, act_out)
    mover.start(o_first, first_out)
    mover.start(o_ga, ga_out)
    grad_out = None
    for s in range(2):
        part = mm(att[s].T, gb_all[SEG * s : SEG * s + SEG])
        grad_out = part if grad_out is None else grad_out + part
    grad_out = mm(expander(ROWS), grad_out.astype(LOW))
    grad_out = (grad_out + mm(pick_rows(8), vecs[...].astype(LOW))).astype(LOW)
    for block in range(3):
        o_out[block] = grad_out[:, 128 * block : 128 * block + 128]
    mover.start(o_out, blocks_out)
    out_rest = mm(grad_out[:, 384:], placer(REST, 2 * REST))
    in_t = low_in[...].T[:ROWS]
    gs_t = gs_all[...].T[:ROWS]
    full = hidden_units // 128
    for which, pack, target in ((1, o_other, other_out), (0, o_own, own_out)):
        rest = out_rest
        for m, (left, right) in enumerate(((in_t, inner), (gs_t, active))):
            for a, z in chunks:
                grads = mm(left, right[which, :, a:z]).astype(LOW)
                for block in range(a // 128, min(-(-z // 128), full)):
                    part = grads[:, 128 * block - a : 128 * block - a + 128]
                    put(pack, ROWS * (full * m + block), part)
                if z > 128 * full:
                    rest = rest + mm(grads[:, 128 * full - a :], placer(REST, m * REST))
            span = pl.ds(ROWS * full * m, ROWS * full)
            mover.start(pack.at[span], target.at[span])
        put(pack, ROWS * 2 * full, rest.astype(LOW))
        span = pl.ds(ROWS * 2 * full, pack.shape[0] - ROWS * 2 * full)
        mover.start(pack.at[span], target.at[span])
    for p in range(PAIRS):
        for s in range(2):
            for copy in step_copies(p, s):
                copy.wait()
    mover.finish()


def norm_forward(values):
    centred = values - jnp.mean(values, axis=1, keepdims=True)
    scale = lax.rsqrt(jnp.mean(centred * centred, axis=1, keepdims=True) + EPSILON)
    return centred * scale, scale


def norm_backward(grad, x_hat, scale):
    return scale * (
        grad
        - jnp.mean(grad, axis=1, keepdims=True)
        - x_hat * jnp.mean(grad * x_hat, axis=1, keepdims=True)
    )


GELU_A = math.sqrt(2.0 / math.pi)
GELU_B = 0.044715


def gelu_both(x):
    square = x * x
    bent = jnp.tanh(x * (GELU_A + (GELU_A * GELU_B) * square))
    half_up = 0.5 + 0.5 * bent
    slope = half_up + (0.5 * x) * (1.0 - bent * bent) * (GELU_A + (3.0 * GELU_A * GELU_B) * square)
    return x * half_up, slope


def total_rows(values):
    return jnp.sum(values, axis=0, keepdims=True)


def placer(count, offset):
    row = lax.broadcasted_iota(jnp.int32, (count, 128), 0)
    lane = lax.broadcasted_iota(jnp.int32, (count, 128), 1)
    return jnp.where(lane == row + offset, 1.0, 0.0).astype(LOW)


def put(ref, start, values):
    ref[start : start + values.shape[0]] = values


def pick_rows(count):
    row = lax.broadcasted_iota(jnp.int32, (ROWS, count), 0)
    lane = lax.broadcasted_iota(jnp.int32, (ROWS, count), 1)
    return jnp.where(row == D + lane, 1.0, 0.0).astype(LOW)


def back_kernel(*refs, pairs, calls, fetched):
    refs = list(refs)

    def take(count):
        part = refs[:count]
        del refs[:count]
        return part

    sources = take(9)
    earlier = take(2 + 2 * calls) if calls else []
    outs = take(3)
    o_token = outs[0]
    loads = [([], []) for _ in pairs]
    if fetched:
        probs_hbm, kv_hbm, uv_hbm, rel_hbm, ga_hbm, att_hbm, inv_hbm, joined_hbm, pos_hbm = sources
        probs, kv, uv, rel, ga, att, inv, joined, pos = take(9)
        mover = Mover(take(1)[0])
        for n, pair in enumerate(pairs):
            lanes = slice(128 * pair, 128 * pair + 128)
            for s in range(2):
                for source, target in ((ga_hbm, ga), (att_hbm, att), (inv_hbm, inv)):
                    loads[n][s].append(mover.start(source.at[s, :, lanes], target.at[n, s]))
                for source, target in ((uv_hbm, uv), (kv_hbm, kv), (probs_hbm, probs)):
                    loads[n][s].append(mover.start(source.at[pair, s], target.at[n, s]))
                if s == 0:
                    loads[n][s].append(mover.start(rel_hbm.at[pair], rel.at[n]))
                if n == 0:
                    loads[n][s].append(mover.start(joined_hbm.at[s], joined.at[s]))
        loads[0][1].append(mover.start(pos_hbm, pos))
    else:
        probs, kv, uv, rel, ga, att, inv, joined, pos = sources
    scores, spread, grel, dkv, wide, sums = take(6)
    base = 0
    if calls:
        (whole,) = take(1)
        for source, tops in zip(earlier[2 : 2 + calls], earlier[2 + calls :]):
            count = source.shape[0]
            wide[base : base + count] = source[...]
            sums[base : base + count] = tops[...]
            base += count
    flip = reversal(HALF)
    first_head = lax.broadcasted_iota(jnp.int32, (HALF, 128), 1) < 64
    zero = jnp.zeros((HALF, 128), LOW)
    lane = lax.broadcasted_iota(jnp.int32, (SEG, 128), 1)
    into = lax.broadcasted_iota(jnp.int32, (128, 128), 0)
    out = lax.broadcasted_iota(jnp.int32, (128, 128), 1)
    head_sum = jnp.where(((out & 62) == 62) & ((into >> 6) == (out >> 6)), 1.0, 0.0).astype(LOW)
    for n, pair in enumerate(pairs):
        here = n if fetched else pair
        lanes = slice(128 * pair, 128 * pair + 128)

        def columns(values, s, n=n, lanes=lanes):
            return values[n, s] if fetched else values[s, :, lanes]

        grad_atts, u_ts, ga_ts = [], [], []
        for s in range(2):
            if fetched:
                mover.wait(*loads[n][s])
            wide_grad = columns(ga, s)
            inverse = columns(inv, s)
            inner = wide_grad * columns(att, s)
            inner_high = inner.astype(LOW)
            inner_low = (inner - inner_high.astype(F32)).astype(LOW)
            row_sums = (mm(inner_high, head_sum) + mm(inner_low, head_sum)) * inverse
            sums_high = row_sums.astype(LOW).astype(F32)
            grad_atts.append(
                jnp.where(
                    (lane & 63) == 62,
                    -sums_high,
                    jnp.where((lane & 63) == 63, sums_high - row_sums, wide_grad * inverse),
                ).astype(LOW)
            )
            u_ts.append(uv[here, s, :, :128].T)
            ga_ts.append(grad_atts[s].T)
        v_ts = [
            jnp.concatenate(
                [
                    mm(flip, uv[here, s, HALF * b : HALF * b + HALF, 128:]).astype(LOW).T
                    for s in range(2)
                ],
                axis=1,
            )
            for b in range(2)
        ]

        def differentiate(s, b):
            count = KEYS if b else KEYS - HALF
            part = grad_atts[s][HALF * b : HALF * b + HALF]
            both = jnp.concatenate(
                [jnp.where(first_head, part, zero), jnp.where(first_head, zero, part)], axis=0
            )
            return mm_nt(both, kv[here, s, :count, 128:])

        def spread_out(s, b, grad_probs):
            count = KEYS if b else KEYS - HALF
            rows = slice(HALF * b, HALF * b + HALF)
            for h in range(2):
                attn = probs[here, s, h, rows, :count].astype(F32)
                grad_scores = (attn * grad_probs[HALF * h : HALF * h + HALF]).astype(LOW)
                scores[s, h, rows, :count] = grad_scores
                if b == 0:
                    scores[s, h, rows, count:] = jnp.zeros((HALF, HALF), LOW)
                turned = pltpu.roll(mm(flip, grad_scores), 0, 1, stride=1, stride_axis=0)
                spread[b, h, HALF * s : HALF * s + HALF, :count] = turned.astype(LOW)

        def collect(s, b):
            count = KEYS if b else KEYS - HALF
            rows = slice(HALF * b, HALF * b + HALF)
            start_row = HALF - HALF * b

            def both(values):
                product = jnp.where(first_head, values[:HALF], values[HALF:])
                return product * FACTOR

            grad_u = both(
                mm(
                    jnp.concatenate([scores[s, h, rows, :count] for h in range(2)], axis=0),
                    kv[here, s, :count, :128],
                )
            )
            part = slice(HALF * s, HALF * s + HALF)
            grad_v = both(
                mm(
                    jnp.concatenate([spread[b, h, part, :count] for h in range(2)], axis=0),
                    rel[here, start_row : start_row + count],
                )
            )
            high = grad_v.astype(LOW)
            low = (grad_v - high.astype(F32)).astype(LOW)
            grad_q = (grad_u + (mm(flip, high) + mm(flip, low))).astype(LOW)
            o_token[n, s, rows, :128] = grad_q
            return total_rows(grad_u), total_rows(grad_v)

        parts = [(s, b) for s in range(2) for b in range(2)]
        grad_probs = differentiate(*parts[0])
        tops = []
        for k, part in enumerate(parts):
            following = differentiate(*parts[k + 1]) if k + 1 < len(parts) else None
            spread_out(*part, grad_probs)
            if k:
                tops.append(collect(*parts[k - 1]))
            grad_probs = following
        tops.append(collect(*parts[-1]))
        sum_u, sum_v = (sum(t[1:], t[0]) for t in zip(*tops))
        weight_kv, weight_q = None, None
        for s in range(2):
            for h in range(2):
                part = slice(64 * h, 64 * h + 64)
                dkv[s, part] = (mm(u_ts[s][part], scores[s, h]) * FACTOR).astype(LOW)
                dkv[s, 128 + 64 * h : 192 + 64 * h] = mm(ga_ts[s][part], probs[here, s, h]).astype(LOW)
            o_token[n, s, :, 128:] = dkv[s, :, MEM:].T
            part_kv = mm(dkv[s], joined[s])
            part_q = mm(o_token[n, s, :, :128].T, joined[s, MEM:])
            weight_kv = part_kv if weight_kv is None else weight_kv + part_kv
            weight_q = part_q if weight_q is None else weight_q + part_q
        for h in range(2):
            part = slice(64 * h, 64 * h + 64)
            first = mm(v_ts[0][part], spread[0, h, :, : KEYS - HALF])
            second = mm(v_ts[1][part], spread[1, h])
            grel[part, :HALF] = second[:, :HALF]
            grel[part, HALF:KEYS] = second[:, HALF:] + first
        spot = base + n
        wide[spot, :128] = weight_q.astype(LOW)
        wide[spot, 128:384] = weight_kv.astype(LOW)
        wide[spot, 384:] = mm((grel[...] * FACTOR).astype(LOW), pos[:KEYS]).astype(LOW)
        sums[spot] = jnp.concatenate([sum_u, sum_v, jnp.zeros((6, 128), F32)], axis=0)
    if calls:
        pack_attention(earlier[0], earlier[1], wide, sums, outs[1], outs[2], whole)
    else:
        outs[1][...] = wide[...]
        outs[2][...] = sums[...]


def pack_attention(place, out_blocks, wides, sums, keep, send, whole):
    core = place[0]
    pick = expander(ROWS)
    back = compressor()
    rest = jnp.zeros((ROWS, 128), F32)
    for m in range(4):
        total = None
        for p in range(PAIRS):
            part = mm(pick[:, 128 * p : 128 * p + 128], wides[p, 128 * m : 128 * m + 128])
            total = part if total is None else total + part
        if m == 0:
            vectors = None
            for p in range(PAIRS):
                part = mm(sums[p].astype(LOW), back[128 * p : 128 * p + 128])
                vectors = part if vectors is None else vectors + part
            total = total + mm(pick_rows(8), vectors.astype(LOW))
        total = total.astype(LOW)
        for block in range(3):
            whole[3 * m + block] = total[:, 128 * block : 128 * block + 128]
        rest = rest + mm(total[:, 384:], placer(REST, m * REST))
    whole[12] = rest.astype(LOW)
    for block in range(3):
        whole[13 + block] = out_blocks[block]
    half = whole.shape[0] // 2
    for block in range(half):
        keep[ROWS * block : ROWS * block + ROWS] = whole[core * half + block]
        send[ROWS * block : ROWS * block + ROWS] = whole[(1 - core) * half + block]
    if keep.shape[0] > half * ROWS:
        extra = keep.shape[0] - half * ROWS
        keep[half * ROWS :] = jnp.zeros((extra, 128), LOW)
        send[half * ROWS :] = jnp.zeros((extra, 128), LOW)


def input_kernel(*refs, count):
    sources, (result_hbm, *targets), (o_input, sems) = (
        refs[:count], refs[count : 2 * count + 1], refs[2 * count + 1 :]
    )
    mover = Mover(sems)
    loads = [mover.start(a, b) for a, b in zip(sources, targets)]
    first_grad, wq, wkv, *tokens = targets
    mover.wait(*loads[:3])
    total = [first_grad[s] for s in range(2)]
    p = 0
    for token, load in zip(tokens, loads[3:]):
        mover.wait(load)
        for n in range(token.shape[0]):
            weights = jnp.concatenate([wq[p], wkv[p]], axis=1)
            for s in range(2):
                total[s] = total[s] + mm_nt(token[n, s], weights)
            p += 1
    for s in range(2):
        o_input[s] = total[s]
        mover.start(o_input.at[s], result_hbm.at[s])
    mover.finish()


def gathered(where, target, base, pieces, per_side):
    size = pieces[0].shape[0] // per_side
    for side, ref in enumerate(pieces):

        def body(r, carry, side=side, ref=ref):
            spot = jnp.bitwise_xor(r + side * per_side, where)
            row = pl.multiple_of(base + spot * size, 16)
            target[pl.ds(row, size)] = ref[pl.ds(pl.multiple_of(r * size, 16), size)]
            return carry

        lax.fori_loop(0, per_side, body, 0)


def unpack_attention_kernel(
    places, a0, a1, b0, b1, o_rest, o_query, o_key, o_value, o_pos, o_out,
    o_bias_u, o_bias_v, o_gain_1, o_shift_1, o_gain_2, o_shift_2, o_ffn_bias, whole, *, per_side
):
    core = places[2]
    total = 2 * a0.shape[0]
    gathered(places[0], whole, core * total, (a0, a1), per_side)
    gathered(places[1], whole, (1 - core) * total, (b0, b1), per_side)
    half = HALF_BLOCKS

    def fetch(block):
        start = (block // half) * total + ROWS * (block % half)
        return whole[start : start + ROWS]

    def vectors(targets, rows, start):
        for k, ref in enumerate(targets):
            ref[:, start : start + rows.shape[1]] = rows[k : k + 1]

    norms = (o_gain_1, o_shift_1, o_gain_2, o_shift_2, o_ffn_bias)
    unit = identity(128)
    rest = fetch(12)
    for m, ref in enumerate((o_query, o_key, o_value, o_pos)):
        for block in range(3):
            part = fetch(3 * m + block)
            ref[128 * block : 128 * block + 128, :] = mm_nt(unit, part)[:, :D]
            if m == 0:
                vectors((o_bias_u, o_bias_v), part[400:].astype(F32)[10:], 128 * block)
        tail = mm_nt(placer(REST, m * REST), rest)
        ref[384:, :] = tail[:, :D]
        if m == 0:
            vectors((o_bias_u, o_bias_v), rest[400:, :REST].astype(F32)[10:], 384)
    for block in range(3):
        part = fetch(13 + block).astype(F32)
        o_out[:, 128 * block : 128 * block + 128] = part[:D]
        vectors(norms, part[D:], 128 * block)
    tail = mm_nt(o_rest[...], placer(REST, 2 * REST))
    o_out[:, 384:] = tail[:D]
    vectors(norms, tail[D:], 384)


def unpack_ffn_kernel(places, a0, a1, o_in, o_bias, o_out_t, o_rest, whole, *, per_side):
    gathered(places[0], whole, 0, (a0, a1), per_side)
    units = o_in.shape[1]
    full = units // 128
    for block in range(full):
        lanes = slice(128 * block, 128 * block + 128)
        part = whole[ROWS * block : ROWS * block + ROWS].astype(F32)
        o_in[:, lanes] = part[:D]
        o_bias[:, lanes] = part[D : D + 1]
        start = ROWS * (full + block)
        o_out_t[:, lanes] = whole[start : start + ROWS].astype(F32)[:D]
    rest = whole[ROWS * 2 * full : ROWS * 2 * full + ROWS]
    o_rest[...] = rest
    left = units - 128 * full
    part = mm_nt(rest, placer(left, 0))
    o_in[:, 128 * full :] = part[:D]
    o_bias[:, 128 * full :] = part[D : D + 1]
    o_out_t[:, 128 * full :] = mm_nt(rest, placer(left, left))[:D]


def whole_spec():
    return pl.BlockSpec(memory_space=pltpu.VMEM)


def any_spec():
    return pl.BlockSpec(memory_space=pl.ANY)


def far_spec():
    return pl.BlockSpec(memory_space=pltpu.HBM)


def scalar_spec():
    return pl.BlockSpec(memory_space=pltpu.SMEM)


def params(limit=VMEM_BYTES):
    return pltpu.CompilerParams(vmem_limit_bytes=limit)


def cost(flops, moved):
    return pl.CostEstimate(flops=int(flops), bytes_accessed=int(moved), transcendentals=0)


def shape(dims, dtype=LOW):
    return jax.ShapeDtypeStruct(dims, dtype)


def prepare(w_query, w_key, w_value, w_pos, w_out, bias_u, bias_v, pos_table):
    operands = (w_query, w_key, w_value, w_pos, w_out, bias_u[None], bias_v[None], pos_table)
    results = (
        ((PAIRS, D, 128), LOW),
        ((PAIRS, D, 256), LOW),
        ((PAIRS, SPAN, 128), LOW),
        ((WIDE, D), LOW),
        ((PAIRS, 2, 8, 128), F32),
    )
    return pl.pallas_call(
        prep_kernel,
        out_shape=tuple(shape(*r) for r in results),
        in_specs=[far_spec()] * len(operands),
        out_specs=(far_spec(),) * len(results),
        scratch_shapes=[pltpu.VMEM(a.shape, a.dtype) for a in operands]
        + [pltpu.VMEM(*r) for r in results]
        + [pltpu.SemaphoreType.DMA((16,))],
        compiler_params=params(),
        cost_estimate=cost(3e9, 5e6),
        name="prepare_weights",
    )(*operands)


def near(values):
    return pltpu.with_memory_space_constraint(values, pltpu.VMEM)


def far(values):
    return pltpu.with_memory_space_constraint(values, pltpu.HBM)


def layer(place, seg_len, mem_len, rows, reset, wq, wkv, rel, bias, wo, out_grads, own, other, vectors, size):
    units = own[0].shape[1]
    weights = (own[0], other[0], own[1], other[1], own[2], other[2])
    operands = [*rows, reset, wq, wkv, rel, bias, wo, *out_grads, *weights, *vectors]
    for k in RECEIVED:
        operands[k] = pltpu.with_memory_space_constraint(operands[k], pltpu.VMEM)
    results = (
        ((PAIRS, 2, 2, SEG, KEYS), LOW),
        ((PAIRS, 2, KEYS, 256), LOW),
        ((PAIRS, 2, SEG, 256), LOW),
        ((2, SEG, WIDE), F32),
        ((2, SEG, WIDE), F32),
        ((2, KEYS, D), LOW),
        ((2, SEG, D), LOW),
        ((2, SEG, D), F32),
        ((2, SEG, WIDE), F32),
        ((size, 128), LOW),
        ((size, 128), LOW),
        ((3, ROWS, 128), LOW),
    )
    return pl.pallas_call(
        layer_kernel,
        out_shape=tuple(shape(*r) for r in results),
        in_specs=[scalar_spec()] * 3
        + [any_spec() if k in RECEIVED else far_spec() for k in range(len(operands))],
        out_specs=(far_spec(),) * len(results),
        scratch_shapes=[pltpu.VMEM(a.shape, a.dtype) for a in operands]
        + [pltpu.VMEM(*r) for r in results]
        + [
            pltpu.VMEM((4, 4 * D, 128), F32),
            pltpu.VMEM((2, SEG, KEYS), F32),
            pltpu.VMEM((2, SEG, D), LOW),
            pltpu.VMEM((2 * SEG, 512), LOW),
            pltpu.VMEM((2 * SEG, D), LOW),
            pltpu.VMEM((2 * SEG, 512), LOW),
            pltpu.VMEM((2, 2 * SEG, units), LOW),
            pltpu.VMEM((2, 2 * SEG, units), LOW),
            pltpu.VMEM((8, D), F32),
            pltpu.VMEM((2, SEG, WIDE), LOW),
            pltpu.VMEM((2, 2 * SEG, units), F32),
            pltpu.SemaphoreType.DMA((48,)),
            pltpu.SemaphoreType.DMA((3, PAIRS, 2)),
        ],
        compiler_params=params(LAYER_BYTES),
        cost_estimate=cost(2e10, 3e7),
        name="layer",
    )(place, seg_len, mem_len, *operands)


def attend_back(pairs, operands, extra=(), size=0, fetched=False):
    count = len(pairs)
    total = PAIRS if size else count
    results = [shape((count, 2, SEG, 384))]
    if size:
        results += [shape((size, 128)), shape((size, 128))]
    else:
        results += [shape((count, 512, D)), shape((count, 8, 128), F32)]
    scratch = []
    if fetched:
        scratch = [
            pltpu.VMEM((count, 2, 2, SEG, KEYS), LOW),
            pltpu.VMEM((count, 2, KEYS, 256), LOW),
            pltpu.VMEM((count, 2, SEG, 256), LOW),
            pltpu.VMEM((count, SPAN, 128), LOW),
            pltpu.VMEM((count, 2, SEG, 128), F32),
            pltpu.VMEM((count, 2, SEG, 128), F32),
            pltpu.VMEM((count, 2, SEG, 128), F32),
            pltpu.VMEM((2, KEYS, D), LOW),
            pltpu.VMEM((SPAN, D), LOW),
            pltpu.SemaphoreType.DMA((20 * count,)),
        ]
    scratch += [
        pltpu.VMEM((2, 2, SEG, KEYS), LOW),
        pltpu.VMEM((2, 2, SEG, KEYS), LOW),
        pltpu.VMEM((128, KEYS), F32),
        pltpu.VMEM((2, 256, KEYS), LOW),
        pltpu.VMEM((total, 512, D), LOW),
        pltpu.VMEM((total, 8, 128), F32),
    ]
    if size:
        scratch.append(pltpu.VMEM((2 * HALF_BLOCKS, ROWS, 128), LOW))
    place = far if fetched else near
    return pl.pallas_call(
        functools.partial(
            back_kernel, pairs=pairs, calls=max(0, len(extra) // 2 - 1), fetched=fetched
        ),
        out_shape=tuple(results),
        in_specs=[far_spec() if fetched else whole_spec()] * 9
        + ([scalar_spec()] + [whole_spec()] * (len(extra) - 1) if size else []),
        out_specs=(whole_spec(),) * 3,
        scratch_shapes=scratch,
        compiler_params=params(LESS_BYTES),
        cost_estimate=cost(1.5e10 * count, 8e6),
        name=f"attend_back_{pairs[0]}",
    )(*(place(a) for a in operands), *extra)


def input_gradient(first_grad, tokens, wq, wkv):
    operands = [
        pltpu.with_memory_space_constraint(a, pltpu.HBM) for a in (first_grad, wq, wkv, *tokens)
    ]
    return pl.pallas_call(
        functools.partial(input_kernel, count=len(operands)),
        out_shape=shape((2, SEG, D), F32),
        in_specs=[far_spec()] * len(operands),
        out_specs=far_spec(),
        scratch_shapes=[pltpu.VMEM(a.shape, a.dtype) for a in operands]
        + [pltpu.VMEM((2, SEG, D), F32), pltpu.SemaphoreType.DMA((len(operands) + 2,))],
        compiler_params=params(LESS_BYTES),
        cost_estimate=cost(1.6e9, 6e6),
        name="input_gradient",
    )(*operands)


def unpack_attention(places, pieces, rest, dp_size):
    total = sum(p.shape[0] for p in pieces)
    return pl.pallas_call(
        functools.partial(unpack_attention_kernel, per_side=dp_size // 2),
        out_shape=(shape((D, D), F32),) * 5 + (shape((1, D), F32),) * 7,
        in_specs=[scalar_spec()] + [whole_spec()] * 5,
        out_specs=(whole_spec(),) * 12,
        scratch_shapes=[pltpu.VMEM((total, 128), LOW)],
        compiler_params=params(LESS_BYTES),
        cost_estimate=cost(5e8, 6e6),
        name="unpack_attention",
    )(places, *pieces, rest)


def unpack_ffn(places, pieces, units, dp_size):
    total = sum(p.shape[0] for p in pieces)
    return pl.pallas_call(
        functools.partial(unpack_ffn_kernel, per_side=dp_size // 2),
        out_shape=(
            shape((D, units), F32), shape((1, units), F32), shape((D, units), F32),
            shape((ROWS, 128)),
        ),
        in_specs=[scalar_spec()] + [whole_spec()] * 2,
        out_specs=(whole_spec(),) * 4,
        scratch_shapes=[pltpu.VMEM((total, 128), LOW)],
        compiler_params=params(LESS_BYTES),
        cost_estimate=cost(5e8, 6e6),
        name="unpack_ffn",
    )(places, *pieces)


def swap(values):
    return lax.ppermute(values, "tp", [(0, 1), (1, 0)])


def orders_of(dp_size):
    bits = list(range(dp_size.bit_length() - 1))
    turned = list(bits)
    for k in range(0, len(bits) - 1, 2):
        turned[k], turned[k + 1] = bits[k + 1], bits[k]
    return bits, turned


class Ring:
    def __init__(self, dp_size, index, core):
        self.size, self.orders = dp_size, orders_of(dp_size)
        self.steps = len(self.orders[0])
        self.bits = [
            jnp.where(core == 0, (index >> a) & 1, (index >> b) & 1)
            for a, b in zip(*self.orders)
        ]

    def place(self, index, order):
        spot = 0
        for k in self.orders[order]:
            spot = 2 * spot + ((index >> k) & 1)
        return spot

    def send(self, values, step):
        pairs = []
        for i in range(self.size):
            for c in range(2):
                pairs.append((2 * i + c, 2 * (i ^ (1 << self.orders[c][step])) + c))
        return lax.ppermute(values, ("dp", "tp"), pairs)

    def sides(self, keep, came, step):
        rows = keep.shape[0] // 2
        bit = self.bits[step]

        def side(which):
            start = which * rows
            return lax.dynamic_slice_in_dim(keep, start, rows, 0) + lax.dynamic_slice_in_dim(
                came, start, rows, 0
            )

        return side(1 - bit), side(bit)


def after(value, *others):
    return lax.optimization_barrier((value,) + others)


def rounded_rows(rows, unit):
    return -(-rows // unit) * unit


def make_shards(dp_size):
    table = position_table()

    def shards(
        hidden, memory, segment_length, memory_length, doc_reset, w_query, w_key, w_value, w_pos,
        bias_u, bias_v, w_out, first_gain, first_shift, ffn_in, ffn_in_bias, ffn_out, ffn_out_bias,
        second_gain, second_shift, out_grad,
    ):
        core = lax.axis_index("tp")
        index = lax.axis_index("dp")
        place = core[None].astype(jnp.int32)
        units = ffn_in.shape[1]
        pos_table = jnp.asarray(table)

        def by_feature(values):
            return values.transpose(2, 0, 1).reshape(-1, values.shape[1])

        hidden_t, memory_t, out_grad_t = (by_feature(a) for a in (hidden, memory, out_grad))
        hidden_in, memory_in, out_grad_in = swap(hidden_t), swap(memory_t), swap(out_grad_t)
        own_ffn = (ffn_in, ffn_in_bias[None], ffn_out.T)
        other_ffn = tuple(swap(a) for a in own_ffn)

        wq, wkv, rel, wo, bias = prepare(
            w_query, w_key, w_value, w_pos, w_out, bias_u, bias_v, pos_table
        )
        full = units // 128
        unit = 16 * dp_size
        (
            probs, kv, uv, att, inv, joined, act, first_grad, ga, ffn_own, ffn_other, out_blocks
        ) = layer(
            place, segment_length, memory_length, (hidden_t, memory_t, hidden_in, memory_in),
            doc_reset, wq, wkv, rel, bias, wo, (out_grad_t, out_grad_in), own_ffn, other_ffn,
            tuple(v[None] for v in (first_gain, first_shift, ffn_out_bias, second_gain, second_shift)),
            rounded_rows(ROWS * (2 * full + 1), unit),
        )
        ring = Ring(dp_size, index, core)
        straight, turned = ring.place(index, 0), ring.place(index, 1)
        places = jnp.stack(
            [
                jnp.where(core == 0, straight, turned),
                jnp.where(core == 0, turned, straight),
                core,
            ]
        ).astype(jnp.int32)

        def give_back(values, dtype):
            rows = values.shape[1] // 2
            mine = lax.dynamic_slice_in_dim(values, core * rows, rows, 1)
            theirs = lax.dynamic_slice_in_dim(values, (1 - core) * rows, rows, 1)
            came = swap(theirs.astype(LOW)).astype(dtype)
            mine = mine.astype(dtype)
            whole = jnp.where(
                core == 0,
                jnp.concatenate([mine, came], axis=0),
                jnp.concatenate([came, mine], axis=0),
            )
            return with_layout_constraint(whole, Layout(major_to_minor=(2, 0, 1)))

        def kept_memory(hidden):
            rows = hidden.shape[1]
            positions = core * rows + jnp.arange(rows)
            later = (jnp.arange(SEG)[:, None] > positions[None, :]).astype(LOW)
            resets = jnp.dot(doc_reset.astype(LOW), later, preferred_element_type=F32)
            keep = (resets == 0.0) & (positions[None, :] < segment_length[:, None])
            by_feature = hidden.transpose(2, 0, 1)
            return jnp.where(keep[None], by_feature, jnp.zeros_like(by_feature))

        steps = ring.steps
        slots = [[(0,)], [(1, 2, 3)], [(4,)]]
        operands = [probs, kv, uv, rel, ga, att, inv, joined, pos_table]
        tokens, wides, biases = [], [], []

        def back_slot(waited, slot):
            packed = None
            for pairs in slot:
                last = pairs[-1] == PAIRS - 1
                result = attend_back(
                    pairs,
                    operands,
                    (place, out_blocks, *wides, *biases) if last else (),
                    rounded_rows(ROWS * HALF_BLOCKS, unit) if last else 0,
                    fetched=not pairs[0],
                )
                waited, *result = after(waited, *result)
                tokens.append(result[0])
                operands[4], _ = after(operands[4], result[0])
                if last:
                    packed = result[1:]
                else:
                    wides.append(result[1])
                    biases.append(result[2])
            return waited, packed

        keep, came = ffn_own, swap(ffn_other)
        came, _ = back_slot(came, slots[0])
        first_steps = len(slots) - 1
        for step in range(first_steps):
            sent, kept = ring.sides(keep, came, step)
            sent, kept, operands[4] = after(sent, kept, operands[4])
            keep, came = kept, ring.send(sent, step)
            came, packed = back_slot(came, slots[step + 1])
        att_keep, att_send = packed
        att_came = swap(att_send)
        places, att_came = after(places, att_came)
        ffn = {"keep": keep, "came": came}

        def ffn_hop(kind, step, *others):
            ffn["keep"], ffn["came"], *_ = after(ffn["keep"], ffn["came"], *others)
            if kind == "scatter":
                sent, ffn["keep"] = ring.sides(ffn["keep"], ffn["came"], step)
            elif step == steps - 1:
                sent = ffn["keep"] = ffn["keep"] + ffn["came"]
            else:
                sent = ffn["keep"] = jnp.concatenate([ffn["keep"], ffn["came"]], axis=0)
            ffn["came"] = ring.send(sent, step)
            return sent

        hops = [("scatter", k) for k in range(first_steps, steps)]
        hops += [("gather", k) for k in range(steps - 1, -1, -1)]
        sent = ffn_hop(*hops.pop(0))
        att_keep, _ = after(att_keep, sent)
        for step in range(steps):
            sent, kept = ring.sides(att_keep, att_came, step)
            att_keep, att_came = kept, ring.send(sent, step)
            if len(hops) > 1:
                ffn_hop(*hops.pop(0), sent)
            if step == 0:
                first_grad, att_keep = after(first_grad, att_keep)
                input_own = input_gradient(first_grad, tokens, wq, wkv)
                att_came, input_own = after(att_came, input_own)
            elif step == 3:
                act, late_hidden, att_keep = after(act, hidden, att_keep)
                activations, new_memory = give_back(act, LOW), kept_memory(late_hidden)
                att_came, activations, new_memory = after(att_came, activations, new_memory)
        summed = att_keep + att_came
        for hop in hops:
            ffn_hop(*hop, summed)
        ffn_pieces = (ffn["keep"], ffn["came"])
        values = summed
        for step in range(steps - 1, 0, -1):
            came = ring.send(values, step)
            if step == steps - 1:
                input_own, values = after(input_own, values)
                input_grad = give_back(input_own, F32)
                came, input_grad = after(came, input_grad)
            values = jnp.concatenate([values, came], axis=0)
        came = ring.send(values, 0)
        near = swap(values)
        filled = list(unpack_ffn(places, ffn_pieces, units, dp_size))
        filled[1] = filled[1].reshape(-1)
        came, near, *filled = after(came, near, *filled)
        grad_in, grad_in_bias, grad_ffn_out_t, rest = filled
        g_query, g_key, g_value, g_pos, g_out, *vectors = unpack_attention(
            places, (values, came, near, swap(came)), rest, dp_size
        )
        g_bias_u, g_bias_v, g_gain_1, g_shift_1, g_gain_2, g_shift_2, g_ffn_bias = (
            v[0] for v in vectors
        )

        def by_token(values):
            return values.transpose(1, 2, 0)

        return (
            by_token(new_memory), activations, input_grad,
            g_query, g_key, g_value, g_pos, g_bias_u, g_bias_v, g_out, g_gain_1, g_shift_1,
            grad_in, grad_in_bias, grad_ffn_out_t.T, g_ffn_bias, g_gain_2, g_shift_2,
        )

    return shards


def solution(mesh):
    rows, copied = P("dp", "tp", None), P()
    shards = make_shards(mesh.shape["dp"])
    return jax.shard_map(
        shards,
        mesh=mesh,
        in_specs=(
            rows, rows, P("dp"), P("dp"), P("dp", None),
            copied, copied, copied, copied, copied, copied, copied, copied, copied,
            P(None, "tp"), P("tp"), P("tp", None),
            copied, copied, copied, rows,
        ),
        out_specs=(
            rows, rows, rows, copied, copied, copied, copied, copied, copied, copied, copied, copied,
            P(None, "tp"), P("tp"), P("tp", None), copied, copied, copied,
        ),
        check_vma=False,
    )
```

```python
import functools
import math

import jax
import jax.numpy as jnp
import ml_dtypes
import numpy as np
from jax import lax
from jax.experimental import pallas as pl
from jax.experimental.layout import Layout, with_layout_constraint
from jax.experimental.pallas import tpu as pltpu
from jax.sharding import PartitionSpec as P

D = 410
HEADS = 10
DHEAD = 41
SEG = 256
MEM = 256
KEYS = MEM + SEG
HALF = 128
PAIRS = HEADS // 2
WIDE = PAIRS * 128
ROWS = 416
SPAN = 768
REST = 26
HALF_BLOCKS = 8
RECEIVED = (2, 3, 11, 13, 17)
EPSILON = 1e-05
NEG_LARGE = -1e30
FACTOR = 1.0 / math.sqrt(DHEAD)
LOG2E = 1.0 / math.log(2.0)
LOW = jnp.bfloat16
VMEM_BYTES = 60 * 1024 * 1024
LAYER_BYTES = 54 * 1024 * 1024
LESS_BYTES = 15 * 1024 * 1024
F32 = jnp.float32


def position_table():
    distance = (KEYS - 1 - np.arange(SPAN)).astype(np.float32)
    inverse = np.float32(1.0) / np.float32(10000.0) ** (
        np.arange(0, D, 2).astype(np.float32) / np.float32(D)
    )
    angles = distance[:, None] * inverse[None, :].astype(np.float32)
    table = np.concatenate([np.sin(angles), np.cos(angles)], axis=1)
    return table.astype(ml_dtypes.bfloat16)


def mm(left, right):
    return lax.dot_general(left, right, (((1,), (0,)), ((), ())), preferred_element_type=F32)


def mm_nt(left, right):
    return lax.dot_general(left, right, (((1,), (1,)), ((), ())), preferred_element_type=F32)


def expander(rows):
    row = lax.broadcasted_iota(jnp.int32, (rows, WIDE), 0)
    lane = lax.broadcasted_iota(jnp.int32, (rows, WIDE), 1)
    inside = lane & 63
    hit = (inside < DHEAD) & (row == (lane >> 6) * DHEAD + inside)
    return jnp.where(hit, 1.0, 0.0).astype(LOW)


def compressor():
    row = lax.broadcasted_iota(jnp.int32, (WIDE, D), 0)
    lane = lax.broadcasted_iota(jnp.int32, (WIDE, D), 1)
    inside = row & 63
    hit = (inside < DHEAD) & (lane == (row >> 6) * DHEAD + inside)
    return jnp.where(hit, 1.0, 0.0).astype(LOW)


def identity(size):
    row = lax.broadcasted_iota(jnp.int32, (size, size), 0)
    lane = lax.broadcasted_iota(jnp.int32, (size, size), 1)
    return jnp.where(row == lane, 1.0, 0.0).astype(LOW)


def reversal(size):
    row = lax.broadcasted_iota(jnp.int32, (size, size), 0)
    lane = lax.broadcasted_iota(jnp.int32, (size, size), 1)
    return jnp.where(row + lane == size - 1, 1.0, 0.0).astype(LOW)


class Mover:
    def __init__(self, sems):
        self.sems, self.used, self.open = sems, 0, []

    def start(self, source, target):
        copy = pltpu.make_async_copy(source, target, self.sems.at[self.used])
        self.used += 1
        copy.start()
        self.open.append(copy)
        return copy

    def finish(self):
        for copy in self.open:
            copy.wait()
        self.open = []

    def wait(self, *copies):
        for copy in copies:
            copy.wait()
        self.open = [c for c in self.open if all(c is not d for d in copies)]


def prep_kernel(
    wq_in, wk_in, wv_in, wp_in, wo_in, bias_u_in, bias_v_in, pos_in, q_out, kv_out, rel_out, wo_out,
    bias_out, wq, wk, wv, wp, wo, bias_u, bias_v, pos, o_q, o_kv, o_rel, o_wo, o_bias, sems
):
    mover = Mover(sems)
    loads = [
        mover.start(a, b)
        for a, b in zip(
            (wp_in, pos_in, wk_in, wv_in, wq_in, wo_in, bias_u_in, bias_v_in),
            (wp, pos, wk, wv, wq, wo, bias_u, bias_v),
        )
    ]
    expand = expander(D)
    mover.wait(*loads[:2])
    rel = mm(pos[...], mm(wp[...], expand).astype(LOW)).astype(LOW)
    for p in range(PAIRS):
        o_rel[p] = rel[:, 128 * p : 128 * p + 128]
    mover.start(o_rel, rel_out)
    mover.wait(*loads[2:4])
    k_wide = mm(wk[...], expand).astype(LOW)
    v_wide = mm(wv[...], expand).astype(LOW)
    for p in range(PAIRS):
        o_kv[p, :, :128] = k_wide[:, 128 * p : 128 * p + 128]
        o_kv[p, :, 128:] = v_wide[:, 128 * p : 128 * p + 128]
    mover.start(o_kv, kv_out)
    mover.wait(*loads[4:])
    q_wide = mm(wq[...], expand).astype(LOW)
    for p in range(PAIRS):
        o_q[p] = q_wide[:, 128 * p : 128 * p + 128]
    mover.start(o_q, q_out)
    o_wo[...] = mm(compressor(), wo[...]).astype(LOW)
    mover.start(o_wo, wo_out)
    parts = []
    for bias in (bias_u, bias_v):
        rest = bias[...]
        for _ in range(3):
            parts.append(rest.astype(LOW).astype(F32))
            rest = rest - parts[-1]
    wide = mm(jnp.concatenate(parts + [jnp.zeros((2, D), F32)], axis=0).astype(LOW), expand)
    for k in range(2):
        row = jnp.broadcast_to(wide[3 * k : 3 * k + 1] + wide[3 * k + 1 : 3 * k + 2], (8, WIDE))
        row = row + wide[3 * k + 2 : 3 * k + 3]
        for p in range(PAIRS):
            o_bias[p, k] = row[:, 128 * p : 128 * p + 128]
    mover.start(o_bias, bias_out)
    mover.finish()


def spread_streams(source, raw, core, unit, store):
    raw[...] = source[...].astype(F32)
    for s in range(2):
        columns = raw[pl.ds(2 * core + s, D, stride=4), :].astype(LOW)
        store(s, mm_nt(unit, columns).astype(LOW))


def layer_kernel(
    place, seg_len, mem_len, hidden_hbm, memory_hbm, hidden_in_hbm, memory_in_hbm, reset_hbm,
    wq_hbm, wkv_hbm, rel_hbm, bias_hbm, wo_hbm, out_grad_hbm, out_grad_in_hbm,
    win_a_hbm, win_b_hbm, bin_a_hbm, bin_b_hbm, wout_a_hbm, wout_b_hbm,
    gain_1_hbm, shift_1_hbm, bias_out_hbm, gain_2_hbm, shift_2_hbm,
    probs_out, kv_out, uv_out, att_out, inv_out, joined_out,
    act_out, first_out, ga_out, own_out, other_out, blocks_out,
    hidden, memory, hidden_in, memory_in, reset, wq, wkv, rel, bias, wo, out_grad, out_grad_in,
    win_a, win_b, bin_a, bin_b, wout_a, wout_b, gain_1, shift_1, bias_out, gain_2, shift_2,
    o_probs, o_kv, o_uv, o_att, o_inv, o_joined, o_act, o_first, o_ga, o_own, o_other, o_out,
    raw, mask, og, low_in, gb_all, gs_all, active, inner, vecs, att, slopes, sems, step_sems
):
    mover = Mover(sems)
    loads = [
        mover.start(a, b)
        for a, b in zip(
            (
                memory_hbm, memory_in_hbm, hidden_hbm, hidden_in_hbm, reset_hbm,
                wkv_hbm, wq_hbm, bias_hbm, rel_hbm,
                gain_1_hbm, shift_1_hbm, bias_out_hbm, gain_2_hbm, shift_2_hbm, bin_a_hbm,
                bin_b_hbm, wo_hbm, out_grad_hbm, out_grad_in_hbm,
                win_a_hbm, wout_a_hbm, win_b_hbm, wout_b_hbm,
            ),
            (
                memory, memory_in, hidden, hidden_in, reset, wkv, wq, bias, rel,
                gain_1, shift_1, bias_out, gain_2, shift_2, bin_a,
                bin_b, wo, out_grad, out_grad_in, win_a, wout_a, win_b, wout_b,
            ),
        )
    ]
    core = place[0]
    mine = pl.multiple_of(HALF * core, HALF)
    other = pl.multiple_of(HALF * (1 - core), HALF)
    unit = identity(HALF)
    row = lax.broadcasted_iota(jnp.int32, (SEG, SEG), 0)
    lane = lax.broadcasted_iota(jnp.int32, (SEG, SEG), 1)
    lower = jnp.where(row >= lane, 1.0, 0.0).astype(LOW)
    for index, (source, base) in enumerate(
        ((memory, mine), (memory_in, other), (hidden, MEM + mine), (hidden_in, MEM + other))
    ):

        def store(s, values, base=base):
            o_joined[s, pl.ds(pl.multiple_of(base, HALF), HALF)] = values

        mover.wait(loads[index])
        spread_streams(source, raw.at[index], core, unit, store)
    mover.wait(*loads[4:9])
    mover.start(o_joined, joined_out)
    for s in range(2):
        own = 2 * core + s
        starts = jnp.broadcast_to(reset[pl.ds(own, 1), :].astype(F32), (8, SEG)).astype(LOW)
        doc_column = mm_nt(lower, starts)[:, :1]
        doc_row = mm_nt(starts, lower)[:1, :]
        memory_ok = (lane >= MEM - mem_len[own]) & (doc_column == 0.0)
        segment_ok = ((row > lane) & (doc_row == doc_column) & (lane < seg_len[own])) | (row == lane)
        mask[s, :, :MEM] = jnp.where(memory_ok, 0.0, NEG_LARGE)
        mask[s, :, MEM:] = jnp.where(segment_ok, 0.0, NEG_LARGE)
    first_head = lax.broadcasted_iota(jnp.int32, (HALF, 128), 1) < 64
    zero = jnp.zeros((HALF, 128), LOW)
    ones_lane = (lax.broadcasted_iota(jnp.int32, (KEYS, 256), 1) & 190) == 190

    for p in range(PAIRS):
        for s in range(2):
            pair_rows = jnp.where(ones_lane, 1.0, mm(o_joined[s], wkv[p])).astype(LOW)
            o_kv[p, s] = pair_rows
            queries = mm(o_joined[s, MEM:], wq[p])
            o_uv[p, s, :, :128] = (queries + bias[p, 0, :1]).astype(LOW)
            o_uv[p, s, :, 128:] = (queries + bias[p, 1, :1]).astype(LOW)

    def stacked(values):
        return jnp.concatenate(
            [jnp.where(first_head, values, zero), jnp.where(first_head, zero, values)], axis=0
        )

    def score(p, s, b):
        count = KEYS if b else KEYS - HALF
        rows = slice(HALF * b, HALF * b + HALF)
        start_row = HALF - HALF * b
        content = mm_nt(stacked(o_uv[p, s, rows, :128]), o_kv[p, s, :count, :128])
        relative = mm_nt(stacked(o_uv[p, s, rows, 128:]), rel[p, start_row : start_row + count])
        spots = mask[s, rows, :count]
        scores = []
        for h in range(2):
            part = slice(HALF * h, HALF * h + HALF)
            turned = pltpu.roll(relative[part], count - HALF + 1, 1, stride=1, stride_axis=0)
            scores.append((content[part] + turned) * (FACTOR * LOG2E) + spots)
        return scores

    def soften(p, s, b, scores):
        count = KEYS if b else KEYS - HALF
        rows = slice(HALF * b, HALF * b + HALF)
        exp_terms = []
        for h in range(2):
            top = jnp.max(scores[h], axis=1, keepdims=True)
            exp_terms.append(jnp.exp2(scores[h] - top).astype(LOW))
            o_probs[p, s, h, rows, :count] = exp_terms[h]
            if b == 0:
                o_probs[p, s, h, rows, count:] = jnp.zeros((HALF, HALF), LOW)
        return jnp.concatenate(exp_terms, axis=0)

    def mix(p, s, b, exp_terms):
        lanes = pl.ds(pl.multiple_of(128 * p, 128), 128)
        count = KEYS if b else KEYS - HALF
        rows = slice(HALF * b, HALF * b + HALF)
        mixed = mm(exp_terms, o_kv[p, s, :count, 128:])
        inverse = jnp.where(first_head, 1.0 / mixed[:HALF, 63:64], 1.0 / mixed[HALF:, 127:])
        o_inv[s, rows, lanes] = inverse
        o_att[s, rows, lanes] = jnp.where(first_head, mixed[:HALF], mixed[HALF:]) * inverse

    def step(p, carry):
        blocks = [(s, b) for s in range(2) for b in range(2)]
        scores, mixing = score(p, *blocks[0]), None
        for k, block in enumerate(blocks):
            following = score(p, *blocks[k + 1]) if k + 1 < len(blocks) else None
            exp_terms = soften(p, *block, scores)
            if mixing is not None:
                mix(p, *mixing)
            mixing, scores = (*block, exp_terms), following
        mix(p, *mixing)
        for s in range(2):
            for copy in step_copies(p, s):
                copy.start()
        return carry

    def step_copies(p, s):
        return [
            pltpu.make_async_copy(a.at[p, s], b.at[p, s], step_sems.at[k, p, s])
            for k, (a, b) in enumerate(((o_probs, probs_out), (o_kv, kv_out), (o_uv, uv_out)))
        ]

    lax.fori_loop(0, PAIRS, step, 0)
    mover.start(o_att, att_out)
    mover.start(o_inv, inv_out)
    hidden_units = win_a.shape[1]
    chunks = [(a, min(a + 256, hidden_units)) for a in range(0, hidden_units, 256)]
    halves = ((win_a, bin_a, wout_a), (win_b, bin_b, wout_b))
    low_in[:, 384:] = jnp.where(
        lax.broadcasted_iota(jnp.int32, (2 * SEG, 128), 1) == D - 384, 1.0, 0.0
    ).astype(LOW)
    gs_all[:, 384:] = jnp.zeros((2 * SEG, 128), LOW)
    vecs[...] = jnp.zeros_like(vecs)
    att[...] = o_att[...].astype(LOW)
    mover.wait(*loads[9:])
    for index, (source, base) in enumerate(((out_grad, mine), (out_grad_in, other))):

        def store_grad(s, values, base=base):
            og[s, pl.ds(base, HALF)] = values

        spread_streams(source, raw.at[index], core, unit, store_grad)
    tokens = 2 * SEG
    hid = o_joined[:, MEM:].reshape(tokens, D).astype(F32)
    hat_1, scale_1 = norm_forward(hid + mm(att[...].reshape(tokens, WIDE), wo[...]))
    first = hat_1 * gain_1[...] + shift_1[...]
    first_low = first.astype(LOW)
    low_in[:, :D] = first_low
    ffn_sum = first + bias_out[...]
    for which, (win, b_in, wout) in enumerate(halves):
        for a, z in chunks:
            pre = mm(first_low, win[:, a:z]) + b_in[:, a:z].astype(F32)
            act, slope = gelu_both(pre)
            act = act.astype(LOW)
            slopes[which, :, a:z] = slope
            active[which, :, a:z] = act
            ffn_sum = ffn_sum + mm_nt(act, wout[:, a:z])
    hat_2, scale_2 = norm_forward(ffn_sum)
    o_act[...] = (hat_2 * gain_2[...] + shift_2[...]).astype(LOW).reshape(2, SEG, D)
    cot = og[...].reshape(tokens, D).astype(F32)
    vecs[2:3] = total_rows(cot * hat_2)
    vecs[3:4] = total_rows(cot)
    grad_second = norm_backward(cot * gain_2[...], hat_2, scale_2)
    vecs[4:5] = total_rows(grad_second)
    gs_low = grad_second.astype(LOW)
    gs_all[:, :D] = gs_low
    grad_first = grad_second
    for which, (win, b_in, wout) in enumerate(halves):
        for a, z in chunks:
            grad_inner = (mm(gs_low, wout[:, a:z]) * slopes[which, :, a:z]).astype(LOW)
            inner[which, :, a:z] = grad_inner
            grad_first = grad_first + mm_nt(grad_inner, win[:, a:z])
    vecs[0:1] = total_rows(grad_first * hat_1)
    vecs[1:2] = total_rows(grad_first)
    grad_pre = norm_backward(grad_first * gain_1[...], hat_1, scale_1)
    o_first[...] = grad_pre.reshape(2, SEG, D)
    grad_branch = grad_pre.astype(LOW)
    gb_all[...] = grad_branch
    o_ga[...] = mm_nt(grad_branch, wo[...]).reshape(2, SEG, WIDE)
    mover.start(o_act, act_out)
    mover.start(o_first, first_out)
    mover.start(o_ga, ga_out)
    grad_out = None
    for s in range(2):
        part = mm(att[s].T, gb_all[SEG * s : SEG * s + SEG])
        grad_out = part if grad_out is None else grad_out + part
    grad_out = mm(expander(ROWS), grad_out.astype(LOW))
    grad_out = (grad_out + mm(pick_rows(8), vecs[...].astype(LOW))).astype(LOW)
    for block in range(3):
        o_out[block] = grad_out[:, 128 * block : 128 * block + 128]
    mover.start(o_out, blocks_out)
    out_rest = mm(grad_out[:, 384:], placer(REST, 2 * REST))
    in_t = low_in[...].T[:ROWS]
    gs_t = gs_all[...].T[:ROWS]
    full = hidden_units // 128
    for which, pack, target in ((1, o_other, other_out), (0, o_own, own_out)):
        rest = out_rest
        for m, (left, right) in enumerate(((in_t, inner), (gs_t, active))):
            for a, z in chunks:
                grads = mm(left, right[which, :, a:z]).astype(LOW)
                for block in range(a // 128, min(-(-z // 128), full)):
                    part = grads[:, 128 * block - a : 128 * block - a + 128]
                    put(pack, ROWS * (full * m + block), part)
                if z > 128 * full:
                    rest = rest + mm(grads[:, 128 * full - a :], placer(REST, m * REST))
            span = pl.ds(ROWS * full * m, ROWS * full)
            mover.start(pack.at[span], target.at[span])
        put(pack, ROWS * 2 * full, rest.astype(LOW))
        span = pl.ds(ROWS * 2 * full, pack.shape[0] - ROWS * 2 * full)
        mover.start(pack.at[span], target.at[span])
    for p in range(PAIRS):
        for s in range(2):
            for copy in step_copies(p, s):
                copy.wait()
    mover.finish()


def norm_forward(values):
    centred = values - jnp.mean(values, axis=1, keepdims=True)
    scale = lax.rsqrt(jnp.mean(centred * centred, axis=1, keepdims=True) + EPSILON)
    return centred * scale, scale


def norm_backward(grad, x_hat, scale):
    return scale * (
        grad
        - jnp.mean(grad, axis=1, keepdims=True)
        - x_hat * jnp.mean(grad * x_hat, axis=1, keepdims=True)
    )


GELU_A = math.sqrt(2.0 / math.pi)
GELU_B = 0.044715


def gelu_both(x):
    square = x * x
    bent = jnp.tanh(x * (GELU_A + (GELU_A * GELU_B) * square))
    half_up = 0.5 + 0.5 * bent
    slope = half_up + (0.5 * x) * (1.0 - bent * bent) * (GELU_A + (3.0 * GELU_A * GELU_B) * square)
    return x * half_up, slope


def total_rows(values):
    return jnp.sum(values, axis=0, keepdims=True)


def placer(count, offset):
    row = lax.broadcasted_iota(jnp.int32, (count, 128), 0)
    lane = lax.broadcasted_iota(jnp.int32, (count, 128), 1)
    return jnp.where(lane == row + offset, 1.0, 0.0).astype(LOW)


def put(ref, start, values):
    ref[start : start + values.shape[0]] = values


def pick_rows(count):
    row = lax.broadcasted_iota(jnp.int32, (ROWS, count), 0)
    lane = lax.broadcasted_iota(jnp.int32, (ROWS, count), 1)
    return jnp.where(row == D + lane, 1.0, 0.0).astype(LOW)


def back_kernel(*refs, pairs, calls, fetched):
    refs = list(refs)

    def take(count):
        part = refs[:count]
        del refs[:count]
        return part

    sources = take(9)
    earlier = take(2 + 2 * calls) if calls else []
    outs = take(3)
    o_token = outs[0]
    loads = [([], []) for _ in pairs]
    if fetched:
        probs_hbm, kv_hbm, uv_hbm, rel_hbm, ga_hbm, att_hbm, inv_hbm, joined_hbm, pos_hbm = sources
        probs, kv, uv, rel, ga, att, inv, joined, pos = take(9)
        mover = Mover(take(1)[0])
        for n, pair in enumerate(pairs):
            lanes = slice(128 * pair, 128 * pair + 128)
            for s in range(2):
                for source, target in ((ga_hbm, ga), (att_hbm, att), (inv_hbm, inv)):
                    loads[n][s].append(mover.start(source.at[s, :, lanes], target.at[n, s]))
                for source, target in ((uv_hbm, uv), (kv_hbm, kv), (probs_hbm, probs)):
                    loads[n][s].append(mover.start(source.at[pair, s], target.at[n, s]))
                if s == 0:
                    loads[n][s].append(mover.start(rel_hbm.at[pair], rel.at[n]))
                if n == 0:
                    loads[n][s].append(mover.start(joined_hbm.at[s], joined.at[s]))
        loads[0][1].append(mover.start(pos_hbm, pos))
    else:
        probs, kv, uv, rel, ga, att, inv, joined, pos = sources
    scores, spread, grel, dkv, wide, sums = take(6)
    base = 0
    if calls:
        (whole,) = take(1)
        for source, tops in zip(earlier[2 : 2 + calls], earlier[2 + calls :]):
            count = source.shape[0]
            wide[base : base + count] = source[...]
            sums[base : base + count] = tops[...]
            base += count
    flip = reversal(HALF)
    first_head = lax.broadcasted_iota(jnp.int32, (HALF, 128), 1) < 64
    zero = jnp.zeros((HALF, 128), LOW)
    lane = lax.broadcasted_iota(jnp.int32, (SEG, 128), 1)
    into = lax.broadcasted_iota(jnp.int32, (128, 128), 0)
    out = lax.broadcasted_iota(jnp.int32, (128, 128), 1)
    head_sum = jnp.where(((out & 62) == 62) & ((into >> 6) == (out >> 6)), 1.0, 0.0).astype(LOW)
    for n, pair in enumerate(pairs):
        here = n if fetched else pair
        lanes = slice(128 * pair, 128 * pair + 128)

        def columns(values, s, n=n, lanes=lanes):
            return values[n, s] if fetched else values[s, :, lanes]

        grad_atts, u_ts, ga_ts = [], [], []
        for s in range(2):
            if fetched:
                mover.wait(*loads[n][s])
            wide_grad = columns(ga, s)
            inverse = columns(inv, s)
            inner = wide_grad * columns(att, s)
            inner_high = inner.astype(LOW)
            inner_low = (inner - inner_high.astype(F32)).astype(LOW)
            row_sums = (mm(inner_high, head_sum) + mm(inner_low, head_sum)) * inverse
            sums_high = row_sums.astype(LOW).astype(F32)
            grad_atts.append(
                jnp.where(
                    (lane & 63) == 62,
                    -sums_high,
                    jnp.where((lane & 63) == 63, sums_high - row_sums, wide_grad * inverse),
                ).astype(LOW)
            )
            u_ts.append(uv[here, s, :, :128].T)
            ga_ts.append(grad_atts[s].T)
        v_ts = [
            jnp.concatenate(
                [
                    mm(flip, uv[here, s, HALF * b : HALF * b + HALF, 128:]).astype(LOW).T
                    for s in range(2)
                ],
                axis=1,
            )
            for b in range(2)
        ]

        def differentiate(s, b):
            count = KEYS if b else KEYS - HALF
            part = grad_atts[s][HALF * b : HALF * b + HALF]
            both = jnp.concatenate(
                [jnp.where(first_head, part, zero), jnp.where(first_head, zero, part)], axis=0
            )
            return mm_nt(both, kv[here, s, :count, 128:])

        def spread_out(s, b, grad_probs):
            count = KEYS if b else KEYS - HALF
            rows = slice(HALF * b, HALF * b + HALF)
            for h in range(2):
                attn = probs[here, s, h, rows, :count].astype(F32)
                grad_scores = (attn * grad_probs[HALF * h : HALF * h + HALF]).astype(LOW)
                scores[s, h, rows, :count] = grad_scores
                if b == 0:
                    scores[s, h, rows, count:] = jnp.zeros((HALF, HALF), LOW)
                turned = pltpu.roll(mm(flip, grad_scores), 0, 1, stride=1, stride_axis=0)
                spread[b, h, HALF * s : HALF * s + HALF, :count] = turned.astype(LOW)

        def collect(s, b):
            count = KEYS if b else KEYS - HALF
            rows = slice(HALF * b, HALF * b + HALF)
            start_row = HALF - HALF * b

            def both(values):
                product = jnp.where(first_head, values[:HALF], values[HALF:])
                return product * FACTOR

            grad_u = both(
                mm(
                    jnp.concatenate([scores[s, h, rows, :count] for h in range(2)], axis=0),
                    kv[here, s, :count, :128],
                )
            )
            part = slice(HALF * s, HALF * s + HALF)
            grad_v = both(
                mm(
                    jnp.concatenate([spread[b, h, part, :count] for h in range(2)], axis=0),
                    rel[here, start_row : start_row + count],
                )
            )
            high = grad_v.astype(LOW)
            low = (grad_v - high.astype(F32)).astype(LOW)
            grad_q = (grad_u + (mm(flip, high) + mm(flip, low))).astype(LOW)
            o_token[n, s, rows, :128] = grad_q
            return total_rows(grad_u), total_rows(grad_v)

        parts = [(s, b) for s in range(2) for b in range(2)]
        grad_probs = differentiate(*parts[0])
        tops = []
        for k, part in enumerate(parts):
            following = differentiate(*parts[k + 1]) if k + 1 < len(parts) else None
            spread_out(*part, grad_probs)
            if k:
                tops.append(collect(*parts[k - 1]))
            grad_probs = following
        tops.append(collect(*parts[-1]))
        sum_u, sum_v = (sum(t[1:], t[0]) for t in zip(*tops))
        weight_kv, weight_q = None, None
        for s in range(2):
            for h in range(2):
                part = slice(64 * h, 64 * h + 64)
                dkv[s, part] = (mm(u_ts[s][part], scores[s, h]) * FACTOR).astype(LOW)
                dkv[s, 128 + 64 * h : 192 + 64 * h] = mm(ga_ts[s][part], probs[here, s, h]).astype(LOW)
            o_token[n, s, :, 128:] = dkv[s, :, MEM:].T
            part_kv = mm(dkv[s], joined[s])
            part_q = mm(o_token[n, s, :, :128].T, joined[s, MEM:])
            weight_kv = part_kv if weight_kv is None else weight_kv + part_kv
            weight_q = part_q if weight_q is None else weight_q + part_q
        for h in range(2):
            part = slice(64 * h, 64 * h + 64)
            first = mm(v_ts[0][part], spread[0, h, :, : KEYS - HALF])
            second = mm(v_ts[1][part], spread[1, h])
            grel[part, :HALF] = second[:, :HALF]
            grel[part, HALF:KEYS] = second[:, HALF:] + first
        spot = base + n
        wide[spot, :128] = weight_q.astype(LOW)
        wide[spot, 128:384] = weight_kv.astype(LOW)
        wide[spot, 384:] = mm((grel[...] * FACTOR).astype(LOW), pos[:KEYS]).astype(LOW)
        sums[spot] = jnp.concatenate([sum_u, sum_v, jnp.zeros((6, 128), F32)], axis=0)
    if calls:
        pack_attention(earlier[0], earlier[1], wide, sums, outs[1], outs[2], whole)
    else:
        outs[1][...] = wide[...]
        outs[2][...] = sums[...]


def pack_attention(place, out_blocks, wides, sums, keep, send, whole):
    core = place[0]
    pick = expander(ROWS)
    back = compressor()
    rest = jnp.zeros((ROWS, 128), F32)
    for m in range(4):
        total = None
        for p in range(PAIRS):
            part = mm(pick[:, 128 * p : 128 * p + 128], wides[p, 128 * m : 128 * m + 128])
            total = part if total is None else total + part
        if m == 0:
            vectors = None
            for p in range(PAIRS):
                part = mm(sums[p].astype(LOW), back[128 * p : 128 * p + 128])
                vectors = part if vectors is None else vectors + part
            total = total + mm(pick_rows(8), vectors.astype(LOW))
        total = total.astype(LOW)
        for block in range(3):
            whole[3 * m + block] = total[:, 128 * block : 128 * block + 128]
        rest = rest + mm(total[:, 384:], placer(REST, m * REST))
    whole[12] = rest.astype(LOW)
    for block in range(3):
        whole[13 + block] = out_blocks[block]
    half = whole.shape[0] // 2
    for block in range(half):
        keep[ROWS * block : ROWS * block + ROWS] = whole[core * half + block]
        send[ROWS * block : ROWS * block + ROWS] = whole[(1 - core) * half + block]
    if keep.shape[0] > half * ROWS:
        extra = keep.shape[0] - half * ROWS
        keep[half * ROWS :] = jnp.zeros((extra, 128), LOW)
        send[half * ROWS :] = jnp.zeros((extra, 128), LOW)


def input_kernel(*refs, count):
    sources, (result_hbm, *targets), (o_input, sems) = (
        refs[:count], refs[count : 2 * count + 1], refs[2 * count + 1 :]
    )
    mover = Mover(sems)
    loads = [mover.start(a, b) for a, b in zip(sources, targets)]
    first_grad, wq, wkv, *tokens = targets
    mover.wait(*loads[:3])
    total = [first_grad[s] for s in range(2)]
    p = 0
    for token, load in zip(tokens, loads[3:]):
        mover.wait(load)
        for n in range(token.shape[0]):
            weights = jnp.concatenate([wq[p], wkv[p]], axis=1)
            for s in range(2):
                total[s] = total[s] + mm_nt(token[n, s], weights)
            p += 1
    for s in range(2):
        o_input[s] = total[s]
        mover.start(o_input.at[s], result_hbm.at[s])
    mover.finish()


def gathered(where, target, base, pieces, per_side):
    size = pieces[0].shape[0] // per_side
    for side, ref in enumerate(pieces):

        def body(r, carry, side=side, ref=ref):
            spot = jnp.bitwise_xor(r + side * per_side, where)
            row = pl.multiple_of(base + spot * size, 16)
            target[pl.ds(row, size)] = ref[pl.ds(pl.multiple_of(r * size, 16), size)]
            return carry

        lax.fori_loop(0, per_side, body, 0)


def unpack_attention_kernel(
    places, a0, a1, b0, b1, o_rest, o_query, o_key, o_value, o_pos, o_out,
    o_bias_u, o_bias_v, o_gain_1, o_shift_1, o_gain_2, o_shift_2, o_ffn_bias, whole, *, per_side
):
    core = places[2]
    total = 2 * a0.shape[0]
    gathered(places[0], whole, core * total, (a0, a1), per_side)
    gathered(places[1], whole, (1 - core) * total, (b0, b1), per_side)
    half = HALF_BLOCKS

    def fetch(block):
        start = (block // half) * total + ROWS * (block % half)
        return whole[start : start + ROWS]

    def vectors(targets, rows, start):
        for k, ref in enumerate(targets):
            ref[:, start : start + rows.shape[1]] = rows[k : k + 1]

    norms = (o_gain_1, o_shift_1, o_gain_2, o_shift_2, o_ffn_bias)
    unit = identity(128)
    rest = fetch(12)
    for m, ref in enumerate((o_query, o_key, o_value, o_pos)):
        for block in range(3):
            part = fetch(3 * m + block)
            ref[128 * block : 128 * block + 128, :] = mm_nt(unit, part)[:, :D]
            if m == 0:
                vectors((o_bias_u, o_bias_v), part[400:].astype(F32)[10:], 128 * block)
        tail = mm_nt(placer(REST, m * REST), rest)
        ref[384:, :] = tail[:, :D]
        if m == 0:
            vectors((o_bias_u, o_bias_v), rest[400:, :REST].astype(F32)[10:], 384)
    for block in range(3):
        part = fetch(13 + block).astype(F32)
        o_out[:, 128 * block : 128 * block + 128] = part[:D]
        vectors(norms, part[D:], 128 * block)
    tail = mm_nt(o_rest[...], placer(REST, 2 * REST))
    o_out[:, 384:] = tail[:D]
    vectors(norms, tail[D:], 384)


def unpack_ffn_kernel(places, a0, a1, o_in, o_bias, o_out_t, o_rest, whole, *, per_side):
    gathered(places[0], whole, 0, (a0, a1), per_side)
    units = o_in.shape[1]
    full = units // 128
    for block in range(full):
        lanes = slice(128 * block, 128 * block + 128)
        part = whole[ROWS * block : ROWS * block + ROWS].astype(F32)
        o_in[:, lanes] = part[:D]
        o_bias[:, lanes] = part[D : D + 1]
        start = ROWS * (full + block)
        o_out_t[:, lanes] = whole[start : start + ROWS].astype(F32)[:D]
    rest = whole[ROWS * 2 * full : ROWS * 2 * full + ROWS]
    o_rest[...] = rest
    left = units - 128 * full
    part = mm_nt(rest, placer(left, 0))
    o_in[:, 128 * full :] = part[:D]
    o_bias[:, 128 * full :] = part[D : D + 1]
    o_out_t[:, 128 * full :] = mm_nt(rest, placer(left, left))[:D]


def whole_spec():
    return pl.BlockSpec(memory_space=pltpu.VMEM)


def any_spec():
    return pl.BlockSpec(memory_space=pl.ANY)


def far_spec():
    return pl.BlockSpec(memory_space=pltpu.HBM)


def scalar_spec():
    return pl.BlockSpec(memory_space=pltpu.SMEM)


def params(limit=VMEM_BYTES):
    return pltpu.CompilerParams(vmem_limit_bytes=limit)


def cost(flops, moved):
    return pl.CostEstimate(flops=int(flops), bytes_accessed=int(moved), transcendentals=0)


def shape(dims, dtype=LOW):
    return jax.ShapeDtypeStruct(dims, dtype)


def prepare(w_query, w_key, w_value, w_pos, w_out, bias_u, bias_v, pos_table):
    operands = (w_query, w_key, w_value, w_pos, w_out, bias_u[None], bias_v[None], pos_table)
    results = (
        ((PAIRS, D, 128), LOW),
        ((PAIRS, D, 256), LOW),
        ((PAIRS, SPAN, 128), LOW),
        ((WIDE, D), LOW),
        ((PAIRS, 2, 8, 128), F32),
    )
    return pl.pallas_call(
        prep_kernel,
        out_shape=tuple(shape(*r) for r in results),
        in_specs=[far_spec()] * len(operands),
        out_specs=(far_spec(),) * len(results),
        scratch_shapes=[pltpu.VMEM(a.shape, a.dtype) for a in operands]
        + [pltpu.VMEM(*r) for r in results]
        + [pltpu.SemaphoreType.DMA((16,))],
        compiler_params=params(),
        cost_estimate=cost(3e9, 5e6),
        name="prepare_weights",
    )(*operands)


def near(values):
    return pltpu.with_memory_space_constraint(values, pltpu.VMEM)


def far(values):
    return pltpu.with_memory_space_constraint(values, pltpu.HBM)


def layer(place, seg_len, mem_len, rows, reset, wq, wkv, rel, bias, wo, out_grads, own, other, vectors, size):
    units = own[0].shape[1]
    weights = (own[0], other[0], own[1], other[1], own[2], other[2])
    operands = [*rows, reset, wq, wkv, rel, bias, wo, *out_grads, *weights, *vectors]
    for k in RECEIVED:
        operands[k] = pltpu.with_memory_space_constraint(operands[k], pltpu.VMEM)
    results = (
        ((PAIRS, 2, 2, SEG, KEYS), LOW),
        ((PAIRS, 2, KEYS, 256), LOW),
        ((PAIRS, 2, SEG, 256), LOW),
        ((2, SEG, WIDE), F32),
        ((2, SEG, WIDE), F32),
        ((2, KEYS, D), LOW),
        ((2, SEG, D), LOW),
        ((2, SEG, D), F32),
        ((2, SEG, WIDE), F32),
        ((size, 128), LOW),
        ((size, 128), LOW),
        ((3, ROWS, 128), LOW),
    )
    return pl.pallas_call(
        layer_kernel,
        out_shape=tuple(shape(*r) for r in results),
        in_specs=[scalar_spec()] * 3
        + [any_spec() if k in RECEIVED else far_spec() for k in range(len(operands))],
        out_specs=(far_spec(),) * len(results),
        scratch_shapes=[pltpu.VMEM(a.shape, a.dtype) for a in operands]
        + [pltpu.VMEM(*r) for r in results]
        + [
            pltpu.VMEM((4, 4 * D, 128), F32),
            pltpu.VMEM((2, SEG, KEYS), F32),
            pltpu.VMEM((2, SEG, D), LOW),
            pltpu.VMEM((2 * SEG, 512), LOW),
            pltpu.VMEM((2 * SEG, D), LOW),
            pltpu.VMEM((2 * SEG, 512), LOW),
            pltpu.VMEM((2, 2 * SEG, units), LOW),
            pltpu.VMEM((2, 2 * SEG, units), LOW),
            pltpu.VMEM((8, D), F32),
            pltpu.VMEM((2, SEG, WIDE), LOW),
            pltpu.VMEM((2, 2 * SEG, units), F32),
            pltpu.SemaphoreType.DMA((48,)),
            pltpu.SemaphoreType.DMA((3, PAIRS, 2)),
        ],
        compiler_params=params(LAYER_BYTES),
        cost_estimate=cost(2e10, 3e7),
        name="layer",
    )(place, seg_len, mem_len, *operands)


def attend_back(pairs, operands, extra=(), size=0, fetched=False):
    count = len(pairs)
    total = PAIRS if size else count
    results = [pltpu.HBM((count, 2, SEG, 384), LOW)]
    if size:
        results += [shape((size, 128)), shape((size, 128))]
    else:
        results += [shape((count, 512, D)), shape((count, 8, 128), F32)]
    scratch = []
    if fetched:
        scratch = [
            pltpu.VMEM((count, 2, 2, SEG, KEYS), LOW),
            pltpu.VMEM((count, 2, KEYS, 256), LOW),
            pltpu.VMEM((count, 2, SEG, 256), LOW),
            pltpu.VMEM((count, SPAN, 128), LOW),
            pltpu.VMEM((count, 2, SEG, 128), F32),
            pltpu.VMEM((count, 2, SEG, 128), F32),
            pltpu.VMEM((count, 2, SEG, 128), F32),
            pltpu.VMEM((2, KEYS, D), LOW),
            pltpu.VMEM((SPAN, D), LOW),
            pltpu.SemaphoreType.DMA((20 * count,)),
        ]
    scratch += [
        pltpu.VMEM((2, 2, SEG, KEYS), LOW),
        pltpu.VMEM((2, 2, SEG, KEYS), LOW),
        pltpu.VMEM((128, KEYS), F32),
        pltpu.VMEM((2, 256, KEYS), LOW),
        pltpu.VMEM((total, 512, D), LOW),
        pltpu.VMEM((total, 8, 128), F32),
    ]
    if size:
        scratch.append(pltpu.VMEM((2 * HALF_BLOCKS, ROWS, 128), LOW))
    place = far if fetched else near
    return pl.pallas_call(
        functools.partial(
            back_kernel, pairs=pairs, calls=max(0, len(extra) // 2 - 1), fetched=fetched
        ),
        out_shape=tuple(results),
        in_specs=[far_spec() if fetched else whole_spec()] * 9
        + ([scalar_spec()] + [whole_spec()] * (len(extra) - 1) if size else []),
        out_specs=(whole_spec(),) * 3,
        scratch_shapes=scratch,
        compiler_params=params(LESS_BYTES),
        cost_estimate=cost(1.5e10 * count, 8e6),
        name=f"attend_back_{pairs[0]}",
    )(*(place(a) for a in operands), *extra)


def input_gradient(first_grad, tokens, wq, wkv):
    operands = [
        pltpu.with_memory_space_constraint(a, pltpu.HBM) for a in (first_grad, wq, wkv, *tokens)
    ]
    return pl.pallas_call(
        functools.partial(input_kernel, count=len(operands)),
        out_shape=shape((2, SEG, D), F32),
        in_specs=[far_spec()] * len(operands),
        out_specs=far_spec(),
        scratch_shapes=[pltpu.VMEM(a.shape, a.dtype) for a in operands]
        + [pltpu.VMEM((2, SEG, D), F32), pltpu.SemaphoreType.DMA((len(operands) + 2,))],
        compiler_params=params(LESS_BYTES),
        cost_estimate=cost(1.6e9, 6e6),
        name="input_gradient",
    )(*operands)


def unpack_attention(places, pieces, rest, dp_size):
    total = sum(p.shape[0] for p in pieces)
    return pl.pallas_call(
        functools.partial(unpack_attention_kernel, per_side=dp_size // 2),
        out_shape=(shape((D, D), F32),) * 5 + (shape((1, D), F32),) * 7,
        in_specs=[scalar_spec()] + [whole_spec()] * 5,
        out_specs=(whole_spec(),) * 12,
        scratch_shapes=[pltpu.VMEM((total, 128), LOW)],
        compiler_params=params(LESS_BYTES),
        cost_estimate=cost(5e8, 6e6),
        name="unpack_attention",
    )(places, *pieces, rest)


def unpack_ffn(places, pieces, units, dp_size):
    total = sum(p.shape[0] for p in pieces)
    return pl.pallas_call(
        functools.partial(unpack_ffn_kernel, per_side=dp_size // 2),
        out_shape=(
            shape((D, units), F32), shape((1, units), F32), shape((D, units), F32),
            shape((ROWS, 128)),
        ),
        in_specs=[scalar_spec()] + [whole_spec()] * 2,
        out_specs=(whole_spec(),) * 4,
        scratch_shapes=[pltpu.VMEM((total, 128), LOW)],
        compiler_params=params(LESS_BYTES),
        cost_estimate=cost(5e8, 6e6),
        name="unpack_ffn",
    )(places, *pieces)


def swap(values):
    return lax.ppermute(values, "tp", [(0, 1), (1, 0)])


def orders_of(dp_size):
    bits = list(range(dp_size.bit_length() - 1))
    turned = list(bits)
    for k in range(0, len(bits) - 1, 2):
        turned[k], turned[k + 1] = bits[k + 1], bits[k]
    return bits, turned


class Ring:
    def __init__(self, dp_size, index, core):
        self.size, self.orders = dp_size, orders_of(dp_size)
        self.steps = len(self.orders[0])
        self.bits = [
            jnp.where(core == 0, (index >> a) & 1, (index >> b) & 1)
            for a, b in zip(*self.orders)
        ]

    def place(self, index, order):
        spot = 0
        for k in self.orders[order]:
            spot = 2 * spot + ((index >> k) & 1)
        return spot

    def send(self, values, step):
        pairs = []
        for i in range(self.size):
            for c in range(2):
                pairs.append((2 * i + c, 2 * (i ^ (1 << self.orders[c][step])) + c))
        return lax.ppermute(values, ("dp", "tp"), pairs)

    def sides(self, keep, came, step):
        rows = keep.shape[0] // 2
        bit = self.bits[step]

        def side(which):
            start = which * rows
            return lax.dynamic_slice_in_dim(keep, start, rows, 0) + lax.dynamic_slice_in_dim(
                came, start, rows, 0
            )

        return side(1 - bit), side(bit)


def after(value, *others):
    return lax.optimization_barrier((value,) + others)


def rounded_rows(rows, unit):
    return -(-rows // unit) * unit


def make_shards(dp_size):
    table = position_table()

    def shards(
        hidden, memory, segment_length, memory_length, doc_reset, w_query, w_key, w_value, w_pos,
        bias_u, bias_v, w_out, first_gain, first_shift, ffn_in, ffn_in_bias, ffn_out, ffn_out_bias,
        second_gain, second_shift, out_grad,
    ):
        core = lax.axis_index("tp")
        index = lax.axis_index("dp")
        place = core[None].astype(jnp.int32)
        units = ffn_in.shape[1]
        pos_table = jnp.asarray(table)

        def by_feature(values):
            return values.transpose(2, 0, 1).reshape(-1, values.shape[1])

        hidden_t, memory_t, out_grad_t = (by_feature(a) for a in (hidden, memory, out_grad))
        hidden_in, memory_in, out_grad_in = swap(hidden_t), swap(memory_t), swap(out_grad_t)
        own_ffn = (ffn_in, ffn_in_bias[None], ffn_out.T)
        other_ffn = tuple(swap(a) for a in own_ffn)

        wq, wkv, rel, wo, bias = prepare(
            w_query, w_key, w_value, w_pos, w_out, bias_u, bias_v, pos_table
        )
        full = units // 128
        unit = 16 * dp_size
        (
            probs, kv, uv, att, inv, joined, act, first_grad, ga, ffn_own, ffn_other, out_blocks
        ) = layer(
            place, segment_length, memory_length, (hidden_t, memory_t, hidden_in, memory_in),
            doc_reset, wq, wkv, rel, bias, wo, (out_grad_t, out_grad_in), own_ffn, other_ffn,
            tuple(v[None] for v in (first_gain, first_shift, ffn_out_bias, second_gain, second_shift)),
            rounded_rows(ROWS * (2 * full + 1), unit),
        )
        ring = Ring(dp_size, index, core)
        straight, turned = ring.place(index, 0), ring.place(index, 1)
        places = jnp.stack(
            [
                jnp.where(core == 0, straight, turned),
                jnp.where(core == 0, turned, straight),
                core,
            ]
        ).astype(jnp.int32)

        def give_back(values, dtype):
            rows = values.shape[1] // 2
            mine = lax.dynamic_slice_in_dim(values, core * rows, rows, 1)
            theirs = lax.dynamic_slice_in_dim(values, (1 - core) * rows, rows, 1)
            came = swap(theirs.astype(LOW)).astype(dtype)
            mine = mine.astype(dtype)
            whole = jnp.where(
                core == 0,
                jnp.concatenate([mine, came], axis=0),
                jnp.concatenate([came, mine], axis=0),
            )
            return with_layout_constraint(whole, Layout(major_to_minor=(2, 0, 1)))

        def kept_memory(hidden):
            rows = hidden.shape[1]
            positions = core * rows + jnp.arange(rows)
            later = (jnp.arange(SEG)[:, None] > positions[None, :]).astype(LOW)
            resets = jnp.dot(doc_reset.astype(LOW), later, preferred_element_type=F32)
            keep = (resets == 0.0) & (positions[None, :] < segment_length[:, None])
            by_feature = hidden.transpose(2, 0, 1)
            return jnp.where(keep[None], by_feature, jnp.zeros_like(by_feature))

        steps = ring.steps
        slots = [[(0,)], [(1, 2, 3)], [(4,)]]
        operands = [probs, kv, uv, rel, ga, att, inv, joined, pos_table]
        tokens, wides, biases = [], [], []

        def back_slot(waited, slot):
            packed = None
            for pairs in slot:
                last = pairs[-1] == PAIRS - 1
                result = attend_back(
                    pairs,
                    operands,
                    (place, out_blocks, *wides, *biases) if last else (),
                    rounded_rows(ROWS * HALF_BLOCKS, unit) if last else 0,
                    fetched=not pairs[0],
                )
                waited, *result = after(waited, *result)
                tokens.append(result[0])
                operands[4], _ = after(operands[4], result[0])
                if last:
                    packed = result[1:]
                else:
                    wides.append(result[1])
                    biases.append(result[2])
            return waited, packed

        keep, came = ffn_own, swap(ffn_other)
        came, _ = back_slot(came, slots[0])
        first_steps = len(slots) - 1
        for step in range(first_steps):
            sent, kept = ring.sides(keep, came, step)
            sent, kept, operands[4] = after(sent, kept, operands[4])
            keep, came = kept, ring.send(sent, step)
            came, packed = back_slot(came, slots[step + 1])
        att_keep, att_send = packed
        att_came = swap(att_send)
        places, att_came = after(places, att_came)
        ffn = {"keep": keep, "came": came}

        def ffn_hop(kind, step, *others):
            ffn["keep"], ffn["came"], *_ = after(ffn["keep"], ffn["came"], *others)
            if kind == "scatter":
                sent, ffn["keep"] = ring.sides(ffn["keep"], ffn["came"], step)
            elif step == steps - 1:
                sent = ffn["keep"] = ffn["keep"] + ffn["came"]
            else:
                sent = ffn["keep"] = jnp.concatenate([ffn["keep"], ffn["came"]], axis=0)
            ffn["came"] = ring.send(sent, step)
            return sent

        hops = [("scatter", k) for k in range(first_steps, steps)]
        hops += [("gather", k) for k in range(steps - 1, -1, -1)]
        sent = ffn_hop(*hops.pop(0))
        att_keep, _ = after(att_keep, sent)
        for step in range(steps):
            sent, kept = ring.sides(att_keep, att_came, step)
            att_keep, att_came = kept, ring.send(sent, step)
            if len(hops) > 1:
                ffn_hop(*hops.pop(0), sent)
            if step == 0:
                first_grad, att_keep = after(first_grad, att_keep)
                input_own = input_gradient(first_grad, tokens, wq, wkv)
                att_came, input_own = after(att_came, input_own)
            elif step == 3:
                act, late_hidden, att_keep = after(act, hidden, att_keep)
                activations, new_memory = give_back(act, LOW), kept_memory(late_hidden)
                att_came, activations, new_memory = after(att_came, activations, new_memory)
        summed = att_keep + att_came
        for hop in hops:
            ffn_hop(*hop, summed)
        ffn_pieces = (ffn["keep"], ffn["came"])
        values = summed
        for step in range(steps - 1, 0, -1):
            came = ring.send(values, step)
            if step == steps - 1:
                input_own, values = after(input_own, values)
                input_grad = give_back(input_own, F32)
                came, input_grad = after(came, input_grad)
            values = jnp.concatenate([values, came], axis=0)
        came = ring.send(values, 0)
        near = swap(values)
        filled = list(unpack_ffn(places, ffn_pieces, units, dp_size))
        filled[1] = filled[1].reshape(-1)
        came, near, *filled = after(came, near, *filled)
        grad_in, grad_in_bias, grad_ffn_out_t, rest = filled
        g_query, g_key, g_value, g_pos, g_out, *vectors = unpack_attention(
            places, (values, came, near, swap(came)), rest, dp_size
        )
        g_bias_u, g_bias_v, g_gain_1, g_shift_1, g_gain_2, g_shift_2, g_ffn_bias = (
            v[0] for v in vectors
        )

        def by_token(values):
            return values.transpose(1, 2, 0)

        return (
            by_token(new_memory), activations, input_grad,
            g_query, g_key, g_value, g_pos, g_bias_u, g_bias_v, g_out, g_gain_1, g_shift_1,
            grad_in, grad_in_bias, grad_ffn_out_t.T, g_ffn_bias, g_gain_2, g_shift_2,
        )

    return shards


def solution(mesh):
    rows, copied = P("dp", "tp", None), P()
    shards = make_shards(mesh.shape["dp"])
    return jax.shard_map(
        shards,
        mesh=mesh,
        in_specs=(
            rows, rows, P("dp"), P("dp"), P("dp", None),
            copied, copied, copied, copied, copied, copied, copied, copied, copied,
            P(None, "tp"), P("tp"), P("tp", None),
            copied, copied, copied, rows,
        ),
        out_specs=(
            rows, rows, rows, copied, copied, copied, copied, copied, copied, copied, copied, copied,
            P(None, "tp"), P("tp"), P("tp", None), copied, copied, copied,
        ),
        check_vma=False,
    )
```

```python
import functools
import math

import jax
import jax.numpy as jnp
import ml_dtypes
import numpy as np
from jax import lax
from jax.experimental import pallas as pl
from jax.experimental.layout import Layout, with_layout_constraint
from jax.experimental.pallas import tpu as pltpu
from jax.sharding import PartitionSpec as P

D = 410
HEADS = 10
DHEAD = 41
SEG = 256
MEM = 256
KEYS = MEM + SEG
HALF = 128
PAIRS = HEADS // 2
WIDE = PAIRS * 128
ROWS = 416
SPAN = 768
REST = 26
HALF_BLOCKS = 8
RECEIVED = (2, 3, 11, 13, 17)
EPSILON = 1e-05
NEG_LARGE = -1e30
FACTOR = 1.0 / math.sqrt(DHEAD)
LOG2E = 1.0 / math.log(2.0)
LOW = jnp.bfloat16
VMEM_BYTES = 60 * 1024 * 1024
LAYER_BYTES = 54 * 1024 * 1024
LESS_BYTES = 15 * 1024 * 1024
F32 = jnp.float32


def position_table():
    distance = (KEYS - 1 - np.arange(SPAN)).astype(np.float32)
    inverse = np.float32(1.0) / np.float32(10000.0) ** (
        np.arange(0, D, 2).astype(np.float32) / np.float32(D)
    )
    angles = distance[:, None] * inverse[None, :].astype(np.float32)
    table = np.concatenate([np.sin(angles), np.cos(angles)], axis=1)
    return table.astype(ml_dtypes.bfloat16)


def mm(left, right):
    return lax.dot_general(left, right, (((1,), (0,)), ((), ())), preferred_element_type=F32)


def mm_nt(left, right):
    return lax.dot_general(left, right, (((1,), (1,)), ((), ())), preferred_element_type=F32)


def expander(rows):
    row = lax.broadcasted_iota(jnp.int32, (rows, WIDE), 0)
    lane = lax.broadcasted_iota(jnp.int32, (rows, WIDE), 1)
    inside = lane & 63
    hit = (inside < DHEAD) & (row == (lane >> 6) * DHEAD + inside)
    return jnp.where(hit, 1.0, 0.0).astype(LOW)


def compressor():
    row = lax.broadcasted_iota(jnp.int32, (WIDE, D), 0)
    lane = lax.broadcasted_iota(jnp.int32, (WIDE, D), 1)
    inside = row & 63
    hit = (inside < DHEAD) & (lane == (row >> 6) * DHEAD + inside)
    return jnp.where(hit, 1.0, 0.0).astype(LOW)


def identity(size):
    row = lax.broadcasted_iota(jnp.int32, (size, size), 0)
    lane = lax.broadcasted_iota(jnp.int32, (size, size), 1)
    return jnp.where(row == lane, 1.0, 0.0).astype(LOW)


def reversal(size):
    row = lax.broadcasted_iota(jnp.int32, (size, size), 0)
    lane = lax.broadcasted_iota(jnp.int32, (size, size), 1)
    return jnp.where(row + lane == size - 1, 1.0, 0.0).astype(LOW)


class Mover:
    def __init__(self, sems):
        self.sems, self.used, self.open = sems, 0, []

    def start(self, source, target):
        copy = pltpu.make_async_copy(source, target, self.sems.at[self.used])
        self.used += 1
        copy.start()
        self.open.append(copy)
        return copy

    def finish(self):
        for copy in self.open:
            copy.wait()
        self.open = []

    def wait(self, *copies):
        for copy in copies:
            copy.wait()
        self.open = [c for c in self.open if all(c is not d for d in copies)]


def prep_kernel(
    wq_in, wk_in, wv_in, wp_in, wo_in, bias_u_in, bias_v_in, pos_in, q_out, kv_out, rel_out, wo_out,
    bias_out, wq, wk, wv, wp, wo, bias_u, bias_v, pos, o_q, o_kv, o_rel, o_wo, o_bias, sems
):
    mover = Mover(sems)
    loads = [
        mover.start(a, b)
        for a, b in zip(
            (wp_in, pos_in, wk_in, wv_in, wq_in, wo_in, bias_u_in, bias_v_in),
            (wp, pos, wk, wv, wq, wo, bias_u, bias_v),
        )
    ]
    expand = expander(D)
    mover.wait(*loads[:2])
    rel = mm(pos[...], mm(wp[...], expand).astype(LOW)).astype(LOW)
    for p in range(PAIRS):
        o_rel[p] = rel[:, 128 * p : 128 * p + 128]
    mover.start(o_rel, rel_out)
    mover.wait(*loads[2:4])
    k_wide = mm(wk[...], expand).astype(LOW)
    v_wide = mm(wv[...], expand).astype(LOW)
    for p in range(PAIRS):
        o_kv[p, :, :128] = k_wide[:, 128 * p : 128 * p + 128]
        o_kv[p, :, 128:] = v_wide[:, 128 * p : 128 * p + 128]
    mover.start(o_kv, kv_out)
    mover.wait(*loads[4:])
    q_wide = mm(wq[...], expand).astype(LOW)
    for p in range(PAIRS):
        o_q[p] = q_wide[:, 128 * p : 128 * p + 128]
    mover.start(o_q, q_out)
    o_wo[...] = mm(compressor(), wo[...]).astype(LOW)
    mover.start(o_wo, wo_out)
    parts = []
    for bias in (bias_u, bias_v):
        rest = bias[...]
        for _ in range(3):
            parts.append(rest.astype(LOW).astype(F32))
            rest = rest - parts[-1]
    wide = mm(jnp.concatenate(parts + [jnp.zeros((2, D), F32)], axis=0).astype(LOW), expand)
    for k in range(2):
        row = jnp.broadcast_to(wide[3 * k : 3 * k + 1] + wide[3 * k + 1 : 3 * k + 2], (8, WIDE))
        row = row + wide[3 * k + 2 : 3 * k + 3]
        for p in range(PAIRS):
            o_bias[p, k] = row[:, 128 * p : 128 * p + 128]
    mover.start(o_bias, bias_out)
    mover.finish()


def spread_streams(source, raw, core, unit, store):
    raw[...] = source[...].astype(F32)
    for s in range(2):
        columns = raw[pl.ds(2 * core + s, D, stride=4), :].astype(LOW)
        store(s, mm_nt(unit, columns).astype(LOW))


def layer_kernel(
    place, seg_len, mem_len, hidden_hbm, memory_hbm, hidden_in_hbm, memory_in_hbm, reset_hbm,
    wq_hbm, wkv_hbm, rel_hbm, bias_hbm, wo_hbm, out_grad_hbm, out_grad_in_hbm,
    win_a_hbm, win_b_hbm, bin_a_hbm, bin_b_hbm, wout_a_hbm, wout_b_hbm,
    gain_1_hbm, shift_1_hbm, bias_out_hbm, gain_2_hbm, shift_2_hbm,
    probs_out, kv_out, uv_out, att_out, inv_out, joined_out,
    act_out, first_out, ga_out, own_out, other_out, blocks_out,
    hidden, memory, hidden_in, memory_in, reset, wq, wkv, rel, bias, wo, out_grad, out_grad_in,
    win_a, win_b, bin_a, bin_b, wout_a, wout_b, gain_1, shift_1, bias_out, gain_2, shift_2,
    o_probs, o_kv, o_uv, o_att, o_inv, o_joined, o_act, o_first, o_ga, o_own, o_other, o_out,
    raw, mask, og, low_in, gb_all, gs_all, active, inner, vecs, att, slopes, sems, step_sems
):
    mover = Mover(sems)
    loads = [
        mover.start(a, b)
        for a, b in zip(
            (
                memory_hbm, memory_in_hbm, hidden_hbm, hidden_in_hbm, reset_hbm,
                wkv_hbm, wq_hbm, bias_hbm, rel_hbm,
                gain_1_hbm, shift_1_hbm, bias_out_hbm, gain_2_hbm, shift_2_hbm, bin_a_hbm,
                bin_b_hbm, wo_hbm, out_grad_hbm, out_grad_in_hbm,
                win_a_hbm, wout_a_hbm, win_b_hbm, wout_b_hbm,
            ),
            (
                memory, memory_in, hidden, hidden_in, reset, wkv, wq, bias, rel,
                gain_1, shift_1, bias_out, gain_2, shift_2, bin_a,
                bin_b, wo, out_grad, out_grad_in, win_a, wout_a, win_b, wout_b,
            ),
        )
    ]
    core = place[0]
    mine = pl.multiple_of(HALF * core, HALF)
    other = pl.multiple_of(HALF * (1 - core), HALF)
    unit = identity(HALF)
    row = lax.broadcasted_iota(jnp.int32, (SEG, SEG), 0)
    lane = lax.broadcasted_iota(jnp.int32, (SEG, SEG), 1)
    lower = jnp.where(row >= lane, 1.0, 0.0).astype(LOW)
    for index, (source, base) in enumerate(
        ((memory, mine), (memory_in, other), (hidden, MEM + mine), (hidden_in, MEM + other))
    ):

        def store(s, values, base=base):
            o_joined[s, pl.ds(pl.multiple_of(base, HALF), HALF)] = values

        mover.wait(loads[index])
        spread_streams(source, raw.at[index], core, unit, store)
    mover.wait(*loads[4:9])
    mover.start(o_joined, joined_out)
    for s in range(2):
        own = 2 * core + s
        starts = jnp.broadcast_to(reset[pl.ds(own, 1), :].astype(F32), (8, SEG)).astype(LOW)
        doc_column = mm_nt(lower, starts)[:, :1]
        doc_row = mm_nt(starts, lower)[:1, :]
        memory_ok = (lane >= MEM - mem_len[own]) & (doc_column == 0.0)
        segment_ok = ((row > lane) & (doc_row == doc_column) & (lane < seg_len[own])) | (row == lane)
        mask[s, :, :MEM] = jnp.where(memory_ok, 0.0, NEG_LARGE)
        mask[s, :, MEM:] = jnp.where(segment_ok, 0.0, NEG_LARGE)
    first_head = lax.broadcasted_iota(jnp.int32, (HALF, 128), 1) < 64
    zero = jnp.zeros((HALF, 128), LOW)
    ones_lane = (lax.broadcasted_iota(jnp.int32, (KEYS, 256), 1) & 190) == 190

    for p in range(PAIRS):
        for s in range(2):
            pair_rows = jnp.where(ones_lane, 1.0, mm(o_joined[s], wkv[p])).astype(LOW)
            o_kv[p, s] = pair_rows
            queries = mm(o_joined[s, MEM:], wq[p])
            o_uv[p, s, :, :128] = (queries + bias[p, 0, :1]).astype(LOW)
            o_uv[p, s, :, 128:] = (queries + bias[p, 1, :1]).astype(LOW)

    def stacked(values):
        return jnp.concatenate(
            [jnp.where(first_head, values, zero), jnp.where(first_head, zero, values)], axis=0
        )

    def score(p, s, b):
        count = KEYS if b else KEYS - HALF
        rows = slice(HALF * b, HALF * b + HALF)
        start_row = HALF - HALF * b
        content = mm_nt(stacked(o_uv[p, s, rows, :128]), o_kv[p, s, :count, :128])
        relative = mm_nt(stacked(o_uv[p, s, rows, 128:]), rel[p, start_row : start_row + count])
        spots = mask[s, rows, :count]
        scores = []
        for h in range(2):
            part = slice(HALF * h, HALF * h + HALF)
            turned = pltpu.roll(relative[part], count - HALF + 1, 1, stride=1, stride_axis=0)
            scores.append((content[part] + turned) * (FACTOR * LOG2E) + spots)
        return scores

    def soften(p, s, b, scores):
        count = KEYS if b else KEYS - HALF
        rows = slice(HALF * b, HALF * b + HALF)
        exp_terms = []
        for h in range(2):
            top = jnp.max(scores[h], axis=1, keepdims=True)
            exp_terms.append(jnp.exp2(scores[h] - top).astype(LOW))
            o_probs[p, s, h, rows, :count] = exp_terms[h]
            if b == 0:
                o_probs[p, s, h, rows, count:] = jnp.zeros((HALF, HALF), LOW)
        return jnp.concatenate(exp_terms, axis=0)

    def mix(p, s, b, exp_terms):
        lanes = pl.ds(pl.multiple_of(128 * p, 128), 128)
        count = KEYS if b else KEYS - HALF
        rows = slice(HALF * b, HALF * b + HALF)
        mixed = mm(exp_terms, o_kv[p, s, :count, 128:])
        inverse = jnp.where(first_head, 1.0 / mixed[:HALF, 63:64], 1.0 / mixed[HALF:, 127:])
        o_inv[s, rows, lanes] = inverse
        o_att[s, rows, lanes] = jnp.where(first_head, mixed[:HALF], mixed[HALF:]) * inverse

    def step(p, carry):
        blocks = [(s, b) for s in range(2) for b in range(2)]
        scores, mixing = score(p, *blocks[0]), None
        for k, block in enumerate(blocks):
            following = score(p, *blocks[k + 1]) if k + 1 < len(blocks) else None
            exp_terms = soften(p, *block, scores)
            if mixing is not None:
                mix(p, *mixing)
            mixing, scores = (*block, exp_terms), following
        mix(p, *mixing)
        for s in range(2):
            for copy in step_copies(p, s):
                copy.start()
        return carry

    def step_copies(p, s):
        return [
            pltpu.make_async_copy(a.at[p, s], b.at[p, s], step_sems.at[k, p, s])
            for k, (a, b) in enumerate(((o_probs, probs_out), (o_kv, kv_out), (o_uv, uv_out)))
        ]

    lax.fori_loop(0, PAIRS, step, 0)
    mover.start(o_att, att_out)
    mover.start(o_inv, inv_out)
    hidden_units = win_a.shape[1]
    chunks = [(a, min(a + 256, hidden_units)) for a in range(0, hidden_units, 256)]
    halves = ((win_a, bin_a, wout_a), (win_b, bin_b, wout_b))
    low_in[:, 384:] = jnp.where(
        lax.broadcasted_iota(jnp.int32, (2 * SEG, 128), 1) == D - 384, 1.0, 0.0
    ).astype(LOW)
    gs_all[:, 384:] = jnp.zeros((2 * SEG, 128), LOW)
    vecs[...] = jnp.zeros_like(vecs)
    att[...] = o_att[...].astype(LOW)
    mover.wait(*loads[9:])
    for index, (source, base) in enumerate(((out_grad, mine), (out_grad_in, other))):

        def store_grad(s, values, base=base):
            og[s, pl.ds(base, HALF)] = values

        spread_streams(source, raw.at[index], core, unit, store_grad)
    tokens = 2 * SEG
    hid = o_joined[:, MEM:].reshape(tokens, D).astype(F32)
    hat_1, scale_1 = norm_forward(hid + mm(att[...].reshape(tokens, WIDE), wo[...]))
    first = hat_1 * gain_1[...] + shift_1[...]
    first_low = first.astype(LOW)
    low_in[:, :D] = first_low
    ffn_sum = first + bias_out[...]
    for which, (win, b_in, wout) in enumerate(halves):
        for a, z in chunks:
            pre = mm(first_low, win[:, a:z]) + b_in[:, a:z].astype(F32)
            act, slope = gelu_both(pre)
            act = act.astype(LOW)
            slopes[which, :, a:z] = slope
            active[which, :, a:z] = act
            ffn_sum = ffn_sum + mm_nt(act, wout[:, a:z])
    hat_2, scale_2 = norm_forward(ffn_sum)
    o_act[...] = (hat_2 * gain_2[...] + shift_2[...]).astype(LOW).reshape(2, SEG, D)
    cot = og[...].reshape(tokens, D).astype(F32)
    vecs[2:3] = total_rows(cot * hat_2)
    vecs[3:4] = total_rows(cot)
    grad_second = norm_backward(cot * gain_2[...], hat_2, scale_2)
    vecs[4:5] = total_rows(grad_second)
    gs_low = grad_second.astype(LOW)
    gs_all[:, :D] = gs_low
    grad_first = grad_second
    for which, (win, b_in, wout) in enumerate(halves):
        for a, z in chunks:
            grad_inner = (mm(gs_low, wout[:, a:z]) * slopes[which, :, a:z]).astype(LOW)
            inner[which, :, a:z] = grad_inner
            grad_first = grad_first + mm_nt(grad_inner, win[:, a:z])
    vecs[0:1] = total_rows(grad_first * hat_1)
    vecs[1:2] = total_rows(grad_first)
    grad_pre = norm_backward(grad_first * gain_1[...], hat_1, scale_1)
    o_first[...] = grad_pre.reshape(2, SEG, D)
    grad_branch = grad_pre.astype(LOW)
    gb_all[...] = grad_branch
    o_ga[...] = mm_nt(grad_branch, wo[...]).reshape(2, SEG, WIDE)
    mover.start(o_act, act_out)
    mover.start(o_first, first_out)
    mover.start(o_ga, ga_out)
    grad_out = None
    for s in range(2):
        part = mm(att[s].T, gb_all[SEG * s : SEG * s + SEG])
        grad_out = part if grad_out is None else grad_out + part
    grad_out = mm(expander(ROWS), grad_out.astype(LOW))
    grad_out = (grad_out + mm(pick_rows(8), vecs[...].astype(LOW))).astype(LOW)
    for block in range(3):
        o_out[block] = grad_out[:, 128 * block : 128 * block + 128]
    mover.start(o_out, blocks_out)
    out_rest = mm(grad_out[:, 384:], placer(REST, 2 * REST))
    in_t = low_in[...].T[:ROWS]
    gs_t = gs_all[...].T[:ROWS]
    full = hidden_units // 128
    for which, pack, target in ((1, o_other, other_out), (0, o_own, own_out)):
        rest = out_rest
        for m, (left, right) in enumerate(((in_t, inner), (gs_t, active))):
            for a, z in chunks:
                grads = mm(left, right[which, :, a:z]).astype(LOW)
                for block in range(a // 128, min(-(-z // 128), full)):
                    part = grads[:, 128 * block - a : 128 * block - a + 128]
                    put(pack, ROWS * (full * m + block), part)
                if z > 128 * full:
                    rest = rest + mm(grads[:, 128 * full - a :], placer(REST, m * REST))
            span = pl.ds(ROWS * full * m, ROWS * full)
            mover.start(pack.at[span], target.at[span])
        put(pack, ROWS * 2 * full, rest.astype(LOW))
        span = pl.ds(ROWS * 2 * full, pack.shape[0] - ROWS * 2 * full)
        mover.start(pack.at[span], target.at[span])
    for p in range(PAIRS):
        for s in range(2):
            for copy in step_copies(p, s):
                copy.wait()
    mover.finish()


def norm_forward(values):
    centred = values - jnp.mean(values, axis=1, keepdims=True)
    scale = lax.rsqrt(jnp.mean(centred * centred, axis=1, keepdims=True) + EPSILON)
    return centred * scale, scale


def norm_backward(grad, x_hat, scale):
    return scale * (
        grad
        - jnp.mean(grad, axis=1, keepdims=True)
        - x_hat * jnp.mean(grad * x_hat, axis=1, keepdims=True)
    )


GELU_A = math.sqrt(2.0 / math.pi)
GELU_B = 0.044715


def gelu_both(x):
    square = x * x
    bent = jnp.tanh(x * (GELU_A + (GELU_A * GELU_B) * square))
    half_up = 0.5 + 0.5 * bent
    slope = half_up + (0.5 * x) * (1.0 - bent * bent) * (GELU_A + (3.0 * GELU_A * GELU_B) * square)
    return x * half_up, slope


def total_rows(values):
    return jnp.sum(values, axis=0, keepdims=True)


def placer(count, offset):
    row = lax.broadcasted_iota(jnp.int32, (count, 128), 0)
    lane = lax.broadcasted_iota(jnp.int32, (count, 128), 1)
    return jnp.where(lane == row + offset, 1.0, 0.0).astype(LOW)


def put(ref, start, values):
    ref[start : start + values.shape[0]] = values


def pick_rows(count):
    row = lax.broadcasted_iota(jnp.int32, (ROWS, count), 0)
    lane = lax.broadcasted_iota(jnp.int32, (ROWS, count), 1)
    return jnp.where(row == D + lane, 1.0, 0.0).astype(LOW)


def back_kernel(*refs, pairs, calls, fetched):
    refs = list(refs)

    def take(count):
        part = refs[:count]
        del refs[:count]
        return part

    sources = take(9)
    earlier = take(2 + 2 * calls) if calls else []
    outs = take(3)
    o_token = outs[0]
    loads = [([], []) for _ in pairs]
    if fetched:
        probs_hbm, kv_hbm, uv_hbm, rel_hbm, ga_hbm, att_hbm, inv_hbm, joined_hbm, pos_hbm = sources
        probs, kv, uv, rel, ga, att, inv, joined, pos = take(9)
        mover = Mover(take(1)[0])
        for n, pair in enumerate(pairs):
            lanes = slice(128 * pair, 128 * pair + 128)
            for s in range(2):
                for source, target in ((ga_hbm, ga), (att_hbm, att), (inv_hbm, inv)):
                    loads[n][s].append(mover.start(source.at[s, :, lanes], target.at[n, s]))
                for source, target in ((uv_hbm, uv), (kv_hbm, kv), (probs_hbm, probs)):
                    loads[n][s].append(mover.start(source.at[pair, s], target.at[n, s]))
                if s == 0:
                    loads[n][s].append(mover.start(rel_hbm.at[pair], rel.at[n]))
                if n == 0:
                    loads[n][s].append(mover.start(joined_hbm.at[s], joined.at[s]))
        loads[0][1].append(mover.start(pos_hbm, pos))
    else:
        probs, kv, uv, rel, ga, att, inv, joined, pos = sources
    scores, spread, grel, dkv, wide, sums = take(6)
    base = 0
    if calls:
        (whole,) = take(1)
        for source, tops in zip(earlier[2 : 2 + calls], earlier[2 + calls :]):
            count = source.shape[0]
            wide[base : base + count] = source[...]
            sums[base : base + count] = tops[...]
            base += count
    flip = reversal(HALF)
    first_head = lax.broadcasted_iota(jnp.int32, (HALF, 128), 1) < 64
    zero = jnp.zeros((HALF, 128), LOW)
    lane = lax.broadcasted_iota(jnp.int32, (SEG, 128), 1)
    into = lax.broadcasted_iota(jnp.int32, (128, 128), 0)
    out = lax.broadcasted_iota(jnp.int32, (128, 128), 1)
    head_sum = jnp.where(((out & 62) == 62) & ((into >> 6) == (out >> 6)), 1.0, 0.0).astype(LOW)
    for n, pair in enumerate(pairs):
        here = n if fetched else pair
        lanes = slice(128 * pair, 128 * pair + 128)

        def columns(values, s, n=n, lanes=lanes):
            return values[n, s] if fetched else values[s, :, lanes]

        grad_atts, u_ts, ga_ts = [], [], []
        for s in range(2):
            if fetched:
                mover.wait(*loads[n][s])
            wide_grad = columns(ga, s)
            inverse = columns(inv, s)
            inner = wide_grad * columns(att, s)
            inner_high = inner.astype(LOW)
            inner_low = (inner - inner_high.astype(F32)).astype(LOW)
            row_sums = (mm(inner_high, head_sum) + mm(inner_low, head_sum)) * inverse
            sums_high = row_sums.astype(LOW).astype(F32)
            grad_atts.append(
                jnp.where(
                    (lane & 63) == 62,
                    -sums_high,
                    jnp.where((lane & 63) == 63, sums_high - row_sums, wide_grad * inverse),
                ).astype(LOW)
            )
            u_ts.append(uv[here, s, :, :128].T)
            ga_ts.append(grad_atts[s].T)
        v_ts = [
            jnp.concatenate(
                [
                    mm(flip, uv[here, s, HALF * b : HALF * b + HALF, 128:]).astype(LOW).T
                    for s in range(2)
                ],
                axis=1,
            )
            for b in range(2)
        ]

        def differentiate(s, b):
            count = KEYS if b else KEYS - HALF
            part = grad_atts[s][HALF * b : HALF * b + HALF]
            both = jnp.concatenate(
                [jnp.where(first_head, part, zero), jnp.where(first_head, zero, part)], axis=0
            )
            return mm_nt(both, kv[here, s, :count, 128:])

        def spread_out(s, b, grad_probs):
            count = KEYS if b else KEYS - HALF
            rows = slice(HALF * b, HALF * b + HALF)
            for h in range(2):
                attn = probs[here, s, h, rows, :count].astype(F32)
                grad_scores = (attn * grad_probs[HALF * h : HALF * h + HALF]).astype(LOW)
                scores[s, h, rows, :count] = grad_scores
                if b == 0:
                    scores[s, h, rows, count:] = jnp.zeros((HALF, HALF), LOW)
                turned = pltpu.roll(mm(flip, grad_scores), 0, 1, stride=1, stride_axis=0)
                spread[b, h, HALF * s : HALF * s + HALF, :count] = turned.astype(LOW)

        def collect(s, b):
            count = KEYS if b else KEYS - HALF
            rows = slice(HALF * b, HALF * b + HALF)
            start_row = HALF - HALF * b

            def both(values):
                product = jnp.where(first_head, values[:HALF], values[HALF:])
                return product * FACTOR

            grad_u = both(
                mm(
                    jnp.concatenate([scores[s, h, rows, :count] for h in range(2)], axis=0),
                    kv[here, s, :count, :128],
                )
            )
            part = slice(HALF * s, HALF * s + HALF)
            grad_v = both(
                mm(
                    jnp.concatenate([spread[b, h, part, :count] for h in range(2)], axis=0),
                    rel[here, start_row : start_row + count],
                )
            )
            high = grad_v.astype(LOW)
            low = (grad_v - high.astype(F32)).astype(LOW)
            grad_q = (grad_u + (mm(flip, high) + mm(flip, low))).astype(LOW)
            o_token[n, s, rows, :128] = grad_q
            return total_rows(grad_u), total_rows(grad_v)

        parts = [(s, b) for s in range(2) for b in range(2)]
        grad_probs = differentiate(*parts[0])
        tops = []
        for k, part in enumerate(parts):
            following = differentiate(*parts[k + 1]) if k + 1 < len(parts) else None
            spread_out(*part, grad_probs)
            if k:
                tops.append(collect(*parts[k - 1]))
            grad_probs = following
        tops.append(collect(*parts[-1]))
        sum_u, sum_v = (sum(t[1:], t[0]) for t in zip(*tops))
        weight_kv, weight_q = None, None
        for s in range(2):
            for h in range(2):
                part = slice(64 * h, 64 * h + 64)
                dkv[s, part] = (mm(u_ts[s][part], scores[s, h]) * FACTOR).astype(LOW)
                dkv[s, 128 + 64 * h : 192 + 64 * h] = mm(ga_ts[s][part], probs[here, s, h]).astype(LOW)
            o_token[n, s, :, 128:] = dkv[s, :, MEM:].T
            part_kv = mm(dkv[s], joined[s])
            part_q = mm(o_token[n, s, :, :128].T, joined[s, MEM:])
            weight_kv = part_kv if weight_kv is None else weight_kv + part_kv
            weight_q = part_q if weight_q is None else weight_q + part_q
        for h in range(2):
            part = slice(64 * h, 64 * h + 64)
            first = mm(v_ts[0][part], spread[0, h, :, : KEYS - HALF])
            second = mm(v_ts[1][part], spread[1, h])
            grel[part, :HALF] = second[:, :HALF]
            grel[part, HALF:KEYS] = second[:, HALF:] + first
        spot = base + n
        wide[spot, :128] = weight_q.astype(LOW)
        wide[spot, 128:384] = weight_kv.astype(LOW)
        wide[spot, 384:] = mm((grel[...] * FACTOR).astype(LOW), pos[:KEYS]).astype(LOW)
        sums[spot] = jnp.concatenate([sum_u, sum_v, jnp.zeros((6, 128), F32)], axis=0)
    if calls:
        pack_attention(earlier[0], earlier[1], wide, sums, outs[1], outs[2], whole)
    else:
        outs[1][...] = wide[...]
        outs[2][...] = sums[...]


def pack_attention(place, out_blocks, wides, sums, keep, send, whole):
    core = place[0]
    pick = expander(ROWS)
    back = compressor()
    rest = jnp.zeros((ROWS, 128), F32)
    for m in range(4):
        total = None
        for p in range(PAIRS):
            part = mm(pick[:, 128 * p : 128 * p + 128], wides[p, 128 * m : 128 * m + 128])
            total = part if total is None else total + part
        if m == 0:
            vectors = None
            for p in range(PAIRS):
                part = mm(sums[p].astype(LOW), back[128 * p : 128 * p + 128])
                vectors = part if vectors is None else vectors + part
            total = total + mm(pick_rows(8), vectors.astype(LOW))
        total = total.astype(LOW)
        for block in range(3):
            whole[3 * m + block] = total[:, 128 * block : 128 * block + 128]
        rest = rest + mm(total[:, 384:], placer(REST, m * REST))
    whole[12] = rest.astype(LOW)
    for block in range(3):
        whole[13 + block] = out_blocks[block]
    half = whole.shape[0] // 2
    for block in range(half):
        keep[ROWS * block : ROWS * block + ROWS] = whole[core * half + block]
        send[ROWS * block : ROWS * block + ROWS] = whole[(1 - core) * half + block]
    if keep.shape[0] > half * ROWS:
        extra = keep.shape[0] - half * ROWS
        keep[half * ROWS :] = jnp.zeros((extra, 128), LOW)
        send[half * ROWS :] = jnp.zeros((extra, 128), LOW)


def input_kernel(*refs, count):
    sources, (result_hbm, *targets), (o_input, sems) = (
        refs[:count], refs[count : 2 * count + 1], refs[2 * count + 1 :]
    )
    mover = Mover(sems)
    loads = [mover.start(a, b) for a, b in zip(sources, targets)]
    first_grad, wq, wkv, *tokens = targets
    mover.wait(*loads[:3])
    total = [first_grad[s] for s in range(2)]
    p = 0
    for token, load in zip(tokens, loads[3:]):
        mover.wait(load)
        for n in range(token.shape[0]):
            weights = jnp.concatenate([wq[p], wkv[p]], axis=1)
            for s in range(2):
                total[s] = total[s] + mm_nt(token[n, s], weights)
            p += 1
    for s in range(2):
        o_input[s] = total[s]
        mover.start(o_input.at[s], result_hbm.at[s])
    mover.finish()


def gathered(where, target, base, pieces, per_side):
    size = pieces[0].shape[0] // per_side
    for side, ref in enumerate(pieces):

        def body(r, carry, side=side, ref=ref):
            spot = jnp.bitwise_xor(r + side * per_side, where)
            row = pl.multiple_of(base + spot * size, 16)
            target[pl.ds(row, size)] = ref[pl.ds(pl.multiple_of(r * size, 16), size)]
            return carry

        lax.fori_loop(0, per_side, body, 0)


def unpack_attention_kernel(
    places, a0, a1, b0, b1, o_rest, o_query, o_key, o_value, o_pos, o_out,
    o_bias_u, o_bias_v, o_gain_1, o_shift_1, o_gain_2, o_shift_2, o_ffn_bias, whole, *, per_side
):
    core = places[2]
    total = 2 * a0.shape[0]
    gathered(places[0], whole, core * total, (a0, a1), per_side)
    gathered(places[1], whole, (1 - core) * total, (b0, b1), per_side)
    half = HALF_BLOCKS

    def fetch(block):
        start = (block // half) * total + ROWS * (block % half)
        return whole[start : start + ROWS]

    def vectors(targets, rows, start):
        for k, ref in enumerate(targets):
            ref[:, start : start + rows.shape[1]] = rows[k : k + 1]

    norms = (o_gain_1, o_shift_1, o_gain_2, o_shift_2, o_ffn_bias)
    unit = identity(128)
    rest = fetch(12)
    for m, ref in enumerate((o_query, o_key, o_value, o_pos)):
        for block in range(3):
            part = fetch(3 * m + block)
            ref[128 * block : 128 * block + 128, :] = mm_nt(unit, part)[:, :D]
            if m == 0:
                vectors((o_bias_u, o_bias_v), part[400:].astype(F32)[10:], 128 * block)
        tail = mm_nt(placer(REST, m * REST), rest)
        ref[384:, :] = tail[:, :D]
        if m == 0:
            vectors((o_bias_u, o_bias_v), rest[400:, :REST].astype(F32)[10:], 384)
    for block in range(3):
        part = fetch(13 + block).astype(F32)
        o_out[:, 128 * block : 128 * block + 128] = part[:D]
        vectors(norms, part[D:], 128 * block)
    tail = mm_nt(o_rest[...], placer(REST, 2 * REST))
    o_out[:, 384:] = tail[:D]
    vectors(norms, tail[D:], 384)


def unpack_ffn_kernel(places, a0, a1, o_in, o_bias, o_out_t, o_rest, whole, *, per_side):
    gathered(places[0], whole, 0, (a0, a1), per_side)
    units = o_in.shape[1]
    full = units // 128
    for block in range(full):
        lanes = slice(128 * block, 128 * block + 128)
        part = whole[ROWS * block : ROWS * block + ROWS].astype(F32)
        o_in[:, lanes] = part[:D]
        o_bias[:, lanes] = part[D : D + 1]
        start = ROWS * (full + block)
        o_out_t[:, lanes] = whole[start : start + ROWS].astype(F32)[:D]
    rest = whole[ROWS * 2 * full : ROWS * 2 * full + ROWS]
    o_rest[...] = rest
    left = units - 128 * full
    part = mm_nt(rest, placer(left, 0))
    o_in[:, 128 * full :] = part[:D]
    o_bias[:, 128 * full :] = part[D : D + 1]
    o_out_t[:, 128 * full :] = mm_nt(rest, placer(left, left))[:D]


def whole_spec():
    return pl.BlockSpec(memory_space=pltpu.VMEM)


def any_spec():
    return pl.BlockSpec(memory_space=pl.ANY)


def far_spec():
    return pl.BlockSpec(memory_space=pltpu.HBM)


def scalar_spec():
    return pl.BlockSpec(memory_space=pltpu.SMEM)


def params(limit=VMEM_BYTES):
    return pltpu.CompilerParams(vmem_limit_bytes=limit)


def cost(flops, moved):
    return pl.CostEstimate(flops=int(flops), bytes_accessed=int(moved), transcendentals=0)


def shape(dims, dtype=LOW):
    return jax.ShapeDtypeStruct(dims, dtype)


def prepare(w_query, w_key, w_value, w_pos, w_out, bias_u, bias_v, pos_table):
    operands = (w_query, w_key, w_value, w_pos, w_out, bias_u[None], bias_v[None], pos_table)
    results = (
        ((PAIRS, D, 128), LOW),
        ((PAIRS, D, 256), LOW),
        ((PAIRS, SPAN, 128), LOW),
        ((WIDE, D), LOW),
        ((PAIRS, 2, 8, 128), F32),
    )
    return pl.pallas_call(
        prep_kernel,
        out_shape=tuple(shape(*r) for r in results),
        in_specs=[far_spec()] * len(operands),
        out_specs=(far_spec(),) * len(results),
        scratch_shapes=[pltpu.VMEM(a.shape, a.dtype) for a in operands]
        + [pltpu.VMEM(*r) for r in results]
        + [pltpu.SemaphoreType.DMA((16,))],
        compiler_params=params(),
        cost_estimate=cost(3e9, 5e6),
        name="prepare_weights",
    )(*operands)


def near(values):
    return pltpu.with_memory_space_constraint(values, pltpu.VMEM)


def far(values):
    return pltpu.with_memory_space_constraint(values, pltpu.HBM)


def layer(place, seg_len, mem_len, rows, reset, wq, wkv, rel, bias, wo, out_grads, own, other, vectors, size):
    units = own[0].shape[1]
    weights = (own[0], other[0], own[1], other[1], own[2], other[2])
    operands = [*rows, reset, wq, wkv, rel, bias, wo, *out_grads, *weights, *vectors]
    for k in RECEIVED:
        operands[k] = pltpu.with_memory_space_constraint(operands[k], pltpu.VMEM)
    results = (
        ((PAIRS, 2, 2, SEG, KEYS), LOW),
        ((PAIRS, 2, KEYS, 256), LOW),
        ((PAIRS, 2, SEG, 256), LOW),
        ((2, SEG, WIDE), F32),
        ((2, SEG, WIDE), F32),
        ((2, KEYS, D), LOW),
        ((2, SEG, D), LOW),
        ((2, SEG, D), F32),
        ((2, SEG, WIDE), F32),
        ((size, 128), LOW),
        ((size, 128), LOW),
        ((3, ROWS, 128), LOW),
    )
    return pl.pallas_call(
        layer_kernel,
        out_shape=tuple(shape(*r) for r in results),
        in_specs=[scalar_spec()] * 3
        + [any_spec() if k in RECEIVED else far_spec() for k in range(len(operands))],
        out_specs=(far_spec(),) * len(results),
        scratch_shapes=[pltpu.VMEM(a.shape, a.dtype) for a in operands]
        + [pltpu.VMEM(*r) for r in results]
        + [
            pltpu.VMEM((4, 4 * D, 128), F32),
            pltpu.VMEM((2, SEG, KEYS), F32),
            pltpu.VMEM((2, SEG, D), LOW),
            pltpu.VMEM((2 * SEG, 512), LOW),
            pltpu.VMEM((2 * SEG, D), LOW),
            pltpu.VMEM((2 * SEG, 512), LOW),
            pltpu.VMEM((2, 2 * SEG, units), LOW),
            pltpu.VMEM((2, 2 * SEG, units), LOW),
            pltpu.VMEM((8, D), F32),
            pltpu.VMEM((2, SEG, WIDE), LOW),
            pltpu.VMEM((2, 2 * SEG, units), F32),
            pltpu.SemaphoreType.DMA((48,)),
            pltpu.SemaphoreType.DMA((3, PAIRS, 2)),
        ],
        compiler_params=params(LAYER_BYTES),
        cost_estimate=cost(2e10, 3e7),
        name="layer",
    )(place, seg_len, mem_len, *operands)


def attend_back(pairs, operands, extra=(), size=0, fetched=False):
    count = len(pairs)
    total = PAIRS if size else count
    results = [pltpu.HBM((count, 2, SEG, 384), LOW)]
    if size:
        results += [shape((size, 128)), shape((size, 128))]
    else:
        results += [shape((count, 512, D)), shape((count, 8, 128), F32)]
    scratch = []
    if fetched:
        scratch = [
            pltpu.VMEM((count, 2, 2, SEG, KEYS), LOW),
            pltpu.VMEM((count, 2, KEYS, 256), LOW),
            pltpu.VMEM((count, 2, SEG, 256), LOW),
            pltpu.VMEM((count, SPAN, 128), LOW),
            pltpu.VMEM((count, 2, SEG, 128), F32),
            pltpu.VMEM((count, 2, SEG, 128), F32),
            pltpu.VMEM((count, 2, SEG, 128), F32),
            pltpu.VMEM((2, KEYS, D), LOW),
            pltpu.VMEM((SPAN, D), LOW),
            pltpu.SemaphoreType.DMA((20 * count,)),
        ]
    scratch += [
        pltpu.VMEM((2, 2, SEG, KEYS), LOW),
        pltpu.VMEM((2, 2, SEG, KEYS), LOW),
        pltpu.VMEM((128, KEYS), F32),
        pltpu.VMEM((2, 256, KEYS), LOW),
        pltpu.VMEM((total, 512, D), LOW),
        pltpu.VMEM((total, 8, 128), F32),
    ]
    if size:
        scratch.append(pltpu.VMEM((2 * HALF_BLOCKS, ROWS, 128), LOW))
    place = far if fetched else near
    return pl.pallas_call(
        functools.partial(
            back_kernel, pairs=pairs, calls=max(0, len(extra) // 2 - 1), fetched=fetched
        ),
        out_shape=tuple(results),
        in_specs=[far_spec() if fetched else whole_spec()] * 9
        + ([scalar_spec()] + [whole_spec()] * (len(extra) - 1) if size else []),
        out_specs=(whole_spec(),) * 3,
        scratch_shapes=scratch,
        compiler_params=params(LESS_BYTES),
        cost_estimate=cost(1.5e10 * count, 8e6),
        name=f"attend_back_{pairs[0]}",
    )(*(place(a) for a in operands), *extra)


def input_gradient(first_grad, tokens, wq, wkv):
    operands = [
        pltpu.with_memory_space_constraint(a, pltpu.HBM) for a in (first_grad, wq, wkv, *tokens)
    ]
    return pl.pallas_call(
        functools.partial(input_kernel, count=len(operands)),
        out_shape=shape((2, SEG, D), F32),
        in_specs=[far_spec()] * len(operands),
        out_specs=far_spec(),
        scratch_shapes=[pltpu.VMEM(a.shape, a.dtype) for a in operands]
        + [pltpu.VMEM((2, SEG, D), F32), pltpu.SemaphoreType.DMA((len(operands) + 2,))],
        compiler_params=params(LESS_BYTES),
        cost_estimate=cost(1.6e9, 6e6),
        name="input_gradient",
    )(*operands)


def unpack_attention(places, pieces, rest, dp_size):
    total = sum(p.shape[0] for p in pieces)
    return pl.pallas_call(
        functools.partial(unpack_attention_kernel, per_side=dp_size // 2),
        out_shape=(shape((D, D), F32),) * 5 + (shape((1, D), F32),) * 7,
        in_specs=[scalar_spec()] + [whole_spec()] * 5,
        out_specs=(whole_spec(),) * 12,
        scratch_shapes=[pltpu.VMEM((total, 128), LOW)],
        compiler_params=params(LESS_BYTES),
        cost_estimate=cost(5e8, 6e6),
        name="unpack_attention",
    )(places, *pieces, rest)


def unpack_ffn(places, pieces, units, dp_size):
    total = sum(p.shape[0] for p in pieces)
    return pl.pallas_call(
        functools.partial(unpack_ffn_kernel, per_side=dp_size // 2),
        out_shape=(
            shape((D, units), F32), shape((1, units), F32), shape((D, units), F32),
            shape((ROWS, 128)),
        ),
        in_specs=[scalar_spec()] + [whole_spec()] * 2,
        out_specs=(whole_spec(),) * 4,
        scratch_shapes=[pltpu.VMEM((total, 128), LOW)],
        compiler_params=params(LESS_BYTES),
        cost_estimate=cost(5e8, 6e6),
        name="unpack_ffn",
    )(places, *pieces)


def swap(values):
    return lax.ppermute(values, "tp", [(0, 1), (1, 0)])


def orders_of(dp_size):
    bits = list(range(dp_size.bit_length() - 1))
    turned = list(bits)
    for k in range(0, len(bits) - 1, 2):
        turned[k], turned[k + 1] = bits[k + 1], bits[k]
    return bits, turned


class Ring:
    def __init__(self, dp_size, index, core):
        self.size, self.orders = dp_size, orders_of(dp_size)
        self.steps = len(self.orders[0])
        self.bits = [
            jnp.where(core == 0, (index >> a) & 1, (index >> b) & 1)
            for a, b in zip(*self.orders)
        ]

    def place(self, index, order):
        spot = 0
        for k in self.orders[order]:
            spot = 2 * spot + ((index >> k) & 1)
        return spot

    def send(self, values, step):
        pairs = []
        for i in range(self.size):
            for c in range(2):
                pairs.append((2 * i + c, 2 * (i ^ (1 << self.orders[c][step])) + c))
        return lax.ppermute(values, ("dp", "tp"), pairs)

    def sides(self, keep, came, step):
        rows = keep.shape[0] // 2
        bit = self.bits[step]

        def side(which):
            start = which * rows
            return lax.dynamic_slice_in_dim(keep, start, rows, 0) + lax.dynamic_slice_in_dim(
                came, start, rows, 0
            )

        return side(1 - bit), side(bit)


def after(value, *others):
    return lax.optimization_barrier((value,) + others)


def rounded_rows(rows, unit):
    return -(-rows // unit) * unit


def make_shards(dp_size):
    table = position_table()

    def shards(
        hidden, memory, segment_length, memory_length, doc_reset, w_query, w_key, w_value, w_pos,
        bias_u, bias_v, w_out, first_gain, first_shift, ffn_in, ffn_in_bias, ffn_out, ffn_out_bias,
        second_gain, second_shift, out_grad,
    ):
        core = lax.axis_index("tp")
        index = lax.axis_index("dp")
        place = core[None].astype(jnp.int32)
        units = ffn_in.shape[1]
        pos_table = jnp.asarray(table)

        def by_feature(values):
            return values.transpose(2, 0, 1).reshape(-1, values.shape[1])

        hidden_t, memory_t, out_grad_t = (by_feature(a) for a in (hidden, memory, out_grad))
        hidden_in, memory_in, out_grad_in = swap(hidden_t), swap(memory_t), swap(out_grad_t)
        own_ffn = (ffn_in, ffn_in_bias[None], ffn_out.T)
        other_ffn = tuple(swap(a) for a in own_ffn)

        wq, wkv, rel, wo, bias = prepare(
            w_query, w_key, w_value, w_pos, w_out, bias_u, bias_v, pos_table
        )
        full = units // 128
        unit = 16 * dp_size
        (
            probs, kv, uv, att, inv, joined, act, first_grad, ga, ffn_own, ffn_other, out_blocks
        ) = layer(
            place, segment_length, memory_length, (hidden_t, memory_t, hidden_in, memory_in),
            doc_reset, wq, wkv, rel, bias, wo, (out_grad_t, out_grad_in), own_ffn, other_ffn,
            tuple(v[None] for v in (first_gain, first_shift, ffn_out_bias, second_gain, second_shift)),
            rounded_rows(ROWS * (2 * full + 1), unit),
        )
        ring = Ring(dp_size, index, core)
        straight, turned = ring.place(index, 0), ring.place(index, 1)
        places = jnp.stack(
            [
                jnp.where(core == 0, straight, turned),
                jnp.where(core == 0, turned, straight),
                core,
            ]
        ).astype(jnp.int32)

        def give_back(values, dtype):
            rows = values.shape[1] // 2
            mine = lax.dynamic_slice_in_dim(values, core * rows, rows, 1)
            theirs = lax.dynamic_slice_in_dim(values, (1 - core) * rows, rows, 1)
            came = swap(theirs.astype(LOW)).astype(dtype)
            mine = mine.astype(dtype)
            whole = jnp.where(
                core == 0,
                jnp.concatenate([mine, came], axis=0),
                jnp.concatenate([came, mine], axis=0),
            )
            return with_layout_constraint(whole, Layout(major_to_minor=(2, 0, 1)))

        def kept_memory(hidden):
            rows = hidden.shape[1]
            positions = core * rows + jnp.arange(rows)
            later = (jnp.arange(SEG)[:, None] > positions[None, :]).astype(LOW)
            resets = jnp.dot(doc_reset.astype(LOW), later, preferred_element_type=F32)
            keep = (resets == 0.0) & (positions[None, :] < segment_length[:, None])
            by_feature = hidden.transpose(2, 0, 1)
            return jnp.where(keep[None], by_feature, jnp.zeros_like(by_feature))

        steps = ring.steps
        slots = [[(0,)], [(1, 2, 3)], [(4,)]]
        operands = [probs, kv, uv, rel, ga, att, inv, joined, pos_table]
        tokens, wides, biases = [], [], []

        def back_slot(waited, slot):
            packed = None
            for pairs in slot:
                last = pairs[-1] == PAIRS - 1
                result = attend_back(
                    pairs,
                    operands,
                    (place, out_blocks, *wides, *biases) if last else (),
                    rounded_rows(ROWS * HALF_BLOCKS, unit) if last else 0,
                    fetched=not pairs[0],
                )
                waited, *result = after(waited, *result)
                tokens.append(result[0])
                operands[4], _ = after(operands[4], result[0])
                if last:
                    packed = result[1:]
                else:
                    wides.append(result[1])
                    biases.append(result[2])
            return waited, packed

        keep, came = ffn_own, swap(ffn_other)
        came, _ = back_slot(came, slots[0])
        first_steps = len(slots) - 1
        for step in range(first_steps):
            sent, kept = ring.sides(keep, came, step)
            sent, kept, operands[4] = after(sent, kept, operands[4])
            keep, came = kept, ring.send(sent, step)
            came, packed = back_slot(came, slots[step + 1])
        att_keep, att_send = packed
        att_came = swap(att_send)
        places, att_came = after(places, att_came)
        ffn = {"keep": keep, "came": came}

        def ffn_hop(kind, step, *others):
            ffn["keep"], ffn["came"], *_ = after(ffn["keep"], ffn["came"], *others)
            if kind == "scatter":
                sent, ffn["keep"] = ring.sides(ffn["keep"], ffn["came"], step)
            elif step == steps - 1:
                sent = ffn["keep"] = ffn["keep"] + ffn["came"]
            else:
                sent = ffn["keep"] = jnp.concatenate([ffn["keep"], ffn["came"]], axis=0)
            ffn["came"] = ring.send(sent, step)
            return sent

        hops = [("scatter", k) for k in range(first_steps, steps)]
        hops += [("gather", k) for k in range(steps - 1, -1, -1)]
        sent = ffn_hop(*hops.pop(0))
        att_keep, _ = after(att_keep, sent)
        for step in range(steps):
            sent, kept = ring.sides(att_keep, att_came, step)
            att_keep, att_came = kept, ring.send(sent, step)
            if len(hops) > 1:
                ffn_hop(*hops.pop(0), sent)
            if step == 0:
                first_grad, att_keep = after(first_grad, att_keep)
                input_own = input_gradient(first_grad, tokens, wq, wkv)
                att_came, input_own = after(att_came, input_own)
            elif step == 3:
                act, late_hidden, att_keep = after(act, hidden, att_keep)
                activations, new_memory = give_back(act, LOW), kept_memory(late_hidden)
                att_came, activations, new_memory = after(att_came, activations, new_memory)
        summed = att_keep + att_came
        for hop in hops:
            ffn_hop(*hop, summed)
        ffn_pieces = (ffn["keep"], ffn["came"])
        values = summed
        for step in range(steps - 1, 0, -1):
            came = ring.send(values, step)
            if step == max(1, steps - 2):
                input_own, values = after(input_own, values)
                input_grad = give_back(input_own, F32)
                came, input_grad = after(came, input_grad)
            values = jnp.concatenate([values, came], axis=0)
        came = ring.send(values, 0)
        near = swap(values)
        filled = list(unpack_ffn(places, ffn_pieces, units, dp_size))
        filled[1] = filled[1].reshape(-1)
        came, near, *filled = after(came, near, *filled)
        grad_in, grad_in_bias, grad_ffn_out_t, rest = filled
        g_query, g_key, g_value, g_pos, g_out, *vectors = unpack_attention(
            places, (values, came, near, swap(came)), rest, dp_size
        )
        g_bias_u, g_bias_v, g_gain_1, g_shift_1, g_gain_2, g_shift_2, g_ffn_bias = (
            v[0] for v in vectors
        )

        def by_token(values):
            return values.transpose(1, 2, 0)

        return (
            by_token(new_memory), activations, input_grad,
            g_query, g_key, g_value, g_pos, g_bias_u, g_bias_v, g_out, g_gain_1, g_shift_1,
            grad_in, grad_in_bias, grad_ffn_out_t.T, g_ffn_bias, g_gain_2, g_shift_2,
        )

    return shards


def solution(mesh):
    rows, copied = P("dp", "tp", None), P()
    shards = make_shards(mesh.shape["dp"])
    return jax.shard_map(
        shards,
        mesh=mesh,
        in_specs=(
            rows, rows, P("dp"), P("dp"), P("dp", None),
            copied, copied, copied, copied, copied, copied, copied, copied, copied,
            P(None, "tp"), P("tp"), P("tp", None),
            copied, copied, copied, rows,
        ),
        out_specs=(
            rows, rows, rows, copied, copied, copied, copied, copied, copied, copied, copied, copied,
            P(None, "tp"), P("tp"), P("tp", None), copied, copied, copied,
        ),
        check_vma=False,
    )
```
